32 devices in a mesh: stream: 2 (over x), batch: 4 (over y, core), tensor: 4 (over z).
Axes of the slice: x: 2, y: 2, z: 4, core: 2. Of those that a mesh axis runs over, the one named last changes fastest.
Arguments:
- hidden: bfloat16 [2, 3072, 768], P('stream', 'batch'), may hold values from -6 to 6
- cotangent: bfloat16 [2, 3072, 768], P('stream', 'batch'), may hold values from -6 to 6
- qkv_weight: bfloat16 [2, 768, 2304], P('stream', None, 'tensor'), may hold values from -0.21875 to 0.21875
- proj_weight: bfloat16 [2, 768, 768], P('stream', 'tensor'), may hold values from -1.75 to 1.75
- up_weight: bfloat16 [2, 768, 3072], P('stream', None, 'tensor'), may hold values from -0.21875 to 0.21875
- down_weight: bfloat16 [2, 3072, 768], P('stream', 'tensor'), may hold values from -0.109375 to 0.109375
- query_value_bias: bfloat16 [1536], P('tensor'), may hold values from -2 to 2
- unit_bias: bfloat16 [3072], P('tensor'), may hold values from -2 to 2
- layer_gain: bfloat16 [2, 768], replicated, may hold values from 0.5 to 1.5
- layer_shift: bfloat16 [2, 768], replicated, may hold values from -2 to 2
- output_bias: bfloat16 [2, 768], replicated, may hold values from -2 to 2
- scale_gain: bfloat16 [3, 768], replicated, may hold values from 0.5 to 1.5
- position_bias: bfloat16 [12, 32], P('tensor'), may hold values from -4 to 4
- cross_query: bfloat16 [768, 768], P(None, 'tensor'), may hold values from -0.21875 to 0.21875
- cross_key_value: bfloat16 [768, 1536], P(None, 'tensor'), may hold values from -0.21875 to 0.21875
- cross_proj: bfloat16 [768, 768], P('tensor'), may hold values from -1.75 to 1.75
- encodings: float32 [4, 768, 768], P('batch'), may hold values from -6 to 6
- query_vectors: float32 [4, 768], P('batch'), may hold values from -9 to 9
- passage_lengths: int32 [4, 2], P('batch'), may hold values from 1 to 384, as said below
- target_lengths: int32 [4], P('batch'), may hold values from 1 to 768, as said below
Outputs:
- block_out: bfloat16 [2, 3072, 768], P('stream', 'batch')
- input_grad: float32 [2, 3072, 768], P('stream', 'batch')
- grad_qkv: float32 [2, 768, 2304], P('stream', None, 'tensor')
- grad_proj: float32 [2, 768, 768], P('stream', 'tensor')
- grad_up: float32 [2, 768, 3072], P('stream', None, 'tensor')
- grad_down: float32 [2, 3072, 768], P('stream', 'tensor')
- grad_query_value_bias: float32 [1536], P('tensor')
- grad_unit_bias: float32 [3072], P('tensor')
- grad_layer_gain: float32 [2, 768], replicated
- grad_layer_shift: float32 [2, 768], replicated
- grad_output_bias: float32 [2, 768], replicated
- grad_scale_gain: float32 [3, 768], replicated
- grad_position_bias: float32 [12, 32], P('tensor')
- grad_cross_query: float32 [768, 768], P(None, 'tensor')
- grad_cross_key_value: float32 [768, 1536], P(None, 'tensor')
- grad_cross_proj: float32 [768, 768], P('tensor')
- retrieval_loss: float32 [4], P('batch')
The draws below stay inside these ranges and needn't reach their ends.
Inputs may be any that keep to these rules, and one draw needn't show every extreme that they name: `passage_lengths`: A passage's valid tokens are its first ones; some passage has all 384. `target_lengths`: A query's valid target rows are its first ones; some query has all 768.
All inputs are finite; a program needn't handle non-finite values.
Results may differ from the reference program's by a relative error of at most 0.03.
Values may be sent and summed in bfloat16 or wider, within the bound.
A program may use at most 128 MiB of HBM per device.

```python
from functools import partial
import jax
import jax.numpy as jnp
import numpy as np
from jax import lax

D = 768
HEADS = 12
HEAD_DIM = 64
FF = 3072
NBUCKET = 32
PLEN = 384
NPASS = 2
SEQ = 768
QUERIES = 4
ROWS = 3072
N_TENSOR = 4


def draw_passage_lengths(key, part):
    key = jax.random.fold_in(key, 11)
    drawn_lengths = jax.random.randint(jax.random.fold_in(key, 1), (QUERIES * NPASS,), 1, PLEN + 1)
    chosen = jax.random.randint(jax.random.fold_in(key, 2), (), 0, QUERIES * NPASS)
    filled = jnp.where(jnp.arange(QUERIES * NPASS) == chosen, PLEN, drawn_lengths)
    return filled.reshape(QUERIES, NPASS).astype(jnp.int32)


def draw_target_lengths(key, part):
    key = jax.random.fold_in(key, 23)
    drawn_lengths = jax.random.randint(jax.random.fold_in(key, 1), (QUERIES,), 1, SEQ + 1)
    chosen = jax.random.randint(jax.random.fold_in(key, 2), (), 0, QUERIES)
    return jnp.where(jnp.arange(QUERIES) == chosen, SEQ, drawn_lengths).astype(jnp.int32)


def block_levels(rng, dims, split, low, high):
    gain, own = 1.0, jax.random.fold_in(rng, 6)
    for position, parts in split:
        steps = jnp.exp(jax.random.uniform(jax.random.fold_in(own, position), (parts,), jnp.float32, low / len(split), high / len(split)))
        gain = gain * jnp.repeat(steps, dims[position] // parts).reshape([-1 if axis == position else 1 for axis in range(len(dims))])
    return gain


def bell_draw(stream_key, shape, spread, limit, shards=(), dtype=jnp.bfloat16):
    values = spread * jax.random.normal(stream_key, shape, jnp.float32)
    if shards:
        values = values * block_levels(stream_key, shape, shards, -0.22, 0.18)
    return jnp.clip(values, -limit, limit).astype(dtype)


def setup_inputs(seed: int = 0) -> dict:
    keys = jax.random.split(jax.random.key(seed), 21)
    return {
        "hidden": bell_draw(keys[0], (2, ROWS, D), 1.0, 6.0, ((0, 2), (1, 4))),
        "cotangent": bell_draw(keys[1], (2, ROWS, D), 1.0, 6.0, ((0, 2), (1, 4))),
        "qkv_weight": bell_draw(keys[2], (2, D, 3 * D), D ** -0.5, 0.21875, ((0, 2), (2, 4))),
        "proj_weight": bell_draw(keys[3], (2, D, D), (D // 64) ** -0.5, 1.75, ((0, 2), (1, 4))),
        "up_weight": bell_draw(keys[4], (2, D, FF), D ** -0.5, 0.21875, ((0, 2), (2, 4))),
        "down_weight": bell_draw(keys[5], (2, FF, D), FF ** -0.5, 0.109375, ((0, 2), (1, 4))),
        "query_value_bias": bell_draw(keys[6], (2 * D,), 0.3, 2.0, ((0, 4),)),
        "unit_bias": bell_draw(keys[7], (FF,), 0.3, 2.0, ((0, 4),)),
        "layer_gain": jnp.clip(1.0 + 0.1 * jax.random.normal(keys[8], (2, D), jnp.float32), 0.5, 1.5).astype(jnp.bfloat16),
        "layer_shift": bell_draw(keys[9], (2, D), 0.3, 2.0),
        "output_bias": bell_draw(keys[10], (2, D), 0.3, 2.0),
        "scale_gain": jnp.clip(1.0 + 0.1 * jax.random.normal(keys[11], (3, D), jnp.float32), 0.5, 1.5).astype(jnp.bfloat16),
        "position_bias": bell_draw(keys[12], (HEADS, NBUCKET), 1.0, 4.0, ((0, 4),)),
        "cross_query": bell_draw(keys[13], (D, D), D ** -0.5, 0.21875, ((1, 4),)),
        "cross_key_value": bell_draw(keys[14], (D, 2 * D), D ** -0.5, 0.21875, ((1, 4),)),
        "cross_proj": bell_draw(keys[15], (D, D), (D // 64) ** -0.5, 1.75, ((0, 4),)),
        "encodings": bell_draw(keys[16], (QUERIES, SEQ, D), 1.0, 6.0, ((0, 4),), jnp.float32),
        "query_vectors": bell_draw(keys[17], (QUERIES, D), 1.5, 9.0, ((0, 4),), jnp.float32),
        "passage_lengths": draw_passage_lengths(jax.random.fold_in(keys[20], 71), 0),
        "target_lengths": draw_target_lengths(jax.random.fold_in(keys[20], 71), 0),
    }


EPS = 1e-06
NEG = -1000000000.0
HIGH = lax.Precision.HIGHEST

@jax.custom_vjp
def low(v):
    return lax.optimization_barrier(v.astype(jnp.bfloat16)).astype(jnp.float32)

@jax.custom_vjp
def low_back(v):
    return v

def low_keep(v):
    return (low(v), None)

def low_pass(kept, grad):
    return (grad,)

def back_keep(v):
    return (v, None)

def back_low(kept, grad):
    return (low(grad),)
low.defvjp(low_keep, low_pass)
low_back.defvjp(back_keep, back_low)

def bucket_table(length, buckets):
    exact = buckets // 2
    distance = np.arange(length)
    far_bucket = exact + (np.log(np.maximum(distance, 1) / exact) / np.log(128.0 / exact) * (buckets - exact)).astype(np.int64)
    near_table = np.where(distance < exact, distance, np.minimum(far_bucket, buckets - 1))
    offsets = np.maximum(distance[:, None] - distance[None, :], 0)
    return near_table[offsets].astype(np.int32)

def dot_high(left, right):
    return jnp.dot(left, right, precision=HIGH, preferred_element_type=jnp.float32)

def group_out(values, weight):
    row_count = values.shape[0]
    inner = values.shape[1] // N_TENSOR
    pieces = jnp.einsum('tsk,tkn->tsn', values.reshape(row_count, N_TENSOR, inner).transpose(1, 0, 2), weight.reshape(N_TENSOR, inner, weight.shape[1]), precision=HIGH)
    return lax.optimization_barrier(jnp.sum(low(pieces), axis=0))

def group_in(values, weight):
    copies = low_back(jnp.broadcast_to(values, (N_TENSOR,) + values.shape))
    outer = weight.shape[1] // N_TENSOR
    pieces = jnp.einsum('tsd,dtk->tsk', copies, weight.reshape(weight.shape[0], N_TENSOR, outer), precision=HIGH)
    return pieces.transpose(1, 0, 2).reshape(values.shape[0], weight.shape[1])

def layer_norm(values, norm_gain, norm_shift):
    centered = values - lax.optimization_barrier(jnp.mean(values, axis=-1, keepdims=True))
    inv_root = lax.rsqrt(lax.optimization_barrier(jnp.mean(centered * centered, axis=-1, keepdims=True)) + EPS)
    return centered * inv_root * norm_gain + norm_shift

def root_norm(values, norm_gain):
    inv_root = lax.rsqrt(lax.optimization_barrier(jnp.mean(values * values, axis=-1, keepdims=True)) + EPS)
    return values * inv_root * norm_gain

def passage_keys(pass_lens):
    return (jnp.arange(PLEN)[None, :] < pass_lens[:, None]).reshape(SEQ)

def retriever_mask(pass_lens):
    row_index = jnp.arange(SEQ)[:, None]
    col_index = jnp.arange(SEQ)[None, :]
    return (row_index // PLEN == col_index // PLEN) & passage_keys(pass_lens)[None, :]

def causal_mask(target_len):
    row_index = jnp.arange(SEQ)[:, None]
    col_index = jnp.arange(SEQ)[None, :]
    return (col_index <= row_index) & (col_index < target_len)

def cross_mask(pass_lens):
    return jnp.broadcast_to(passage_keys(pass_lens)[None, :], (SEQ, SEQ))

def softmax_attend(queries, key_heads, values, score_bias, allowed):
    scores = jnp.einsum('ihd,jhd->hij', queries, key_heads, precision=HIGH) * HEAD_DIM ** (-0.5) + score_bias
    scores = low_back(jnp.where(allowed, scores, NEG))
    attn_probs = jax.nn.softmax(scores, axis=-1)
    mixed_out = jnp.einsum('hij,jhd->ihd', low(attn_probs), values, precision=HIGH)
    return (low(low_back(mixed_out)), attn_probs)

def retriever_query(params, query_items):
    qkv_side, proj_side, up_side, down_side, packed_shift, unit_shift, norm_gain, norm_shift, output_shift = params
    source_rows, pass_lens = query_items
    packed = low(low_back(group_in(source_rows, qkv_side) + packed_shift)).reshape(SEQ, HEADS, 3, HEAD_DIM)
    mixed_out, _ = softmax_attend(packed[:, :, 0], packed[:, :, 1], packed[:, :, 2], 0.0, retriever_mask(pass_lens))
    attn_out = low_back(group_out(mixed_out.reshape(SEQ, D), proj_side) + output_shift[0])
    middle = layer_norm(source_rows + attn_out, norm_gain[0], norm_shift[0])
    pre_act = low_back(group_in(low(middle), up_side) + unit_shift)
    unit_out = low_back(group_out(low(jax.nn.gelu(pre_act, approximate=True)), down_side) + output_shift[1])
    return layer_norm(middle + unit_out, norm_gain[1], norm_shift[1])

def reader_query(params, query_items):
    qkv_side, proj_side, up_side, down_side, scale_gains, position_table, cross_queries_w, cross_pairs_w, cross_proj_w = params
    source_rows, encoded, pass_lens, target_len = query_items
    normed = low(root_norm(source_rows, scale_gains[0]))
    packed = low(low_back(group_in(normed, qkv_side))).reshape(SEQ, HEADS, 3, HEAD_DIM)
    score_bias = jnp.take(position_table, jnp.asarray(bucket_table(SEQ, NBUCKET)), axis=1)
    mixed_out, _ = softmax_attend(packed[:, :, 0], packed[:, :, 1], packed[:, :, 2], score_bias, causal_mask(target_len))
    first_sum = source_rows + low_back(group_out(mixed_out.reshape(SEQ, D), proj_side))
    cross_in = low(root_norm(first_sum, scale_gains[1]))
    cross_queries = low(low_back(group_in(cross_in, cross_queries_w))).reshape(SEQ, HEADS, HEAD_DIM)
    cross_keys = low(low_back(dot_high(low(encoded), cross_pairs_w))).reshape(SEQ, HEADS, 2, HEAD_DIM)
    cross_mixed, cross_probs = softmax_attend(cross_queries, cross_keys[:, :, 0], cross_keys[:, :, 1], 0.0, cross_mask(pass_lens))
    second_sum = first_sum + low_back(group_out(cross_mixed.reshape(SEQ, D), cross_proj_w))
    live_rows = (jnp.arange(SEQ) < target_len).astype(jnp.float32)
    group_mass = lax.optimization_barrier(jnp.sum(cross_probs.reshape(N_TENSOR, HEADS // N_TENSOR, SEQ, SEQ) * live_rows[None, None, :, None], axis=(1, 2)))
    passage_mass = lax.optimization_barrier(jnp.sum(low(lax.optimization_barrier(jnp.sum(group_mass.reshape(N_TENSOR, NPASS, PLEN), axis=2))), axis=0)) / (HEADS * target_len.astype(jnp.float32))
    unit_in = low(root_norm(second_sum, scale_gains[2]))
    pre_act = low_back(group_in(unit_in, up_side))
    result = second_sum + low_back(group_out(low(jax.nn.gelu(pre_act, approximate=True)), down_side))
    return (result, passage_mass)

def reference(hidden, cotangent, qkv_weight, proj_weight, up_weight, down_weight, query_value_bias, unit_bias, layer_gain, layer_shift, output_bias, scale_gain, position_bias, cross_query, cross_key_value, cross_proj, encodings, query_vectors, passage_lengths, target_lengths):
    floats = [array.astype(jnp.float32) for array in (hidden, qkv_weight, proj_weight, up_weight, down_weight, query_value_bias, unit_bias, layer_gain, layer_shift, output_bias, scale_gain, position_bias, cross_query, cross_key_value, cross_proj)]
    live_keys = (jnp.arange(PLEN)[None, None, :] < passage_lengths[:, :, None]).astype(jnp.float32)
    pass_count = passage_lengths.astype(jnp.float32)

    def forward(source, qkv_weights, proj_weights, up_weights, down_weights, value_bias, unit_shift, norm_gain, norm_shift, output_shift, scale_gains, position_table, cross_queries_w, cross_pairs_w, cross_proj_w, targets):
        value_heads = value_bias.reshape(HEADS, 2, HEAD_DIM)
        packed_shift = jnp.stack([value_heads[:, 0], jnp.zeros_like(value_heads[:, 0]), value_heads[:, 1]], axis=1).reshape(3 * D)
        retriever_params = (qkv_weights[0], proj_weights[0], up_weights[0], down_weights[0], packed_shift, unit_shift, norm_gain, norm_shift, output_shift)
        reader_params = (qkv_weights[1], proj_weights[1], up_weights[1], down_weights[1], scale_gains, position_table, cross_queries_w, cross_pairs_w, cross_proj_w)
        retriever_out = lax.map(jax.checkpoint(partial(retriever_query, retriever_params)), (source[0].reshape(QUERIES, SEQ, D), passage_lengths))
        reader_out, passage_mass = lax.map(jax.checkpoint(partial(reader_query, reader_params)), (source[1].reshape(QUERIES, SEQ, D), encodings, passage_lengths, target_lengths))
        pooled = lax.optimization_barrier(jnp.sum(retriever_out.reshape(QUERIES, NPASS, PLEN, D) * live_keys[..., None], axis=2)) / pass_count[..., None]
        scores = lax.optimization_barrier(jnp.sum(pooled * query_vectors[:, None, :], axis=-1))
        log_probs = jax.nn.log_softmax(scores, axis=-1)
        kl_loss = lax.optimization_barrier(jnp.sum(targets * (jnp.log(targets) - log_probs), axis=-1))
        return ((retriever_out.reshape(QUERIES * SEQ, D), reader_out.reshape(QUERIES * SEQ, D), kl_loss), passage_mass)
    uniform = jnp.full((QUERIES, NPASS), 1.0 / NPASS, jnp.float32)
    _, passage_mass = forward(*floats, uniform)
    outputs, pull, _ = jax.vjp(partial(forward, targets=passage_mass), *floats, has_aux=True)
    cotangents = (cotangent[0].astype(jnp.float32), cotangent[1].astype(jnp.float32), jnp.ones((QUERIES,), jnp.float32))
    grads = pull(cotangents)
    retriever_out, reader_out, kl_loss = outputs
    block_out = jnp.stack([retriever_out, reader_out]).astype(jnp.bfloat16)
    return (block_out, grads[0], grads[1], grads[2], grads[3], grads[4], grads[5], grads[6], grads[7], grads[8], grads[9], grads[10], grads[11], grads[12], grads[13], grads[14], kl_loss)
```

```python
from functools import partial

import jax
import jax.numpy as jnp
import numpy as np
from jax import lax
from jax.experimental import pallas as pl
from jax.experimental.pallas import tpu as pltpu
from jax.sharding import PartitionSpec as P

HEADS = 12
HEAD_DIM = 64
PLEN = 384
NPASS = 2
SEQ = 768


EPS = 1e-06
NEG = -1000000000.0
HIGH = lax.Precision.HIGHEST


def from_behind(value, axis, steps):
    count = lax.axis_size(axis)
    first, last = (max(0, -steps), min(count, count - steps))
    return lax.ppermute(value, axis, [(source, source + steps) for source in range(first, last)])


def bucket_starts(length, buckets):
    exact = buckets // 2
    distance = np.arange(length)
    far_bucket = exact + (
        np.log(np.maximum(distance, 1) / exact) / np.log(128.0 / exact) * (buckets - exact)
    ).astype(np.int64)
    near_table = np.where(distance < exact, distance, np.minimum(far_bucket, buckets - 1))
    return [int(np.argmax(near_table == bucket)) for bucket in range(buckets)]


CHUNK = 64
MESH = pl.DeviceIdType.MESH


def line_sum_kernel(chunks, x_ref, out_ref, from_outer, from_inner, to_inner, send_sem, recv_sem):
    stream, query, place = (lax.axis_index(name) for name in ("stream", "batch", "tensor"))
    is_end = (place == 0) | (place == 3)
    inner = (stream, query, jnp.where(place == 0, 1, jnp.where(place == 3, 2, 3 - place)))
    outer = (stream, query, jnp.where(place == 1, 0, 3))
    barrier = pltpu.get_barrier_semaphore()
    pl.semaphore_signal(barrier, inc=1, device_id=inner, device_id_type=MESH)

    @pl.when(is_end)
    def _():
        pl.semaphore_wait(barrier, 1)

    @pl.when(jnp.logical_not(is_end))
    def _():
        pl.semaphore_signal(barrier, inc=1, device_id=outer, device_id_type=MESH)
        pl.semaphore_wait(barrier, 2)

    def rows(step):
        return pl.ds(pl.multiple_of(step * CHUNK, CHUNK), CHUNK)

    def to_middle(step):
        return pltpu.make_async_remote_copy(
            x_ref.at[rows(step)], from_outer.at[rows(step)], send_sem.at[0, step], recv_sem.at[0, step],
            device_id=inner, device_id_type=MESH)

    def across(step):
        return pltpu.make_async_remote_copy(
            to_inner.at[rows(step)], from_inner.at[rows(step)], send_sem.at[1, step], recv_sem.at[1, step],
            device_id=inner, device_id_type=MESH)

    def to_end(step):
        return pltpu.make_async_remote_copy(
            out_ref.at[rows(step)], out_ref.at[rows(step)], send_sem.at[2, step], recv_sem.at[2, step],
            device_id=outer, device_id_type=MESH)

    @pl.when(is_end)
    def _():
        @pl.loop(0, chunks)
        def _(step):
            to_middle(step).start()

        @pl.loop(0, chunks)
        def _(step):
            to_middle(step).wait_send()
            to_end(step).wait_recv()

    @pl.when(jnp.logical_not(is_end))
    def _():
        def first(step):
            to_middle(step).wait_recv()
            to_inner[rows(step)] = (
                from_outer[rows(step)].astype(jnp.float32) + x_ref[rows(step)].astype(jnp.float32)
            ).astype(jnp.bfloat16)
            across(step).start()

        def second(step):
            across(step).wait_recv()
            out_ref[rows(step)] = (
                from_inner[rows(step)].astype(jnp.float32) + to_inner[rows(step)].astype(jnp.float32)
            ).astype(jnp.bfloat16)
            to_end(step).start()

        first(0)

        @pl.loop(1, chunks)
        def _(step):
            first(step)
            second(step - 1)

        second(chunks - 1)

        @pl.loop(0, chunks)
        def _(step):
            across(step).wait_send()
            to_end(step).wait_send()


def line_sum(value):
    chunks = value.shape[0] // CHUNK
    block = pltpu.VMEM(value.shape, jnp.bfloat16)
    return pl.pallas_call(
        partial(line_sum_kernel, chunks),
        out_shape=jax.ShapeDtypeStruct(value.shape, jnp.bfloat16),
        in_specs=[pl.BlockSpec(memory_space=pltpu.VMEM)],
        out_specs=pl.BlockSpec(memory_space=pltpu.VMEM),
        scratch_shapes=[block, block, block, pltpu.SemaphoreType.DMA((3, chunks)), pltpu.SemaphoreType.DMA((3, chunks))],
        compiler_params=pltpu.CompilerParams(collective_id=0, has_side_effects=True, vmem_limit_bytes=32 * 2**20),
    )(value.astype(jnp.bfloat16)).astype(jnp.float32)


def layer_norm_forward(values, norm_gain, norm_shift):
    centered = values - jnp.mean(values, axis=-1, keepdims=True)
    inv_root = lax.rsqrt(jnp.mean(centered * centered, axis=-1, keepdims=True) + EPS)
    normed = centered * inv_root
    return (normed * norm_gain + norm_shift, normed, inv_root)


def layer_norm_backward(normed, inv_root, norm_gain, upstream):
    scaled_up = upstream * norm_gain
    grad_in = inv_root * (
        scaled_up
        - jnp.mean(scaled_up, axis=-1, keepdims=True)
        - normed * jnp.mean(scaled_up * normed, axis=-1, keepdims=True)
    )
    return (grad_in, jnp.sum(upstream * normed, axis=0), jnp.sum(upstream, axis=0))


def rms_forward(values, norm_gain):
    inv_root = lax.rsqrt(jnp.mean(values * values, axis=-1, keepdims=True) + EPS)
    return (values * inv_root * norm_gain, inv_root)


def rms_backward(values, inv_root, norm_gain, upstream):
    scaled_up = upstream * norm_gain
    grad_in = inv_root * scaled_up - values * (inv_root * inv_root * inv_root) * jnp.mean(
        scaled_up * values, axis=-1, keepdims=True
    )
    return (grad_in, jnp.sum(upstream * (values * inv_root), axis=0))


def gelu_back(pre_act, upstream):
    _, pull = jax.vjp(partial(jax.nn.gelu, approximate=True), pre_act)
    return pull(upstream)[0]


def passage_keys(pass_lens):
    return (jnp.arange(PLEN)[None, :] < pass_lens[:, None]).reshape(SEQ)


def self_mask(is_first, pass_lens, target_len):
    row_index = jnp.arange(SEQ)[:, None]
    col_index = jnp.arange(SEQ)[None, :]
    within = (row_index // PLEN == col_index // PLEN) & passage_keys(pass_lens)[None, :]
    causal = (col_index <= row_index) & (col_index < target_len)
    return jnp.where(is_first, within, causal)


def cross_mask(pass_lens):
    return jnp.broadcast_to(passage_keys(pass_lens)[None, :], (SEQ, SEQ))


def attend_scores(queries, key_heads, score_bias, allowed):
    scores = (
        jnp.einsum("ihd,jhd->hij", queries, key_heads, preferred_element_type=jnp.float32)
        * HEAD_DIM ** (-0.5)
        + score_bias
    )
    return jnp.where(allowed, scores, NEG)


def attend_forward(queries, key_heads, values, score_bias, allowed):
    scores = attend_scores(queries, key_heads, score_bias, allowed)
    row_max = jnp.max(scores, axis=-1, keepdims=True)
    exp_scores = jnp.exp(scores - row_max)
    total_sum = jnp.sum(exp_scores, axis=-1, keepdims=True)
    attn_probs = exp_scores / total_sum
    mixed_out = jnp.einsum(
        "hij,jhd->ihd", attn_probs.astype(jnp.bfloat16), values, preferred_element_type=jnp.float32
    )
    return (mixed_out.astype(jnp.bfloat16), row_max + jnp.log(total_sum), attn_probs)


def attend_backward(queries, key_heads, values, score_bias, allowed, log_norm, grad_mixed):
    attn_probs = jnp.exp(attend_scores(queries, key_heads, score_bias, allowed) - log_norm)
    grad_probs = jnp.einsum("ihd,jhd->hij", grad_mixed, values, preferred_element_type=jnp.float32)
    grad_s = (
        attn_probs * (grad_probs - jnp.sum(attn_probs * grad_probs, axis=-1, keepdims=True))
    ).astype(jnp.bfloat16)
    grad_q = jnp.einsum(
        "hij,jhd->ihd", grad_s, key_heads, preferred_element_type=jnp.float32
    ) * HEAD_DIM ** (-0.5)
    grad_k = jnp.einsum(
        "hij,ihd->jhd", grad_s, queries, preferred_element_type=jnp.float32
    ) * HEAD_DIM ** (-0.5)
    grad_v = jnp.einsum(
        "hij,ihd->jhd",
        attn_probs.astype(jnp.bfloat16),
        grad_mixed,
        preferred_element_type=jnp.float32,
    )
    return (grad_q, grad_k, grad_v, grad_s)


def sum_units(unit_pair):
    return (
        lax.psum(unit_pair[0].astype(jnp.bfloat16), "batch").astype(jnp.float32),
        lax.psum(unit_pair[1].astype(jnp.bfloat16), "batch").astype(jnp.float32),
    )


def sum_heads(head_pair):
    return (
        lax.psum(head_pair[0].astype(jnp.bfloat16), "batch").astype(jnp.float32),
        lax.psum(head_pair[1].astype(jnp.bfloat16), "batch").astype(jnp.float32),
    )


def local(
    hidden,
    cotangent,
    qkv_weight,
    proj_weight,
    up_weight,
    down_weight,
    query_value_bias,
    unit_bias,
    layer_gain,
    layer_shift,
    output_bias,
    scale_gain,
    position_bias,
    cross_query,
    cross_key_value,
    cross_proj,
    encodings,
    query_vectors,
    passage_lengths,
    target_lengths,
):
    is_first = lax.axis_index("stream") == 0
    local_heads = proj_weight.shape[1] // HEAD_DIM
    query_count = query_vectors.shape[0]
    total_rows = hidden.shape[1]
    width = hidden.shape[2]
    source = hidden[0].astype(jnp.float32)
    qkv_local = qkv_weight[0]
    proj_local = proj_weight[0]
    up_local = up_weight[0]
    down_local = down_weight[0]
    gains = scale_gain.astype(jnp.float32)
    norm_gain = layer_gain.astype(jnp.float32)
    norm_shift = layer_shift.astype(jnp.float32)
    out_shift = jnp.where(is_first, output_bias.astype(jnp.float32), 0.0)
    value_heads = query_value_bias.astype(jnp.float32).reshape(local_heads, 2, HEAD_DIM)
    packed_shift = jnp.stack(
        [value_heads[:, 0], jnp.zeros_like(value_heads[:, 0]), value_heads[:, 1]], axis=1
    ).reshape(-1)
    packed_shift = jnp.where(is_first, packed_shift, 0.0)
    unit_shift = jnp.where(is_first, unit_bias, jnp.zeros_like(unit_bias))
    starts = bucket_starts(SEQ, position_bias.shape[1])
    position_f32 = position_bias.astype(jnp.float32)
    apart = jnp.maximum(jnp.arange(SEQ)[:, None] - jnp.arange(SEQ)[None, :], 0)

    def lookup(table_values):
        band = jnp.broadcast_to(table_values[:, 0][:, None, None], (table_values.shape[0], SEQ, SEQ))
        for bucket in range(1, len(starts)):
            band = jnp.where(apart >= starts[bucket], table_values[:, bucket][:, None, None], band)
        return band

    def lookup_back(score_grads):
        columns = []
        for bucket in range(len(starts)):
            inside = apart >= starts[bucket]
            if bucket + 1 < len(starts):
                inside = inside & (apart < starts[bucket + 1])
            columns.append(jnp.sum(jnp.where(inside, score_grads, 0.0), axis=(1, 2)))
        return jnp.stack(columns, axis=1)

    self_bias = jnp.where(is_first, 0.0, lookup(position_f32))
    enc_low = encodings.astype(jnp.bfloat16).reshape(total_rows, width)
    pre_normed, pre_root = rms_forward(source, gains[0])
    first_in = jnp.where(is_first, source, pre_normed).astype(jnp.bfloat16)
    packed = (
        jnp.dot(first_in, qkv_local, preferred_element_type=jnp.float32) + packed_shift
    ).astype(jnp.bfloat16)
    packed = packed.reshape(query_count, SEQ, local_heads, 3, HEAD_DIM)

    def self_forward(query_items):
        packed_query, pass_lens, target_len = query_items
        allowed = self_mask(is_first, pass_lens, target_len)
        mixed_out, log_norm, _ = attend_forward(
            packed_query[:, :, 0], packed_query[:, :, 1], packed_query[:, :, 2], self_bias, allowed
        )
        return (mixed_out, log_norm)

    self_mixed, self_norm = lax.map(self_forward, (packed, passage_lengths, target_lengths))
    self_flat = self_mixed.reshape(total_rows, -1)
    attn_out = (
        line_sum(jnp.dot(self_flat, proj_local, preferred_element_type=jnp.float32))
        + out_shift[0]
    )
    first_sum = source + attn_out
    first_norm, first_normed, first_root = layer_norm_forward(
        first_sum, norm_gain[0], norm_shift[0]
    )
    middle = jnp.where(is_first, first_norm, first_sum)

    def cross_run(middle_in):
        normed, inv_root = rms_forward(middle_in, gains[1])
        normed_low = normed.astype(jnp.bfloat16)
        cross_queries = (
            jnp.dot(normed_low, cross_query, preferred_element_type=jnp.float32)
            .astype(jnp.bfloat16)
            .reshape(query_count, SEQ, local_heads, HEAD_DIM)
        )
        cross_keys = (
            jnp.dot(enc_low, cross_key_value, preferred_element_type=jnp.float32)
            .astype(jnp.bfloat16)
            .reshape(query_count, SEQ, local_heads, 2, HEAD_DIM)
        )

        def per_query(query_items):
            query_block, key_block, pass_lens, target_len = query_items
            mixed_out, log_norm, attn_probs = attend_forward(
                query_block, key_block[:, :, 0], key_block[:, :, 1], 0.0, cross_mask(pass_lens)
            )
            live_rows = (jnp.arange(SEQ) < target_len).astype(jnp.float32)
            column_mass = jnp.sum(attn_probs * live_rows[None, :, None], axis=(0, 1))
            return (mixed_out, log_norm, jnp.sum(column_mass.reshape(NPASS, PLEN), axis=1))

        cross_mixed, cross_norm, cross_mass = lax.map(
            per_query, (cross_queries, cross_keys, passage_lengths, target_lengths)
        )
        partial_out = jnp.dot(
            cross_mixed.reshape(total_rows, -1), cross_proj, preferred_element_type=jnp.float32
        )
        return (
            partial_out,
            cross_mass,
            normed_low,
            inv_root,
            cross_queries,
            cross_keys,
            cross_mixed,
            cross_norm,
        )

    def cross_skip(middle_in):
        head_zero = jnp.zeros((query_count, SEQ, local_heads, HEAD_DIM), jnp.bfloat16)
        return (
            jnp.zeros((total_rows, width), jnp.float32),
            jnp.zeros((query_count, NPASS), jnp.float32),
            jnp.zeros((total_rows, width), jnp.bfloat16),
            jnp.zeros((total_rows, 1), jnp.float32),
            head_zero,
            jnp.zeros((query_count, SEQ, local_heads, 2, HEAD_DIM), jnp.bfloat16),
            head_zero,
            jnp.zeros((query_count, local_heads, SEQ, 1), jnp.float32),
        )

    (
        cross_part,
        cross_mass,
        cross_normed,
        cross_root,
        cross_queries,
        cross_keys,
        cross_mixed,
        cross_norm,
    ) = lax.cond(is_first, cross_skip, cross_run, middle)
    cross_total, mass_total = (
        line_sum(cross_part),
        lax.psum(cross_mass.astype(jnp.bfloat16), "tensor").astype(jnp.float32),
    )
    second = middle + cross_total
    ffn_normed, ffn_root = rms_forward(second, gains[2])
    ffn_in = jnp.where(is_first, second, ffn_normed).astype(jnp.bfloat16)
    pre_act = jnp.dot(ffn_in, up_local, preferred_element_type=jnp.float32) + unit_shift.astype(
        jnp.float32
    )
    act_low = jax.nn.gelu(pre_act, approximate=True).astype(jnp.bfloat16)
    unit_out = line_sum(jnp.dot(act_low, down_local, preferred_element_type=jnp.float32))
    unit_out = unit_out + out_shift[1]
    final_sum = second + unit_out
    final_norm, final_normed, final_root = layer_norm_forward(
        final_sum, norm_gain[1], norm_shift[1]
    )
    result = jnp.where(is_first, final_norm, final_sum)
    live_keys = (jnp.arange(PLEN)[None, None, :] < passage_lengths[:, :, None]).astype(jnp.float32)
    pass_count = passage_lengths.astype(jnp.float32)
    pooled = (
        jnp.sum(result.reshape(query_count, NPASS, PLEN, width) * live_keys[..., None], axis=2)
        / pass_count[..., None]
    )
    scores = jnp.sum(pooled * query_vectors[:, None, :], axis=-1)
    incoming = from_behind(scores, "stream", 1)
    reader_targets = mass_total / (HEADS * target_lengths.astype(jnp.float32))[:, None]
    targets = jnp.where(is_first, 1.0 / NPASS, reader_targets)
    log_probs = jax.nn.log_softmax(incoming, axis=-1)
    own_loss = jnp.sum(targets * (jnp.log(targets) - log_probs), axis=-1)
    own_score_grad = jnp.exp(log_probs) * jnp.sum(targets, axis=-1, keepdims=True) - targets
    back_grad, back_loss = from_behind((own_score_grad, own_loss), "stream", -1)
    score_grad = jnp.where(is_first, back_grad, own_score_grad)
    kl_loss = jnp.where(is_first, back_loss, own_loss)
    upstream = cotangent[0].astype(jnp.float32)
    pooled_grad = score_grad[..., None] * query_vectors[:, None, :] / pass_count[..., None]
    row_grad = (pooled_grad[:, :, None, :] * live_keys[..., None]).reshape(total_rows, width)
    upstream = upstream + jnp.where(is_first, row_grad, 0.0)
    final_back, gain_grad_two, shift_grad_two = layer_norm_backward(
        final_normed, final_root, norm_gain[1], upstream
    )
    final_grad = jnp.where(is_first, final_back, upstream)
    unit_grad = final_grad.astype(jnp.bfloat16)
    out_grad_two = jnp.sum(unit_grad.astype(jnp.float32), axis=0)
    act_grad = jnp.dot(unit_grad, down_local.T, preferred_element_type=jnp.float32)
    pre_grad = gelu_back(pre_act, act_grad).astype(jnp.bfloat16)
    up_grad = jnp.dot(ffn_in.T, pre_grad, preferred_element_type=jnp.float32)
    down_grad = jnp.dot(act_low.T, unit_grad, preferred_element_type=jnp.float32)
    shift_grad = jnp.sum(pre_grad.astype(jnp.float32), axis=0)
    ffn_in_grad = line_sum(jnp.dot(pre_grad, up_local.T, preferred_element_type=jnp.float32))
    unit_pair = (up_grad, down_grad)
    ffn_back, rms_grad_three = rms_backward(second, ffn_root, gains[2], ffn_in_grad)
    second_grad = final_grad + jnp.where(is_first, ffn_in_grad, ffn_back)

    def cross_back_run(grad_in):
        cross_grad = grad_in.astype(jnp.bfloat16)
        proj_grad = jnp.dot(
            cross_mixed.reshape(total_rows, -1).T, cross_grad, preferred_element_type=jnp.float32
        )
        mixed_grad = (
            jnp.dot(cross_grad, cross_proj.T, preferred_element_type=jnp.float32)
            .astype(jnp.bfloat16)
            .reshape(query_count, SEQ, local_heads, HEAD_DIM)
        )

        def per_query(query_items):
            query_block, key_block, pass_lens, log_norm, grad_block = query_items
            grad_q, grad_k, grad_v, _ = attend_backward(
                query_block,
                key_block[:, :, 0],
                key_block[:, :, 1],
                0.0,
                cross_mask(pass_lens),
                log_norm,
                grad_block,
            )
            return (grad_q, jnp.stack([grad_k, grad_v], axis=2))

        query_grad, pair_grad = lax.map(
            per_query, (cross_queries, cross_keys, passage_lengths, cross_norm, mixed_grad)
        )
        query_grad = query_grad.astype(jnp.bfloat16).reshape(total_rows, -1)
        pair_grad = pair_grad.astype(jnp.bfloat16).reshape(total_rows, -1)
        in_part = jnp.dot(query_grad, cross_query.T, preferred_element_type=jnp.float32)
        query_weight_grad = jnp.dot(cross_normed.T, query_grad, preferred_element_type=jnp.float32)
        pair_weight_grad = jnp.dot(enc_low.T, pair_grad, preferred_element_type=jnp.float32)
        return (in_part, query_weight_grad, pair_weight_grad, proj_grad)

    def cross_back_skip(grad_in):
        return (
            jnp.zeros((total_rows, width), jnp.float32),
            jnp.zeros(cross_query.shape, jnp.float32),
            jnp.zeros(cross_key_value.shape, jnp.float32),
            jnp.zeros(cross_proj.shape, jnp.float32),
        )

    cross_in_part, cross_query_grad, cross_pair_grad, cross_proj_grad = lax.cond(
        is_first, cross_back_skip, cross_back_run, second_grad
    )
    cross_in_grad = line_sum(cross_in_part)
    cross_back, rms_grad_two = rms_backward(middle, cross_root, gains[1], cross_in_grad)
    middle_grad = second_grad + jnp.where(is_first, 0.0, cross_back)
    first_back, gain_grad_one, shift_grad_one = layer_norm_backward(
        first_normed, first_root, norm_gain[0], middle_grad
    )
    first_grad = jnp.where(is_first, first_back, middle_grad)
    attn_grad = first_grad.astype(jnp.bfloat16)
    out_grad_one = jnp.sum(attn_grad.astype(jnp.float32), axis=0)
    proj_weight_grad = jnp.dot(self_flat.T, attn_grad, preferred_element_type=jnp.float32)
    self_grad = (
        jnp.dot(attn_grad, proj_local.T, preferred_element_type=jnp.float32)
        .astype(jnp.bfloat16)
        .reshape(query_count, SEQ, local_heads, HEAD_DIM)
    )

    def self_backward(query_items):
        packed_query, pass_lens, target_len, log_norm, grad_block = query_items
        allowed = self_mask(is_first, pass_lens, target_len)
        grad_q, grad_k, grad_v, grad_s = attend_backward(
            packed_query[:, :, 0],
            packed_query[:, :, 1],
            packed_query[:, :, 2],
            self_bias,
            allowed,
            log_norm,
            grad_block,
        )
        return (
            jnp.stack([grad_q, grad_k, grad_v], axis=2),
            lookup_back(grad_s.astype(jnp.float32)),
        )

    packed_grad, table_grads = lax.map(
        self_backward, (packed, passage_lengths, target_lengths, self_norm, self_grad)
    )
    packed_grad = packed_grad.astype(jnp.bfloat16).reshape(total_rows, -1)
    table_grad = jnp.sum(table_grads, axis=0)
    qkv_weight_grad = jnp.dot(first_in.T, packed_grad, preferred_element_type=jnp.float32)
    shift_heads = jnp.sum(packed_grad.astype(jnp.float32), axis=0).reshape(local_heads, 3, HEAD_DIM)
    value_bias_grad = jnp.stack([shift_heads[:, 0], shift_heads[:, 2]], axis=1).reshape(-1)
    first_in_grad = line_sum(jnp.dot(packed_grad, qkv_local.T, preferred_element_type=jnp.float32))
    pre_back, rms_grad_one = rms_backward(source, pre_root, gains[0], first_in_grad)
    input_grad = first_grad + jnp.where(is_first, first_in_grad, pre_back)
    qkv_sum, proj_sum = sum_heads((qkv_weight_grad, proj_weight_grad))
    up_sum, down_sum = sum_units(unit_pair)

    def retriever_only(values):
        return jnp.where(is_first, values, 0.0)

    def reader_only(values):
        return jnp.where(is_first, 0.0, values)

    side_terms = (
        retriever_only(value_bias_grad),
        retriever_only(shift_grad),
        retriever_only(jnp.stack([gain_grad_one, gain_grad_two])),
        retriever_only(jnp.stack([shift_grad_one, shift_grad_two])),
        retriever_only(jnp.stack([out_grad_one, out_grad_two])),
        reader_only(jnp.stack([rms_grad_one, rms_grad_two, rms_grad_three])),
        reader_only(table_grad),
        cross_query_grad,
        cross_pair_grad,
        cross_proj_grad,
    )
    (
        value_sum,
        unit_bias_sum,
        gain_sum,
        shift_sum,
        out_sum,
        scale_sum,
        table_sum,
        cross_query_sum,
        cross_pair_sum,
        cross_proj_sum,
    ) = lax.psum(
        (
            side_terms[0],
            side_terms[1],
            side_terms[2],
            side_terms[3],
            side_terms[4],
            side_terms[5],
            side_terms[6],
            side_terms[7],
            side_terms[8],
            side_terms[9],
        ),
        ("stream", "batch"),
    )
    return (
        result.astype(jnp.bfloat16)[None],
        input_grad[None],
        qkv_sum[None],
        proj_sum[None],
        up_sum[None],
        down_sum[None],
        value_sum,
        unit_bias_sum,
        gain_sum,
        shift_sum,
        out_sum,
        scale_sum,
        table_sum,
        cross_query_sum,
        cross_pair_sum,
        cross_proj_sum,
        kl_loss,
    )


def solution(mesh):
    in_specs = (
        P("stream", "batch", None),
        P("stream", "batch", None),
        P("stream", None, "tensor"),
        P("stream", "tensor", None),
        P("stream", None, "tensor"),
        P("stream", "tensor", None),
        P("tensor"),
        P("tensor"),
        P(),
        P(),
        P(),
        P(),
        P("tensor", None),
        P(None, "tensor"),
        P(None, "tensor"),
        P("tensor", None),
        P("batch", None, None),
        P("batch", None),
        P("batch", None),
        P("batch"),
    )
    out_specs = (
        P("stream", "batch", None),
        P("stream", "batch", None),
        P("stream", None, "tensor"),
        P("stream", "tensor", None),
        P("stream", None, "tensor"),
        P("stream", "tensor", None),
        P("tensor"),
        P("tensor"),
        P(),
        P(),
        P(),
        P(),
        P("tensor", None),
        P(None, "tensor"),
        P(None, "tensor"),
        P("tensor", None),
        P("batch"),
    )
    return jax.shard_map(local, mesh=mesh, in_specs=in_specs, out_specs=out_specs, check_vma=False)
```

```python
from functools import partial

import jax
import jax.numpy as jnp
import numpy as np
from jax import lax
from jax.experimental import pallas as pl
from jax.experimental.pallas import tpu as pltpu
from jax.sharding import PartitionSpec as P

HEADS = 12
HEAD_DIM = 64
PLEN = 384
NPASS = 2
SEQ = 768
WIDTH = 768
HALF = 384
THIRD = 256
PIECE = 64
PIECES = SEQ // PIECE
AHEAD = 3
LANES = 128

EPS = 1e-06
NEG = -1000000000.0
MESH = pl.DeviceIdType.MESH
BF16 = jnp.bfloat16
F32 = jnp.float32

NN = (((1,), (0,)), ((), ()))
NT = (((1,), (1,)), ((), ()))
TN = (((0,), (0,)), ((), ()))

STREAM, BATCH, TENSOR = "stream", "batch", "tensor"
UP, DOWN, QKV, PROJ, CQ, CKV, CPROJ = "up", "down", "qkv", "proj", "cq", "ckv", "cproj"
WEIGHTS = (UP, DOWN, QKV, PROJ, CQ, CKV, CPROJ)


def bucket_starts(length, buckets):
    exact = buckets // 2
    distance = np.arange(length)
    far_bucket = exact + (
        np.log(np.maximum(distance, 1) / exact) / np.log(128.0 / exact) * (buckets - exact)
    ).astype(np.int64)
    near_table = np.where(distance < exact, distance, np.minimum(far_bucket, buckets - 1))
    return [int(np.argmax(near_table == bucket)) for bucket in range(buckets)]


def dot(left, right, dims):
    return lax.dot_general(left, right, dims, preferred_element_type=F32)


def fold(values):
    return jnp.sum(values.reshape(values.shape[0] // 8, 8, values.shape[1]), axis=0)


def mean(values):
    return jnp.mean(values, axis=-1, keepdims=True)


def weight_shapes(heads):
    inner = heads * HEAD_DIM
    return dict(
        up=(WIDTH, WIDTH),
        down=(WIDTH, WIDTH),
        qkv=(3 * inner, WIDTH),
        proj=(inner, WIDTH),
        cq=(inner, WIDTH),
        ckv=(WIDTH, 2 * inner),
        cproj=(inner, WIDTH),
    )


def scratch_shapes(heads):
    inner = heads * HEAD_DIM

    def low(*shape):
        return pltpu.VMEM(shape, BF16)

    def full(*shape):
        return pltpu.VMEM(shape, F32)

    whole = low(SEQ, WIDTH)
    head_rows = low(heads, SEQ, LANES)
    head_sums = full(heads, SEQ, LANES)
    scores = low(heads, SEQ, SEQ)
    bands = full(heads, 2 * LANES, LANES)
    room = low(3, SEQ, WIDTH)
    line = pltpu.SemaphoreType.DMA((3, 6, PIECES))
    shapes = dict(
        hid=whole, cot=whole, encb=whole, buf_a=whole, buf_b=whole, buf_c=whole, buf_u=whole,
        act=whole, dpre=whole, ag=whole, ybuf=whole,
        h1f=full(SEQ, WIDTH), h2f=full(SEQ, WIDTH),
        qa=head_rows, ka=head_rows, va=head_rows, cqa=head_rows, cka=head_rows, cva=head_rows,
        dk=head_sums, dv=head_sums, e1=scores, e2=scores,
        o1=low(inner, SEQ), o2=low(inner, SEQ), dot_in=low(inner, HALF),
        linv1=full(8, SEQ), linv2=full(8, SEQ),
        pkb=low(SEQ, 3 * inner), cqb=low(SEQ, inner), ckb=low(SEQ, 2 * inner),
        tall=full(SEQ, HALF), tall_low=low(SEQ, HALF), wide=full(HALF, WIDTH),
        band=bands, band_grad=bands, params=full(16, WIDTH), acc=full(10, 8, WIDTH),
        colsum=full(8, 3 * inner), mass_rows=full(8, HALF),
        small=full(16, WIDTH), small_got=full(8, 16, WIDTH), mass=full(8, LANES),
        mass_got=full(4, 8, LANES), part=room, outer=room, total=room,
        in_sem=pltpu.SemaphoreType.DMA((10,)), line_send=line, line_recv=line,
        w_send=pltpu.SemaphoreType.DMA((7, 6)), w_recv=pltpu.SemaphoreType.DMA((7, 5)),
        small_send=pltpu.SemaphoreType.DMA((7,)), small_recv=pltpu.SemaphoreType.DMA((8,)),
        mass_send=pltpu.SemaphoreType.DMA((4,)), mass_recv=pltpu.SemaphoreType.DMA((4,)),
        out_sem=pltpu.SemaphoreType.DMA((2, 3)),
        over_send=pltpu.SemaphoreType.DMA((2, 3)), over_recv=pltpu.SemaphoreType.DMA((2, 3)),
    )
    for name, shape in weight_shapes(heads).items():
        half = (shape[0] // 2, shape[1])
        shapes["w_" + name] = low(*shape)
        shapes["d_" + name] = low(*shape)
        shapes["rc_" + name] = low(*half)
        shapes["ry_" + name] = low(*half)
    return shapes


class Refs:
    pass


def layer_kernel(heads, buckets, names, *refs):
    r = Refs()
    for name, ref in zip(names, refs):
        setattr(r, name, ref)
    stream, query, place = (lax.axis_index(name) for name in (STREAM, BATCH, TENSOR))
    is_reader = stream == 1
    is_end = (place == 0) | (place == 3)
    is_middle = jnp.logical_not(is_end)
    inner_place = jnp.where(place == 0, 1, jnp.where(place == 3, 2, 3 - place))
    outer_place = jnp.where(place == 1, 0, 3)
    core = lax.rem(query, 2)
    group = query - lax.rem(query, 4)
    member = lax.rem(query, 4)

    def other(steps):
        return group + lax.rem(member + steps, 4)

    mate = query + 1 - 2 * core
    across_y = group + lax.rem(member + 2, 4)

    barrier = pltpu.get_barrier_semaphore()

    def greet(device):
        pl.semaphore_signal(barrier, inc=1, device_id=device, device_id_type=MESH)

    for steps in range(1, 4):
        greet((stream, other(steps), place))
    for steps in range(4):
        greet((1 - stream, other(steps), place))
    for steps in range(1, 4):
        greet((1 - stream, query, lax.rem(place + steps, 4)))
    greet((stream, query, inner_place))

    @pl.when(is_middle)
    def _():
        greet((stream, query, outer_place))

    def meet():
        @pl.when(is_end)
        def _():
            pl.semaphore_wait(barrier, 11)

        @pl.when(is_middle)
        def _():
            pl.semaphore_wait(barrier, 12)

    def bring(index, source, target):
        return pltpu.make_async_copy(source, target, r.in_sem.at[index])

    inputs = Refs()
    inputs.hid = bring(0, r.hidden.at[0], r.hid)
    inputs.qkv = bring(1, r.qkv_weight, r.w_qkv)
    inputs.proj = bring(2, r.proj_weight.at[0], r.w_proj)
    inputs.enc = bring(3, r.encodings.at[0], r.h2f)
    inputs.ckv = bring(4, r.cross_key_value, r.w_ckv)
    inputs.cq = bring(5, r.cross_query, r.w_cq)
    inputs.cproj = bring(6, r.cross_proj, r.w_cproj)
    inputs.up = bring(7, r.up_weight.at[0], r.w_up)
    inputs.down = bring(8, r.down_weight.at[0], r.w_down)
    inputs.cot = bring(9, r.cotangent.at[0], r.cot)

    def piece_rows(piece):
        return pl.ds(piece * PIECE, PIECE)

    side = Refs()

    def chunk_rows(chunk):
        return pl.ds(chunk * side.size, side.size)

    def row_loop(chunk, body):
        @pl.loop(0, side.size // PIECE)
        def _(step):
            body(pl.ds(pl.multiple_of(chunk * side.size + step * PIECE, PIECE), PIECE),
                 pl.ds(pl.multiple_of(step * PIECE, PIECE), PIECE))

    def to_middle(line, room, piece):
        rows = piece_rows(piece)
        return pltpu.make_async_remote_copy(
            r.part.at[room, rows], r.outer.at[room, rows],
            r.line_send.at[0, line, piece], r.line_recv.at[0, line, piece],
            device_id=(stream, query, inner_place), device_id_type=MESH)

    def across(line, room, piece):
        rows = piece_rows(piece)
        return pltpu.make_async_remote_copy(
            r.outer.at[room, rows], r.total.at[room, rows],
            r.line_send.at[1, line, piece], r.line_recv.at[1, line, piece],
            device_id=(stream, query, inner_place), device_id_type=MESH)

    def to_end(line, room, piece):
        rows = piece_rows(piece)
        return pltpu.make_async_remote_copy(
            r.total.at[room, rows], r.total.at[room, rows],
            r.line_send.at[2, line, piece], r.line_recv.at[2, line, piece],
            device_id=(stream, query, outer_place), device_id_type=MESH)

    made, added, summed = [], [], []

    def chunk_pieces(chunk):
        count = side.size // PIECE
        return range(chunk * count, (chunk + 1) * count)

    def produce(line, room, pieces):
        @pl.when(is_end)
        def _():
            for piece in pieces:
                to_middle(line, room, piece).start()

        made.extend((line, room, piece) for piece in pieces)

    def add_outer(line, room, piece):
        rows = piece_rows(piece)
        to_middle(line, room, piece).wait_recv()
        r.outer[room, rows] = (
            r.outer[room, rows].astype(F32) + r.part[room, rows].astype(F32)).astype(BF16)
        across(line, room, piece).start()

    def add_inner(line, room, piece):
        rows = piece_rows(piece)
        across(line, room, piece).wait_recv()
        r.total[room, rows] = (
            r.total[room, rows].astype(F32) + r.outer[room, rows].astype(F32)).astype(BF16)
        to_end(line, room, piece).start()

    def advance():
        if len(added) < len(made) and len(added) - len(summed) < AHEAD:
            item = made[len(added)]
            added.append(item)
            add_outer(*item)
        else:
            item = made[len(summed)]
            summed.append(item)
            add_inner(*item)

    def pump(count=1):
        steps = min(2 * count, 2 * len(made) - len(added) - len(summed))
        if steps > 0:
            @pl.when(is_middle)
            def _():
                for _ in range(steps):
                    advance()

    def finish(line, room, pieces):
        last = made.index((line, room, pieces[-1]))

        @pl.when(is_middle)
        def _():
            while len(summed) <= last:
                advance()

        @pl.when(is_end)
        def _():
            for piece in pieces:
                to_end(line, room, piece).wait_recv()
                to_middle(line, room, piece).wait_send()

    def settle(line, room, pieces):
        @pl.when(is_middle)
        def _():
            for piece in pieces:
                across(line, room, piece).wait_send()
                to_end(line, room, piece).wait_send()

    def hand_on(line, room, chunk, before=None):
        pieces = chunk_pieces(chunk)
        if before:
            settle(*before, pieces)
        produce(line, room, pieces)

    def collect(line, room, chunk):
        finish(line, room, chunk_pieces(chunk))

    def hand_over(chunk):
        rows = pl.ds(chunk * THIRD, THIRD)
        return pltpu.make_async_remote_copy(
            r.part.at[2, rows], r.part.at[2, rows], r.over_send.at[0, chunk], r.over_recv.at[0, chunk],
            device_id=(1 - stream, query, place), device_id_type=MESH)

    def hand_back(chunk):
        rows = pl.ds(chunk * THIRD, THIRD)
        return pltpu.make_async_remote_copy(
            r.total.at[2, rows], r.total.at[2, rows], r.over_send.at[1, chunk], r.over_recv.at[1, chunk],
            device_id=(1 - stream, query, place), device_id_type=MESH)

    def third_pieces(chunk):
        count = THIRD // PIECE
        return range(chunk * count, (chunk + 1) * count)

    def w_copy(source, target, index, send, recv, device):
        return pltpu.make_async_remote_copy(
            source, target, r.w_send.at[index, send], r.w_recv.at[index, recv],
            device_id=device, device_id_type=MESH)

    def w_parts(name):
        grad = getattr(r, "d_" + name)
        half = grad.shape[0] // 2
        mine = pl.ds(pl.multiple_of(core * half, half), half)
        theirs = pl.ds(pl.multiple_of((1 - core) * half, half), half)
        return WEIGHTS.index(name), grad, getattr(r, "rc_" + name), getattr(r, "ry_" + name), mine, theirs

    def w_first(name):
        index, grad, rc, ry, mine, theirs = w_parts(name)
        return w_copy(grad.at[theirs], rc, index, 0, 0, (stream, mate, place))

    def w_second(name):
        index, grad, rc, ry, mine, theirs = w_parts(name)
        return w_copy(rc, ry, index, 1, 1, (stream, across_y, place))

    def w_third(name):
        index, grad, rc, ry, mine, theirs = w_parts(name)
        out = getattr(r, name)
        return w_copy(grad.at[mine], out.at[mine], index, 2, 2, (stream, mate, place))

    def w_local(name):
        index, grad, rc, ry, mine, theirs = w_parts(name)
        return pltpu.make_async_copy(grad.at[mine], getattr(r, name).at[mine], r.w_send.at[index, 3])

    def w_other_side(name, crossed):
        index, grad, rc, ry, mine, theirs = w_parts(name)
        device = (1 - stream, mate if crossed else query, place)
        out = getattr(r, name)
        return w_copy(grad.at[mine], out.at[mine], index, 4 + crossed, 3 + crossed, device)

    def w_start(name):
        w_first(name).start()

    def w_combine(name):
        index, grad, rc, ry, mine, theirs = w_parts(name)
        w_first(name).wait_recv()
        step = 48 if rc.shape[0] % 64 else 64

        @pl.loop(0, rc.shape[0] // step)
        def _(i):
            rows = pl.ds(pl.multiple_of(i * step, step), step)
            own = pl.ds(pl.multiple_of(core * rc.shape[0] + i * step, step), step)
            rc[rows] = (grad[own].astype(F32) + rc[rows].astype(F32)).astype(BF16)

        w_second(name).start()

    def w_store(name):
        index, grad, rc, ry, mine, theirs = w_parts(name)
        w_second(name).wait_recv()
        step = 48 if rc.shape[0] % 64 else 64

        @pl.loop(0, rc.shape[0] // step)
        def _(i):
            rows = pl.ds(pl.multiple_of(i * step, step), step)
            own = pl.ds(pl.multiple_of(core * rc.shape[0] + i * step, step), step)
            grad[own] = (ry[rows].astype(F32) + rc[rows].astype(F32)).astype(BF16)

        w_third(name).start()
        w_local(name).start()
        if name in (CQ, CKV, CPROJ):
            w_other_side(name, 0).start()
            w_other_side(name, 1).start()

    def w_end(name):
        w_first(name).wait_send()
        w_second(name).wait_send()
        w_third(name).wait()
        w_local(name).wait()
        if name in (CQ, CKV, CPROJ):
            w_other_side(name, 0).wait_send()
            w_other_side(name, 1).wait_send()

    def softmax(exp_ref, head, chunk, first_key, keys, banded):
        sums = []
        for tile in range(side.size // LANES):
            cols = pl.ds(tile * LANES, LANES)
            rows = pl.ds(chunk * side.size + tile * LANES, LANES)
            end = chunk * side.size + (tile + 1) * LANES if banded else keys
            if banded:
                near = min(end, 2 * LANES)
                r.tall[pl.ds(end - near, near), cols] += r.band[head, pl.ds(2 * LANES - near, near)]
            top = jnp.max(r.tall[pl.ds(0, end), cols], axis=0, keepdims=True)
            parts = [jnp.zeros((1, LANES), F32), jnp.zeros((1, LANES), F32)]
            for key in range(0, end, LANES):
                grown = jnp.exp(r.tall[pl.ds(key, LANES), cols] - top)
                exp_ref[head, pl.ds(first_key + key, LANES), rows] = grown.astype(BF16)
                parts[key // HALF] += jnp.sum(grown, axis=0, keepdims=True)
            for key in range(end, keys, LANES):
                exp_ref[head, pl.ds(first_key + key, LANES), rows] = jnp.zeros((LANES, LANES), BF16)
            sums.append(parts)
        return [jnp.concatenate([parts[p] for parts in sums], axis=1) for p in range(2)]

    def attend(qa, ka, va, exp_ref, out_ref, inv_ref, chunk, first_key, keys, banded, mass, pumps):
        rows = chunk_rows(chunk)
        span = pl.ds(first_key, keys)
        cols_all = pl.ds(0, side.size)
        for head in range(heads):
            r.tall[pl.ds(0, keys), cols_all] = dot(ka[head, span], qa[head, rows], NT)
            parts = softmax(exp_ref, head, chunk, first_key, keys, banded)
            inverse = 1.0 / (parts[0] + parts[1])
            inv_ref[pl.ds(head, 1), rows] = inverse
            if mass:
                live = lax.broadcasted_iota(jnp.int32, (1, side.size), 1) + chunk * side.size < r.target_lengths[0]
                for p in range(NPASS):
                    r.mass_rows[pl.ds(p, 1), cols_all] += jnp.where(live, parts[p] * inverse, 0.0)
            mixed = dot(va[head, span, pl.ds(0, HEAD_DIM)], exp_ref[head, span, rows], TN)
            out_ref[pl.ds(head * HEAD_DIM, HEAD_DIM), rows] = (mixed * inverse).astype(BF16)
            if head < pumps:
                pump()

    def attend_back(qa, ka, va, exp_ref, out_ref, chunk, first_key, keys, fresh, banded, store_query, pumps):
        rows = chunk_rows(chunk)
        span = pl.ds(first_key, keys)
        cols_all = pl.ds(0, side.size)
        for head in range(heads):
            lanes = pl.ds(head * HEAD_DIM, HEAD_DIM)
            grad_out = r.dot_in[lanes, cols_all]
            spread = jnp.sum(
                grad_out.astype(F32) * out_ref[lanes, rows].astype(F32), axis=0, keepdims=True)
            r.tall[pl.ds(0, keys), cols_all] = dot(va[head, span, pl.ds(0, HEAD_DIM)], grad_out, NN)
            for tile in range(side.size // LANES):
                cols = pl.ds(tile * LANES, LANES)
                cut = spread[:, tile * LANES:(tile + 1) * LANES]
                for key in range(0, keys, LANES):
                    block = pl.ds(key, LANES)
                    weight = exp_ref[
                        head, pl.ds(first_key + key, LANES), pl.ds(chunk * side.size + tile * LANES, LANES)]
                    r.tall_low[block, cols] = (
                        weight.astype(F32) * (r.tall[block, cols] - cut)).astype(BF16)
                if banded:
                    end = chunk * side.size + (tile + 1) * LANES
                    near = min(end, 2 * LANES)
                    r.band_grad[head, pl.ds(2 * LANES - near, near)] += (
                        r.tall_low[pl.ds(end - near, near), cols].astype(F32))
            score_grad = r.tall_low[pl.ds(0, keys), cols_all]
            query_grad = dot(score_grad, ka[head, span], TN)
            store_query(head, (query_grad[:, :HEAD_DIM] * HEAD_DIM ** (-0.5)).astype(BF16))
            key_grad = dot(score_grad, qa[head, rows], NN)
            value_grad = dot(exp_ref[head, span, rows], grad_out, NT)
            if fresh:
                r.dk[head, span] = key_grad
                r.dv[head, span, pl.ds(0, HEAD_DIM)] = value_grad
            else:
                r.dk[head, span] += key_grad
                r.dv[head, span, pl.ds(0, HEAD_DIM)] += value_grad
            if head < pumps:
                pump()

    def grad_of_mixed(weight, grad_ref, inv_ref, chunk):
        grads = dot(weight[...], grad_ref[chunk_rows(chunk)], NT)
        for head in range(heads):
            lanes = pl.ds(head * HEAD_DIM, HEAD_DIM)
            r.dot_in[lanes, pl.ds(0, side.size)] = (
                grads[head * HEAD_DIM:(head + 1) * HEAD_DIM] * inv_ref[pl.ds(head, 1), chunk_rows(chunk)]
            ).astype(BF16)

    def fill_tails(qa, ka, valid):
        shape = (SEQ, HEAD_DIM)
        lane = lax.broadcasted_iota(jnp.int32, shape, 1)
        key = lax.broadcasted_iota(jnp.int32, shape, 0)
        ones = jnp.where(lane == 0, 1.0, 0.0).astype(BF16)
        fence = jnp.where((lane == 0) & jnp.logical_not(valid(key)), NEG, 0.0).astype(BF16)
        for head in range(heads):
            qa[head, :, pl.ds(HEAD_DIM, HEAD_DIM)] = ones
            ka[head, :, pl.ds(HEAD_DIM, HEAD_DIM)] = fence

    def in_passage(key):
        low = (key < HALF) & (key < r.passage_lengths[0, 0])
        return low | ((key >= HALF) & (key - HALF < r.passage_lengths[0, 1]))

    def in_target(key):
        return key < r.target_lengths[0]

    def split_packed(chunk):
        rows = chunk_rows(chunk)
        for head in range(heads):
            base = 3 * HEAD_DIM * head
            low = pl.ds(0, HEAD_DIM)
            r.qa[head, rows, low] = (
                r.pkb[rows, pl.ds(base, HEAD_DIM)].astype(F32) * HEAD_DIM ** (-0.5)).astype(BF16)
            r.ka[head, rows, low] = r.pkb[rows, pl.ds(base + HEAD_DIM, HEAD_DIM)]
            r.va[head, rows, low] = r.pkb[rows, pl.ds(base + 2 * HEAD_DIM, HEAD_DIM)]

    def project_out(line, room, chunk, out_ref, weight, before=None):
        for tile in range(side.size // LANES):
            rows = pl.ds(chunk * side.size + tile * LANES, LANES)
            r.part[room, rows] = dot(out_ref[:, rows], weight[...], TN).astype(BF16)
        hand_on(line, room, chunk, before)

    def param(row):
        return r.params[pl.ds(row, 1)]

    def add_to(slot, values):
        r.acc[slot] += fold(values)

    def gelu_parts(values):
        cubic = 0.7978845608028654 * (values + 0.044715 * values * values * values)
        bend = jnp.tanh(cubic)
        slope = 0.7978845608028654 * (1.0 + 3.0 * 0.044715 * values * values)
        return 0.5 * values * (1.0 + bend), 0.5 * (1.0 + bend) + 0.5 * values * (1.0 - bend * bend) * slope

    def pack_grads(chunk):
        rows = chunk_rows(chunk)
        for head in range(heads):
            base = 3 * HEAD_DIM * head
            low = pl.ds(0, HEAD_DIM)
            r.pkb[rows, pl.ds(base + HEAD_DIM, HEAD_DIM)] = r.dk[head, rows, low].astype(BF16)
            r.pkb[rows, pl.ds(base + 2 * HEAD_DIM, HEAD_DIM)] = r.dv[head, rows, low].astype(BF16)

    def input_part(line, room, chunk, before):
        rows = chunk_rows(chunk)
        r.part[room, rows] = dot(r.pkb[rows], r.w_qkv[...], NN).astype(BF16)
        hand_on(line, room, chunk, before)

    def clear():
        r.acc[...] = jnp.zeros_like(r.acc)
        r.small[...] = jnp.zeros_like(r.small)

    def store_input_grad(chunk):
        rows = chunk_rows(chunk)
        return pltpu.make_async_copy(r.h1f.at[rows], r.gin.at[rows], r.out_sem.at[0, chunk])

    def store_result(chunk):
        rows = chunk_rows(chunk)
        return pltpu.make_async_copy(r.ybuf.at[rows], r.y.at[rows], r.out_sem.at[1, chunk])

    def small_copies():
        copies = []
        for side_step in range(2):
            for steps in range(4):
                if side_step == 0 and steps == 0:
                    continue
                device = (lax.rem(stream + side_step, 2), other(steps), place)
                copies.append(pltpu.make_async_remote_copy(
                    r.small, r.small_got.at[stream * 4 + member], r.small_send.at[len(copies)],
                    r.small_recv.at[stream * 4 + member], device_id=device, device_id_type=MESH))
        return copies

    def start_small():
        for copy in small_copies():
            copy.start()
        r.small_got[stream * 4 + member] = r.small[...]

    def end_small():
        for side_step in range(2):
            for steps in range(4):
                if side_step == 0 and steps == 0:
                    continue
                source = lax.rem(stream + side_step, 2) * 4 + lax.rem(member + steps, 4)
                pltpu.make_async_remote_copy(
                    r.small, r.small_got.at[source], r.small_send.at[0], r.small_recv.at[source],
                    device_id=(stream, mate, place), device_id_type=MESH).wait_recv()
        for copy in small_copies():
            copy.wait_send()
        total = r.small_got[0]
        for index in range(1, 8):
            total = total + r.small_got[index]
        loss = r.small_got[member, pl.ds(12, 1)]
        r.small_out[...] = total
        r.small_out[pl.ds(12, 1)] = loss

    def reader():
        side.size = THIRD
        order = (2, 1, 0)
        for copy in (inputs.hid, inputs.qkv, inputs.proj, inputs.enc, inputs.ckv):
            copy.start()
        for copy in (inputs.cq, inputs.cproj, inputs.up, inputs.down, inputs.cot):
            copy.start()
        clear()
        r.params[pl.ds(8, 3)] = r.scale_gain[...].astype(F32)
        r.mass_rows[...] = jnp.zeros_like(r.mass_rows)
        r.band_grad[...] = jnp.zeros_like(r.band_grad)
        starts = bucket_starts(SEQ, buckets)
        shape = (2 * LANES, LANES)
        apart = (
            lax.broadcasted_iota(jnp.int32, shape, 1) + LANES - lax.broadcasted_iota(jnp.int32, shape, 0))
        for head in range(heads):
            last = r.position_bias[head, buckets - 1]
            band = jnp.full(shape, 0.0, F32) + (r.position_bias[head, 0] - last)
            for bucket in range(1, buckets):
                band = jnp.where(apart >= starts[bucket], r.position_bias[head, bucket] - last, band)
            r.band[head] = jnp.where(apart >= 0, band, NEG)
        fill_tails(r.qa, r.ka, in_target)
        fill_tails(r.cqa, r.cka, in_passage)

        inputs.hid.wait()
        gain = param(8)
        for chunk in order:
            def normalize(rows, _):
                values = r.hid[rows].astype(F32)
                r.buf_a[rows] = (values * lax.rsqrt(mean(values * values) + EPS) * gain).astype(BF16)
            row_loop(chunk, normalize)
        inputs.qkv.wait()
        r.pkb[...] = dot(r.buf_a[...], r.w_qkv[...], NT).astype(BF16)
        for chunk in order:
            split_packed(chunk)
        inputs.proj.wait()
        for chunk in order:
            attend(
                r.qa, r.ka, r.va, r.e1, r.o1, r.linv1, chunk, 0, (chunk + 1) * THIRD, True, False,
                1 if chunk == order[-1] else 0)
            if chunk == order[0]:
                meet()
            project_out(0, 0, chunk, r.o1, r.w_proj)

        inputs.enc.wait()
        for chunk in order:
            def lower(rows, _):
                r.encb[rows] = r.h2f[rows].astype(BF16)
            row_loop(chunk, lower)
        inputs.ckv.wait()
        pump()
        for chunk in order:
            rows = chunk_rows(chunk)
            r.ckb[rows] = dot(r.encb[rows], r.w_ckv[...], NN).astype(BF16)
            for head in range(heads):
                low = pl.ds(0, HEAD_DIM)
                r.cka[head, rows, low] = r.ckb[rows, pl.ds(2 * HEAD_DIM * head, HEAD_DIM)]
                r.cva[head, rows, low] = r.ckb[rows, pl.ds(2 * HEAD_DIM * head + HEAD_DIM, HEAD_DIM)]
        pump()
        inputs.down.wait()
        inputs.cot.wait()
        r.buf_c[...] = dot(r.cot[...], r.w_down[...], NT).astype(BF16)
        inputs.cq.wait()
        inputs.cproj.wait()
        inputs.up.wait()

        gain = param(9)
        for chunk in order:
            rows = chunk_rows(chunk)
            collect(0, 0, chunk)

            def first_sum(rows, _):
                values = r.hid[rows].astype(F32) + r.total[0, rows].astype(F32)
                r.h1f[rows] = values
                r.buf_b[rows] = (values * lax.rsqrt(mean(values * values) + EPS) * gain).astype(BF16)
            row_loop(chunk, first_sum)
            r.cqb[rows] = dot(r.buf_b[rows], r.w_cq[...], NT).astype(BF16)
            for head in range(heads):
                r.cqa[head, rows, pl.ds(0, HEAD_DIM)] = (
                    r.cqb[rows, pl.ds(head * HEAD_DIM, HEAD_DIM)].astype(F32) * HEAD_DIM ** (-0.5)
                ).astype(BF16)
            attend(r.cqa, r.cka, r.cva, r.e2, r.o2, r.linv2, chunk, 0, SEQ, False, True, 2)
            project_out(1, 1, chunk, r.o2, r.w_cproj, (0, 0))

        lane = lax.broadcasted_iota(jnp.int32, (8, LANES), 1)
        masses = [jnp.sum(r.mass_rows[pl.ds(p, 1)], axis=1, keepdims=True) for p in range(NPASS)]
        r.mass[...] = jnp.where(lane == 0, masses[0], jnp.where(lane == 1, masses[1], 0.0))

        def mass_copy(steps):
            return pltpu.make_async_remote_copy(
                r.mass, r.mass_got.at[place], r.mass_send.at[steps], r.mass_recv.at[place],
                device_id=(1 - stream, query, lax.rem(place + steps, 4)), device_id_type=MESH)

        for steps in range(4):
            mass_copy(steps).start()

        gain = param(10)
        for chunk in order:
            rows = chunk_rows(chunk)
            collect(1, 1, chunk)

            def second_sum(rows, _):
                values = r.h1f[rows] + r.total[1, rows].astype(F32)
                r.h2f[rows] = values
                r.ybuf[rows] = values.astype(BF16)
                r.buf_u[rows] = (values * lax.rsqrt(mean(values * values) + EPS) * gain).astype(BF16)
            row_loop(chunk, second_sum)
            r.wide[pl.ds(0, side.size)] = dot(r.buf_u[rows], r.w_up[...], NN)
            pump()

            def bend(rows, local):
                value, slope = gelu_parts(r.wide[local])
                r.act[rows] = value.astype(BF16)
                r.dpre[rows] = (r.buf_c[rows].astype(F32) * slope).astype(BF16)
            row_loop(chunk, bend)
            pump()
            r.part[0, rows] = dot(r.dpre[rows], r.w_up[...], NT).astype(BF16)
            hand_on(2, 0, chunk, (1, 1))
            r.part[2, rows] = dot(r.act[rows], r.w_down[...], NN).astype(BF16)
            hand_over(chunk).start()

        r.d_up[...] = dot(r.buf_u[...], r.dpre[...], TN).astype(BF16)
        w_start(UP)
        pump()
        r.d_down[...] = dot(r.act[...], r.cot[...], TN).astype(BF16)
        w_start(DOWN)
        pump()

        for chunk in order:
            rows = chunk_rows(chunk)
            collect(2, 0, chunk)

            def second_grad(rows, _):
                values = r.h2f[rows]
                grads = r.total[0, rows].astype(F32)
                root = lax.rsqrt(mean(values * values) + EPS)
                add_to(2, grads * values * root)
                scaled = grads * gain
                back = root * scaled - values * (root * root * root) * mean(scaled * values)
                result = r.cot[rows].astype(F32) + back
                r.h2f[rows] = result
                r.buf_c[rows] = result.astype(BF16)
            row_loop(chunk, second_grad)
            grad_of_mixed(r.w_cproj, r.buf_c, r.linv2, chunk)

            def store_query(head, values):
                r.cqb[chunk_rows(chunk), pl.ds(head * HEAD_DIM, HEAD_DIM)] = values

            attend_back(
                r.cqa, r.cka, r.cva, r.e2, r.o2, chunk, 0, SEQ, chunk == order[0], False, store_query, 2)
            r.part[1, rows] = dot(r.cqb[rows], r.w_cq[...], NN).astype(BF16)
            hand_on(3, 1, chunk, (2, 0))

        w_combine(UP)
        w_combine(DOWN)
        pump()
        for chunk in order:
            rows = chunk_rows(chunk)
            for head in range(heads):
                low = pl.ds(0, HEAD_DIM)
                r.ckb[rows, pl.ds(2 * HEAD_DIM * head, HEAD_DIM)] = r.dk[head, rows, low].astype(BF16)
                r.ckb[rows, pl.ds(2 * HEAD_DIM * head + HEAD_DIM, HEAD_DIM)] = (
                    r.dv[head, rows, low].astype(BF16))
        r.d_cproj[...] = dot(r.o2[...], r.buf_c[...], NN).astype(BF16)
        w_start(CPROJ)
        r.d_cq[...] = dot(r.cqb[...], r.buf_b[...], TN).astype(BF16)
        w_start(CQ)
        pump()
        r.d_ckv[...] = dot(r.encb[...], r.ckb[...], TN).astype(BF16)
        w_start(CKV)

        gain = param(9)
        for chunk in order:
            rows = chunk_rows(chunk)
            collect(3, 1, chunk)

            def first_grad(rows, _):
                values = r.h1f[rows]
                grads = r.total[1, rows].astype(F32)
                root = lax.rsqrt(mean(values * values) + EPS)
                add_to(1, grads * values * root)
                scaled = grads * gain
                back = root * scaled - values * (root * root * root) * mean(scaled * values)
                result = r.h2f[rows] + back
                r.h1f[rows] = result
                r.ag[rows] = result.astype(BF16)
            row_loop(chunk, first_grad)
            grad_of_mixed(r.w_proj, r.ag, r.linv1, chunk)

            def store_query(head, values):
                r.pkb[chunk_rows(chunk), pl.ds(3 * HEAD_DIM * head, HEAD_DIM)] = values

            attend_back(
                r.qa, r.ka, r.va, r.e1, r.o1, chunk, 0, (chunk + 1) * THIRD, chunk == order[0], True,
                store_query, 2)
            pack_grads(chunk)
            input_part(4, 0, chunk, (3, 1))
        r.d_qkv[...] = dot(r.pkb[...], r.buf_a[...], TN).astype(BF16)
        w_start(QKV)
        r.d_proj[...] = dot(r.o1[...], r.ag[...], NN).astype(BF16)
        w_start(PROJ)
        pump()
        for name in (CPROJ, CQ, CKV):
            w_combine(name)
        pump()
        w_combine(QKV)
        w_combine(PROJ)
        w_store(UP)
        w_store(DOWN)
        pump()

        lane = lax.broadcasted_iota(jnp.int32, (1, LANES), 1)
        table = jnp.zeros((1, LANES), F32)
        for head in range(heads):
            grads = r.band_grad[head]
            rest = jnp.sum(
                jnp.sum(r.dk[head], axis=0, keepdims=True)[:, HEAD_DIM:HEAD_DIM + 1], axis=1, keepdims=True)
            for bucket in range(buckets - 1):
                inside = (apart >= starts[bucket]) & (apart < starts[bucket + 1])
                value = jnp.sum(
                    jnp.sum(jnp.where(inside, grads, 0.0), axis=0, keepdims=True), axis=1, keepdims=True)
                rest = rest - value
                table = jnp.where(lane == head * buckets + bucket, value, table)
            table = jnp.where(lane == head * buckets + buckets - 1, rest, table)
        r.small[pl.ds(11, 1), pl.ds(0, LANES)] = table

        gain = param(8)
        for chunk in order:
            collect(4, 0, chunk)

            def input_grad(rows, _):
                values = r.hid[rows].astype(F32)
                grads = r.total[0, rows].astype(F32)
                root = lax.rsqrt(mean(values * values) + EPS)
                add_to(0, grads * values * root)
                scaled = grads * gain
                back = root * scaled - values * (root * root * root) * mean(scaled * values)
                r.h1f[rows] = r.h1f[rows] + back
            row_loop(chunk, input_grad)
            store_input_grad(chunk).start()
            if chunk == order[0]:
                for name in (CPROJ, CQ, CKV):
                    w_store(name)

        for slot in range(3):
            r.small[pl.ds(8 + slot, 1)] = jnp.sum(r.acc[slot], axis=0, keepdims=True)
        start_small()
        w_store(QKV)
        w_store(PROJ)
        for chunk in order:
            hand_back(chunk).wait_recv()

            def last_sum(rows, _):
                r.ybuf[rows] = (r.ybuf[rows].astype(F32) + r.total[2, rows].astype(F32)).astype(BF16)
            row_loop(chunk, last_sum)
            store_result(chunk).start()
        end_small()
        for chunk in order:
            settle(4, 0, chunk_pieces(chunk))
            hand_over(chunk).wait_send()
            store_input_grad(chunk).wait()
            store_result(chunk).wait()
        for name in WEIGHTS:
            w_end(name)
        for steps in range(4):
            mass_copy(steps).wait_send()

    def retriever():
        side.size = HALF
        order = (1, 0)
        for copy in (inputs.hid, inputs.qkv, inputs.proj, inputs.up, inputs.down, inputs.cot):
            copy.start()
        clear()
        r.params[pl.ds(0, 2)] = r.layer_gain[...].astype(F32)
        r.params[pl.ds(2, 2)] = r.layer_shift[...].astype(F32)
        r.params[pl.ds(4, 2)] = r.output_bias[...].astype(F32)
        r.params[pl.ds(6, 1)] = r.unit_bias[...].astype(F32)
        r.colsum[...] = jnp.zeros_like(r.colsum)
        r.params[pl.ds(11, 1), pl.ds(0, 2 * heads * HEAD_DIM)] = r.qv_bias[...].astype(F32)
        for head in range(heads):
            base = 3 * HEAD_DIM * head
            for k in range(2):
                r.colsum[pl.ds(0, 1), pl.ds(base + 2 * k * HEAD_DIM, HEAD_DIM)] = (
                    r.params[pl.ds(11, 1), pl.ds((2 * head + k) * HEAD_DIM, HEAD_DIM)])
        shift = r.colsum[pl.ds(0, 1)]
        fill_tails(r.qa, r.ka, in_passage)
        inputs.hid.wait()
        inputs.qkv.wait()
        inputs.proj.wait()
        for chunk in order:
            rows = chunk_rows(chunk)
            r.pkb[rows] = (dot(r.hid[rows], r.w_qkv[...], NT) + shift).astype(BF16)
            split_packed(chunk)
            attend(r.qa, r.ka, r.va, r.e1, r.o1, r.linv1, chunk, chunk * HALF, HALF, False, False, 0)
            if chunk == order[0]:
                meet()
            project_out(0, 0, chunk, r.o1, r.w_proj)
        r.colsum[...] = jnp.zeros_like(r.colsum)

        inputs.up.wait()
        inputs.down.wait()
        inputs.cot.wait()
        gain1, gain2 = param(0), param(1)
        shift1, shift2 = param(2), param(3)
        out1, out2, unit = param(4), param(5), param(6)
        for chunk in order:
            rows = chunk_rows(chunk)
            collect(0, 0, chunk)

            def first_norm(rows, _):
                values = r.hid[rows].astype(F32) + r.total[0, rows].astype(F32) + out1
                centered = values - mean(values)
                root = lax.rsqrt(mean(centered * centered) + EPS)
                r.h1f[rows] = values
                r.buf_u[rows] = (centered * root * gain1 + shift1).astype(BF16)
            row_loop(chunk, first_norm)
            r.wide[...] = dot(r.buf_u[rows], r.w_up[...], NN)
            pump()

            def bend(rows, local):
                value, slope = gelu_parts(r.wide[local] + unit)
                r.act[rows] = value.astype(BF16)
                r.buf_a[rows] = slope.astype(BF16)
            row_loop(chunk, bend)
            pump()
            for tile in range(HALF // LANES):
                rows = pl.ds(chunk * HALF + tile * LANES, LANES)
                r.part[1, rows] = dot(r.act[rows], r.w_down[...], NN).astype(BF16)
            hand_on(1, 1, chunk, (0, 0))

        for chunk in order:
            collect(1, 1, chunk)
            length = r.passage_lengths[0, chunk]

            def second_norm(rows, local):
                values = r.h1f[rows]
                centered = values - mean(values)
                root = lax.rsqrt(mean(centered * centered) + EPS)
                values = centered * root * gain1 + shift1 + r.total[1, rows].astype(F32) + out2
                r.h2f[rows] = values
                centered = values - mean(values)
                root = lax.rsqrt(mean(centered * centered) + EPS)
                result = centered * root * gain2 + shift2
                r.ybuf[rows] = result.astype(BF16)
                token = lax.broadcasted_iota(jnp.int32, (PIECE, 1), 0) + local.start
                add_to(8 + chunk, jnp.where(token < length, result, 0.0))
            row_loop(chunk, second_norm)
            store_result(chunk).start()

        vector = r.query_vectors[...]
        scores = [
            jnp.sum(jnp.sum(r.acc[8 + p], axis=0, keepdims=True) * vector, axis=1, keepdims=True)
            / r.passage_lengths[0, p].astype(F32)
            for p in range(NPASS)
        ]

        def mass_wait(source):
            return pltpu.make_async_remote_copy(
                r.mass, r.mass_got.at[source], r.mass_send.at[0], r.mass_recv.at[source],
                device_id=(1 - stream, query, place), device_id_type=MESH)

        for source in range(4):
            mass_wait(source).wait_recv()
        masses = r.mass_got[0].astype(BF16).astype(F32)
        for source in range(1, 4):
            masses = masses + r.mass_got[source].astype(BF16).astype(F32)
        scale = HEADS * r.target_lengths[0].astype(F32)
        targets = [masses[0:1, p:p + 1] / scale for p in range(NPASS)]
        top = jnp.maximum(scores[0], scores[1])
        norm = top + jnp.log(jnp.exp(scores[0] - top) + jnp.exp(scores[1] - top))
        logs = [score - norm for score in scores]
        loss = targets[0] * (jnp.log(targets[0]) - logs[0]) + targets[1] * (jnp.log(targets[1]) - logs[1])
        r.small[pl.ds(12, 1)] = jnp.broadcast_to(loss, (1, WIDTH))
        pulls = [
            (jnp.exp(logs[p]) * (targets[0] + targets[1]) - targets[p])
            / r.passage_lengths[0, p].astype(F32) * vector
            for p in range(NPASS)
        ]

        for chunk in order:
            rows = chunk_rows(chunk)
            length = r.passage_lengths[0, chunk]
            pull = pulls[chunk]

            def final_grad(rows, local):
                token = lax.broadcasted_iota(jnp.int32, (PIECE, 1), 0) + local.start
                upstream = r.cot[rows].astype(F32) + jnp.where(token < length, pull, 0.0)
                values = r.h2f[rows]
                centered = values - mean(values)
                root = lax.rsqrt(mean(centered * centered) + EPS)
                normed = centered * root
                scaled = upstream * gain2
                result = root * (scaled - mean(scaled) - normed * mean(scaled * normed))
                add_to(1, upstream * normed)
                add_to(3, upstream)
                r.h2f[rows] = result
                low = result.astype(BF16)
                r.buf_b[rows] = low
                add_to(5, low.astype(F32))
            row_loop(chunk, final_grad)
            r.wide[...] = dot(r.buf_b[rows], r.w_down[...], NT)

            def bend_back(rows, local):
                low = (r.wide[local] * r.buf_a[rows].astype(F32)).astype(BF16)
                r.dpre[rows] = low
                add_to(6, low.astype(F32))
            row_loop(chunk, bend_back)
            r.part[0, rows] = dot(r.dpre[rows], r.w_up[...], NT).astype(BF16)
            hand_on(2, 0, chunk, (1, 1))

        r.d_up[...] = dot(r.buf_u[...], r.dpre[...], TN).astype(BF16)
        w_start(UP)
        r.d_down[...] = dot(r.act[...], r.buf_b[...], TN).astype(BF16)
        w_start(DOWN)

        for chunk in (2, 1, 0):
            hand_over(chunk).wait_recv()
            produce(5, 2, third_pieces(chunk))

        for chunk in order:
            rows = chunk_rows(chunk)
            collect(2, 0, chunk)

            def middle_grad(rows, _):
                upstream = r.h2f[rows] + r.total[0, rows].astype(F32)
                values = r.h1f[rows]
                centered = values - mean(values)
                root = lax.rsqrt(mean(centered * centered) + EPS)
                normed = centered * root
                scaled = upstream * gain1
                result = root * (scaled - mean(scaled) - normed * mean(scaled * normed))
                add_to(0, upstream * normed)
                add_to(2, upstream)
                r.h1f[rows] = result
                low = result.astype(BF16)
                r.ag[rows] = low
                add_to(4, low.astype(F32))
            row_loop(chunk, middle_grad)
            grad_of_mixed(r.w_proj, r.ag, r.linv1, chunk)

            def store_query(head, values):
                r.pkb[chunk_rows(chunk), pl.ds(3 * HEAD_DIM * head, HEAD_DIM)] = values

            attend_back(
                r.qa, r.ka, r.va, r.e1, r.o1, chunk, chunk * HALF, HALF, True, False, store_query, 2)
            pack_grads(chunk)
            input_part(4, 1, chunk, (2, 0))
            r.colsum[...] += fold(r.pkb[rows].astype(F32))
        w_combine(UP)
        w_combine(DOWN)
        r.d_qkv[...] = dot(r.pkb[...], r.hid[...], TN).astype(BF16)
        w_start(QKV)
        r.d_proj[...] = dot(r.o1[...], r.ag[...], NN).astype(BF16)
        w_start(PROJ)
        pump()

        for chunk in (2, 1, 0):
            finish(5, 2, third_pieces(chunk))
            hand_back(chunk).start()
            if chunk == 1:
                w_combine(QKV)
                w_combine(PROJ)
        w_store(UP)
        w_store(DOWN)
        for chunk in order:
            rows = chunk_rows(chunk)
            collect(4, 1, chunk)

            def input_grad(rows, _):
                r.h1f[rows] = r.h1f[rows] + r.total[1, rows].astype(F32)
            row_loop(chunk, input_grad)
            store_input_grad(chunk).start()

        columns = jnp.sum(r.colsum[...], axis=0, keepdims=True)
        r.colsum[pl.ds(0, 1)] = columns
        for head in range(heads):
            base = 3 * HEAD_DIM * head
            for k in range(2):
                r.small[pl.ds(0, 1), pl.ds((2 * head + k) * HEAD_DIM, HEAD_DIM)] = (
                    r.colsum[pl.ds(0, 1), pl.ds(base + 2 * k * HEAD_DIM, HEAD_DIM)])
        r.small[pl.ds(1, 1)] = jnp.sum(r.acc[6], axis=0, keepdims=True)
        for slot in range(6):
            r.small[pl.ds(2 + slot, 1)] = jnp.sum(r.acc[slot], axis=0, keepdims=True)
        start_small()
        w_store(QKV)
        w_store(PROJ)
        end_small()
        for chunk in order:
            settle(4, 1, chunk_pieces(chunk))
            store_input_grad(chunk).wait()
            store_result(chunk).wait()
        for chunk in (2, 1, 0):
            settle(5, 2, third_pieces(chunk))
            hand_back(chunk).wait_send()
        for name in (UP, DOWN, QKV, PROJ):
            w_end(name)
        for name in (CQ, CKV, CPROJ):
            index, grad, rc, ry, mine, theirs = w_parts(name)
            out = getattr(r, name)
            w_copy(grad.at[mine], out.at[mine], index, 4, 3, (1 - stream, query, place)).wait_recv()
            w_copy(grad.at[mine], out.at[theirs], index, 5, 4, (1 - stream, query, place)).wait_recv()

    @pl.when(is_reader)
    def _():
        reader()

    for items in (made, added, summed):
        items.clear()

    @pl.when(jnp.logical_not(is_reader))
    def _():
        retriever()


def local(
    batch,
    hidden,
    cotangent,
    qkv_weight,
    proj_weight,
    up_weight,
    down_weight,
    query_value_bias,
    unit_bias,
    layer_gain,
    layer_shift,
    output_bias,
    scale_gain,
    position_bias,
    cross_query,
    cross_key_value,
    cross_proj,
    encodings,
    query_vectors,
    passage_lengths,
    target_lengths,
):
    heads = proj_weight.shape[1] // HEAD_DIM
    buckets = position_bias.shape[1]
    inner = heads * HEAD_DIM
    far = dict(
        hidden=hidden, cotangent=cotangent, qkv_weight=qkv_weight[0].T, proj_weight=proj_weight,
        up_weight=up_weight, down_weight=down_weight, cross_query=cross_query.T,
        cross_key_value=cross_key_value, cross_proj=cross_proj, encodings=encodings)
    near = dict(
        qv_bias=query_value_bias.reshape(1, -1), unit_bias=unit_bias.reshape(1, -1),
        layer_gain=layer_gain, layer_shift=layer_shift, output_bias=output_bias,
        scale_gain=scale_gain, query_vectors=query_vectors)
    scalars = dict(
        passage_lengths=passage_lengths, target_lengths=target_lengths,
        position_bias=position_bias.astype(F32))
    anywhere = pl.BlockSpec(memory_space=pl.ANY)
    vector = pl.BlockSpec(memory_space=pltpu.VMEM)
    scalar = pl.BlockSpec(memory_space=pltpu.SMEM)
    out_shapes = dict(
        small_out=jax.ShapeDtypeStruct((16, WIDTH), F32),
        y=jax.ShapeDtypeStruct((SEQ, WIDTH), BF16),
        gin=jax.ShapeDtypeStruct((SEQ, WIDTH), F32))
    for name, shape in weight_shapes(heads).items():
        out_shapes[name] = jax.ShapeDtypeStruct(shape, BF16)
    shapes = scratch_shapes(heads)
    names = [*far, *near, *scalars, *out_shapes, *shapes]
    small, result, input_grad, *grads = pl.pallas_call(
        partial(layer_kernel, heads, buckets, names),
        out_shape=list(out_shapes.values()),
        in_specs=[anywhere] * len(far) + [vector] * len(near) + [scalar] * len(scalars),
        out_specs=[vector] + [anywhere] * (len(out_shapes) - 1),
        scratch_shapes=list(shapes.values()),
        compiler_params=pltpu.CompilerParams(
            collective_id=0, has_side_effects=True, vmem_limit_bytes=63 * 2**20),
    )(*far.values(), *near.values(), *scalars.values())
    grads = [grad.astype(F32) for grad in grads]
    rows = small[:12]
    if batch > 4:
        groups = [[first + step for step in range(0, batch, 4)] for first in range(4)]
        grads, rows = lax.psum((grads, rows), BATCH, axis_index_groups=groups)
    up, down, qkv, proj, cq, ckv, cproj = grads
    return (
        result[None],
        input_grad[None],
        qkv.T[None],
        proj[None],
        up[None],
        down[None],
        rows[0, : 2 * inner],
        rows[1],
        rows[2:4],
        rows[4:6],
        rows[6:8],
        rows[8:11],
        rows[11, : heads * buckets].reshape(heads, buckets),
        cq.T,
        ckv,
        cproj,
        small[12, :1],
    )


def solution(mesh):
    rows = P(STREAM, BATCH, None)
    columns_split = P(STREAM, None, TENSOR)
    rows_split = P(STREAM, TENSOR, None)
    weights = (columns_split, rows_split, columns_split, rows_split)
    cross = (P(None, TENSOR), P(None, TENSOR), P(TENSOR, None))
    vectors = (P(TENSOR), P(TENSOR), P(), P(), P(), P(), P(TENSOR, None))
    in_specs = (rows, rows, *weights, *vectors, *cross)
    in_specs = (*in_specs, P(BATCH, None, None), P(BATCH, None), P(BATCH, None), P(BATCH))
    out_specs = (rows, rows, *weights, *vectors, *cross, P(BATCH))
    return jax.shard_map(
        partial(local, mesh.shape[BATCH]), mesh=mesh, in_specs=in_specs, out_specs=out_specs,
        check_vma=False)
```

```python
from functools import partial

import jax
import jax.numpy as jnp
import numpy as np
from jax import lax
from jax.experimental import pallas as pl
from jax.experimental.pallas import tpu as pltpu
from jax.sharding import PartitionSpec as P

HEADS = 12
HEAD_DIM = 64
PLEN = 384
NPASS = 2
SEQ = 768
WIDTH = 768
HALF = 384
THIRD = 256
PIECE = 64
PIECES = SEQ // PIECE
AHEAD = 3
LANES = 128

EPS = 1e-06
NEG = -1000000000.0
MESH = pl.DeviceIdType.MESH
BF16 = jnp.bfloat16
F32 = jnp.float32

NN = (((1,), (0,)), ((), ()))
NT = (((1,), (1,)), ((), ()))
TN = (((0,), (0,)), ((), ()))

STREAM, BATCH, TENSOR = "stream", "batch", "tensor"
UP, DOWN, QKV, PROJ, CQ, CKV, CPROJ = "up", "down", "qkv", "proj", "cq", "ckv", "cproj"
WEIGHTS = (UP, DOWN, QKV, PROJ, CQ, CKV, CPROJ)


def bucket_starts(length, buckets):
    exact = buckets // 2
    distance = np.arange(length)
    far_bucket = exact + (
        np.log(np.maximum(distance, 1) / exact) / np.log(128.0 / exact) * (buckets - exact)
    ).astype(np.int64)
    near_table = np.where(distance < exact, distance, np.minimum(far_bucket, buckets - 1))
    return [int(np.argmax(near_table == bucket)) for bucket in range(buckets)]


def dot(left, right, dims):
    return lax.dot_general(left, right, dims, preferred_element_type=F32)


def fold(values):
    return jnp.sum(values.reshape(values.shape[0] // 8, 8, values.shape[1]), axis=0)


def mean(values):
    return jnp.mean(values, axis=-1, keepdims=True)


def weight_shapes(heads):
    inner = heads * HEAD_DIM
    return dict(
        up=(WIDTH, WIDTH),
        down=(WIDTH, WIDTH),
        qkv=(3 * inner, WIDTH),
        proj=(inner, WIDTH),
        cq=(inner, WIDTH),
        ckv=(WIDTH, 2 * inner),
        cproj=(inner, WIDTH),
    )


def scratch_shapes(heads):
    inner = heads * HEAD_DIM

    def low(*shape):
        return pltpu.VMEM(shape, BF16)

    def full(*shape):
        return pltpu.VMEM(shape, F32)

    whole = low(SEQ, WIDTH)
    head_rows = low(heads, SEQ, LANES)
    head_sums = full(heads, SEQ, LANES)
    scores = low(heads, SEQ, SEQ)
    bands = full(heads, 2 * LANES, LANES)
    room = low(3, SEQ, WIDTH)
    line = pltpu.SemaphoreType.DMA((3, 6, PIECES))
    shapes = dict(
        hid=whole, cot=whole, encb=whole, buf_a=whole, buf_b=whole, buf_c=whole, buf_u=whole,
        act=whole, dpre=whole, ag=whole, ybuf=whole,
        h1f=full(SEQ, WIDTH), h2f=full(SEQ, WIDTH),
        qa=head_rows, ka=head_rows, va=head_rows, cqa=head_rows, cka=head_rows, cva=head_rows,
        dk=head_sums, dv=head_sums, e1=scores, e2=scores,
        o1=low(inner, SEQ), o2=low(inner, SEQ), dot_in=low(inner, HALF),
        linv1=full(heads, 8, SEQ), linv2=full(heads, 8, SEQ),
        pkb=low(SEQ, 3 * inner), cqb=low(SEQ, inner), ckb=low(SEQ, 2 * inner),
        tall=full(SEQ, HALF), tall_low=low(SEQ, THIRD), wide=full(THIRD, WIDTH),
        band=bands, band_grad=bands, params=full(16, WIDTH), acc=full(10, 8, WIDTH),
        colsum=full(8, 3 * inner), mass_rows=full(8, HALF),
        small=full(16, WIDTH), small_got=full(8, 16, WIDTH), mass=full(8, LANES),
        mass_got=full(4, 8, LANES), part=room, outer=room, total=room,
        in_sem=pltpu.SemaphoreType.DMA((10,)), line_send=line, line_recv=line,
        w_send=pltpu.SemaphoreType.DMA((7, 6)), w_recv=pltpu.SemaphoreType.DMA((7, 5)),
        small_send=pltpu.SemaphoreType.DMA((7,)), small_recv=pltpu.SemaphoreType.DMA((8,)),
        mass_send=pltpu.SemaphoreType.DMA((4,)), mass_recv=pltpu.SemaphoreType.DMA((4,)),
        out_sem=pltpu.SemaphoreType.DMA((2, 3)),
        over_send=pltpu.SemaphoreType.DMA((2, 3)), over_recv=pltpu.SemaphoreType.DMA((2, 3)),
    )
    for name, shape in weight_shapes(heads).items():
        half = (shape[0] // 2, shape[1])
        shapes["w_" + name] = low(*shape)
        shapes["d_" + name] = low(*shape)
        shapes["rc_" + name] = low(*half)
        shapes["ry_" + name] = low(*half)
    return shapes


class Refs:
    pass


def layer_kernel(heads, buckets, names, *refs):
    r = Refs()
    for name, ref in zip(names, refs):
        setattr(r, name, ref)
    stream, query, place = (lax.axis_index(name) for name in (STREAM, BATCH, TENSOR))
    is_reader = stream == 1
    is_end = (place == 0) | (place == 3)
    is_middle = jnp.logical_not(is_end)
    inner_place = jnp.where(place == 0, 1, jnp.where(place == 3, 2, 3 - place))
    outer_place = jnp.where(place == 1, 0, 3)
    core = lax.rem(query, 2)
    group = query - lax.rem(query, 4)
    member = lax.rem(query, 4)

    def other(steps):
        return group + lax.rem(member + steps, 4)

    mate = query + 1 - 2 * core
    across_y = group + lax.rem(member + 2, 4)

    barrier = pltpu.get_barrier_semaphore()

    def greet(device):
        pl.semaphore_signal(barrier, inc=1, device_id=device, device_id_type=MESH)

    for steps in range(1, 4):
        greet((stream, other(steps), place))
    for steps in range(4):
        greet((1 - stream, other(steps), place))
    for steps in range(1, 4):
        greet((1 - stream, query, lax.rem(place + steps, 4)))
    greet((stream, query, inner_place))

    @pl.when(is_middle)
    def _():
        greet((stream, query, outer_place))

    def meet():
        @pl.when(is_end)
        def _():
            pl.semaphore_wait(barrier, 11)

        @pl.when(is_middle)
        def _():
            pl.semaphore_wait(barrier, 12)

    def bring(index, source, target):
        return pltpu.make_async_copy(source, target, r.in_sem.at[index])

    inputs = Refs()
    inputs.hid = bring(0, r.hidden.at[0], r.hid)
    inputs.qkv = bring(1, r.qkv_weight, r.w_qkv)
    inputs.proj = bring(2, r.proj_weight.at[0], r.w_proj)
    inputs.enc = bring(3, r.encodings.at[0], r.h2f)
    inputs.ckv = bring(4, r.cross_key_value, r.w_ckv)
    inputs.cq = bring(5, r.cross_query, r.w_cq)
    inputs.cproj = bring(6, r.cross_proj, r.w_cproj)
    inputs.up = bring(7, r.up_weight.at[0], r.w_up)
    inputs.down = bring(8, r.down_weight.at[0], r.w_down)
    inputs.cot = bring(9, r.cotangent.at[0], r.cot)

    def piece_rows(piece):
        return pl.ds(piece * PIECE, PIECE)

    side = Refs()

    def chunk_rows(chunk):
        return pl.ds(chunk * side.size, side.size)

    def row_loop(chunk, body):
        @pl.loop(0, side.size // LANES)
        def _(step):
            body(pl.ds(pl.multiple_of(chunk * side.size + step * LANES, LANES), LANES),
                 pl.ds(pl.multiple_of(step * LANES, LANES), LANES))

    def to_middle(line, room, piece):
        rows = piece_rows(piece)
        return pltpu.make_async_remote_copy(
            r.part.at[room, rows], r.outer.at[room, rows],
            r.line_send.at[0, line, piece], r.line_recv.at[0, line, piece],
            device_id=(stream, query, inner_place), device_id_type=MESH)

    def across(line, room, piece):
        rows = piece_rows(piece)
        return pltpu.make_async_remote_copy(
            r.outer.at[room, rows], r.total.at[room, rows],
            r.line_send.at[1, line, piece], r.line_recv.at[1, line, piece],
            device_id=(stream, query, inner_place), device_id_type=MESH)

    def to_end(line, room, piece):
        rows = piece_rows(piece)
        return pltpu.make_async_remote_copy(
            r.total.at[room, rows], r.total.at[room, rows],
            r.line_send.at[2, line, piece], r.line_recv.at[2, line, piece],
            device_id=(stream, query, outer_place), device_id_type=MESH)

    made, added, summed = [], [], []

    def chunk_pieces(chunk):
        count = side.size // PIECE
        return range(chunk * count, (chunk + 1) * count)

    def produce(line, room, pieces):
        @pl.when(is_end)
        def _():
            for piece in pieces:
                to_middle(line, room, piece).start()

        made.extend((line, room, piece) for piece in pieces)

    def add_outer(line, room, piece):
        rows = piece_rows(piece)
        to_middle(line, room, piece).wait_recv()
        r.outer[room, rows] += r.part[room, rows]
        across(line, room, piece).start()

    def add_inner(line, room, piece):
        rows = piece_rows(piece)
        across(line, room, piece).wait_recv()
        r.total[room, rows] += r.outer[room, rows]
        to_end(line, room, piece).start()

    def advance():
        if len(added) < len(made) and len(added) - len(summed) < AHEAD:
            item = made[len(added)]
            added.append(item)
            add_outer(*item)
        else:
            item = made[len(summed)]
            summed.append(item)
            add_inner(*item)

    def pump(count=1):
        steps = min(2 * count, 2 * len(made) - len(added) - len(summed))
        if steps > 0:
            @pl.when(is_middle)
            def _():
                for _ in range(steps):
                    advance()

    def finish(line, room, pieces):
        last = max(made.index((line, room, piece)) for piece in pieces)

        @pl.when(is_middle)
        def _():
            while len(summed) <= last:
                advance()

        @pl.when(is_end)
        def _():
            for piece in pieces:
                to_end(line, room, piece).wait_recv()
                to_middle(line, room, piece).wait_send()

    def settle(line, room, pieces):
        @pl.when(is_middle)
        def _():
            for piece in pieces:
                across(line, room, piece).wait_send()
                to_end(line, room, piece).wait_send()

    def hand_on(line, room, chunk, before=None):
        pieces = chunk_pieces(chunk)
        if before:
            settle(*before, pieces)
        produce(line, room, pieces)

    def collect(line, room, chunk):
        finish(line, room, chunk_pieces(chunk))

    def hand_over(chunk):
        rows = pl.ds(chunk * THIRD, THIRD)
        return pltpu.make_async_remote_copy(
            r.part.at[2, rows], r.part.at[2, rows], r.over_send.at[0, chunk], r.over_recv.at[0, chunk],
            device_id=(1 - stream, query, place), device_id_type=MESH)

    def hand_back(chunk):
        rows = pl.ds(chunk * THIRD, THIRD)
        return pltpu.make_async_remote_copy(
            r.total.at[2, rows], r.total.at[2, rows], r.over_send.at[1, chunk], r.over_recv.at[1, chunk],
            device_id=(1 - stream, query, place), device_id_type=MESH)

    def third_pieces(chunk):
        count = THIRD // PIECE
        return range(chunk * count, (chunk + 1) * count)

    def w_copy(source, target, index, send, recv, device):
        return pltpu.make_async_remote_copy(
            source, target, r.w_send.at[index, send], r.w_recv.at[index, recv],
            device_id=device, device_id_type=MESH)

    def w_parts(name):
        grad = getattr(r, "d_" + name)
        half = grad.shape[0] // 2
        mine = pl.ds(pl.multiple_of(core * half, half), half)
        theirs = pl.ds(pl.multiple_of((1 - core) * half, half), half)
        return WEIGHTS.index(name), grad, getattr(r, "rc_" + name), getattr(r, "ry_" + name), mine, theirs

    def w_first(name):
        index, grad, rc, ry, mine, theirs = w_parts(name)
        return w_copy(grad.at[theirs], rc, index, 0, 0, (stream, mate, place))

    def w_second(name):
        index, grad, rc, ry, mine, theirs = w_parts(name)
        return w_copy(rc, ry, index, 1, 1, (stream, across_y, place))

    def w_third(name):
        index, grad, rc, ry, mine, theirs = w_parts(name)
        out = getattr(r, name)
        return w_copy(grad.at[mine], out.at[mine], index, 2, 2, (stream, mate, place))

    def w_local(name):
        index, grad, rc, ry, mine, theirs = w_parts(name)
        return pltpu.make_async_copy(grad.at[mine], getattr(r, name).at[mine], r.w_send.at[index, 3])

    def w_other_side(name):
        index, grad, rc, ry, mine, theirs = w_parts(name)
        out = getattr(r, name)
        return w_copy(grad.at[mine], out.at[mine], index, 4, 3, (1 - stream, query, place))

    def w_forward(name):
        index, grad, rc, ry, mine, theirs = w_parts(name)
        out = getattr(r, name)
        return w_copy(out.at[mine], out.at[mine], index, 5, 4, (stream, mate, place))

    def w_start(name):
        w_first(name).start()

    def w_combine(name):
        index, grad, rc, ry, mine, theirs = w_parts(name)
        w_first(name).wait_recv()
        step = 48 if rc.shape[0] % 64 else 64

        @pl.loop(0, rc.shape[0] // step)
        def _(i):
            rows = pl.ds(pl.multiple_of(i * step, step), step)
            own = pl.ds(pl.multiple_of(core * rc.shape[0] + i * step, step), step)
            rc[rows] += grad[own]

        w_second(name).start()

    def w_store(name):
        index, grad, rc, ry, mine, theirs = w_parts(name)
        w_second(name).wait_recv()
        step = 48 if rc.shape[0] % 64 else 64

        @pl.loop(0, rc.shape[0] // step)
        def _(i):
            rows = pl.ds(pl.multiple_of(i * step, step), step)
            own = pl.ds(pl.multiple_of(core * rc.shape[0] + i * step, step), step)
            grad[own] = ry[rows] + rc[rows]

        w_third(name).start()
        w_local(name).start()
        if name in (CQ, CKV, CPROJ):
            w_other_side(name).start()

    def w_end(name):
        w_first(name).wait_send()
        w_second(name).wait_send()
        w_third(name).wait()
        w_local(name).wait()
        if name in (CQ, CKV, CPROJ):
            w_other_side(name).wait_send()

    def softmax(exp_ref, head, chunk, first_key, keys, banded):
        sums = []
        for tile in range(side.size // LANES):
            cols = pl.ds(tile * LANES, LANES)
            rows = pl.ds(chunk * side.size + tile * LANES, LANES)
            end = chunk * side.size + (tile + 1) * LANES if banded else keys
            if banded:
                near = min(end, 2 * LANES)
                r.tall[pl.ds(end - near, near), cols] += r.band[head, pl.ds(2 * LANES - near, near)]
            top = jnp.max(r.tall[pl.ds(0, end), cols], axis=0, keepdims=True)
            parts = [jnp.zeros((1, LANES), F32), jnp.zeros((1, LANES), F32)]
            for key in range(0, end, LANES):
                grown = jnp.exp(r.tall[pl.ds(key, LANES), cols] - top)
                exp_ref[head, pl.ds(first_key + key, LANES), rows] = grown.astype(BF16)
                parts[key // HALF] += jnp.sum(grown, axis=0, keepdims=True)
            for key in range(end, keys, LANES):
                exp_ref[head, pl.ds(first_key + key, LANES), rows] = jnp.zeros((LANES, LANES), BF16)
            sums.append(parts)
        return [jnp.concatenate([parts[p] for parts in sums], axis=1) for p in range(2)]

    def head_rows(head):
        return pl.ds(pl.multiple_of(head * HEAD_DIM, HEAD_DIM), HEAD_DIM)

    def attend(qa, ka, va, exp_ref, out_ref, inv_ref, chunk, first_key, keys, banded, mass):
        rows = chunk_rows(chunk)
        span = pl.ds(first_key, keys)
        cols = pl.ds(0, side.size)
        live = lax.broadcasted_iota(jnp.int32, (1, side.size), 1) + chunk * side.size < r.target_lengths[0]

        @pl.loop(0, heads)
        def _(head):
            r.tall[pl.ds(0, keys), cols] = dot(ka[head, span], qa[head, rows], NT)
            parts = softmax(exp_ref, head, chunk, first_key, keys, banded)
            inverse = 1.0 / (parts[0] + parts[1])
            inv_ref[head, pl.ds(0, 1), rows] = inverse
            if mass:
                for p in range(NPASS):
                    r.mass_rows[pl.ds(p, 1), cols] += jnp.where(live, parts[p] * inverse, 0.0)
            mixed = dot(va[head, span, pl.ds(0, HEAD_DIM)], exp_ref[head, span, rows], TN)
            out_ref[head_rows(head), rows] = (mixed * inverse).astype(BF16)

    def attend_back(qa, ka, va, exp_ref, out_ref, chunk, first_key, keys, fresh, banded):
        rows = chunk_rows(chunk)
        span = pl.ds(first_key, keys)
        cols = pl.ds(0, side.size)
        low = pl.ds(0, HEAD_DIM)

        @pl.loop(0, heads)
        def _(head):
            lanes = head_rows(head)
            grad_out = r.dot_in[lanes, cols]
            spread = jnp.sum(
                grad_out.astype(F32) * out_ref[lanes, rows].astype(F32), axis=0, keepdims=True)
            weight = exp_ref[head, span, rows]
            score_grad = (
                weight.astype(F32) * (dot(va[head, span, low], grad_out, NN) - spread)).astype(BF16)
            if banded:
                r.tall_low[pl.ds(0, keys), cols] = score_grad
                for tile in range(side.size // LANES):
                    end = chunk * side.size + (tile + 1) * LANES
                    near = min(end, 2 * LANES)
                    r.band_grad[head, pl.ds(2 * LANES - near, near)] += (
                        r.tall_low[pl.ds(end - near, near), pl.ds(tile * LANES, LANES)].astype(F32))
            query_grad = dot(score_grad, ka[head, span], TN)
            key_grad = dot(score_grad, qa[head, rows], NN)
            value_grad = dot(weight, grad_out, NT)
            qa[head, rows, low] = (query_grad[:, :HEAD_DIM] * HEAD_DIM ** (-0.5)).astype(BF16)
            if fresh:
                r.dk[head, span] = key_grad
                r.dv[head, span, low] = value_grad
            else:
                r.dk[head, span] += key_grad
                r.dv[head, span, low] += value_grad

    def grad_of_mixed(weight, grad_ref, inv_ref, chunk):
        grads = dot(weight[...], grad_ref[chunk_rows(chunk)], NT)
        for head in range(heads):
            lanes = pl.ds(head * HEAD_DIM, HEAD_DIM)
            r.dot_in[lanes, pl.ds(0, side.size)] = (
                grads[head * HEAD_DIM:(head + 1) * HEAD_DIM] * inv_ref[head, pl.ds(0, 1), chunk_rows(chunk)]
            ).astype(BF16)

    def fill_tails(qa, ka, valid):
        shape = (SEQ, HEAD_DIM)
        lane = lax.broadcasted_iota(jnp.int32, shape, 1)
        key = lax.broadcasted_iota(jnp.int32, shape, 0)
        ones = jnp.where(lane == 0, 1.0, 0.0).astype(BF16)
        fence = jnp.where((lane == 0) & jnp.logical_not(valid(key)), NEG, 0.0).astype(BF16)
        for head in range(heads):
            qa[head, :, pl.ds(HEAD_DIM, HEAD_DIM)] = ones
            ka[head, :, pl.ds(HEAD_DIM, HEAD_DIM)] = fence

    def in_passage(key):
        low = (key < HALF) & (key < r.passage_lengths[0, 0])
        return low | ((key >= HALF) & (key - HALF < r.passage_lengths[0, 1]))

    def in_target(key):
        return key < r.target_lengths[0]

    def split_packed(rows):
        for head in range(heads):
            base = 3 * HEAD_DIM * head
            low = pl.ds(0, HEAD_DIM)
            r.qa[head, rows, low] = (
                r.pkb[rows, pl.ds(base, HEAD_DIM)].astype(F32) * HEAD_DIM ** (-0.5)).astype(BF16)
            r.ka[head, rows, low] = r.pkb[rows, pl.ds(base + HEAD_DIM, HEAD_DIM)]
            r.va[head, rows, low] = r.pkb[rows, pl.ds(base + 2 * HEAD_DIM, HEAD_DIM)]

    def project_out(line, room, chunk, out_ref, weight, before=None):
        for tile in range(side.size // LANES):
            rows = pl.ds(chunk * side.size + tile * LANES, LANES)
            r.part[room, rows] = dot(out_ref[:, rows], weight[...], TN).astype(BF16)
        hand_on(line, room, chunk, before)

    def param(row):
        return r.params[pl.ds(row, 1)]

    def add_to(slot, values):
        r.acc[slot] += fold(values)

    def gelu_parts(values):
        cubic = 0.7978845608028654 * (values + 0.044715 * values * values * values)
        bend = jnp.tanh(cubic)
        slope = 0.7978845608028654 * (1.0 + 3.0 * 0.044715 * values * values)
        return 0.5 * values * (1.0 + bend), 0.5 * (1.0 + bend) + 0.5 * values * (1.0 - bend * bend) * slope

    def pack_grads(chunk):
        rows = chunk_rows(chunk)
        for head in range(heads):
            base = 3 * HEAD_DIM * head
            low = pl.ds(0, HEAD_DIM)
            r.pkb[rows, pl.ds(base, HEAD_DIM)] = r.qa[head, rows, low]
            r.pkb[rows, pl.ds(base + HEAD_DIM, HEAD_DIM)] = r.dk[head, rows, low].astype(BF16)
            r.pkb[rows, pl.ds(base + 2 * HEAD_DIM, HEAD_DIM)] = r.dv[head, rows, low].astype(BF16)

    def input_part(line, room, chunk, before):
        rows = chunk_rows(chunk)
        r.part[room, rows] = dot(r.pkb[rows], r.w_qkv[...], NN).astype(BF16)
        hand_on(line, room, chunk, before)

    def weight_grad(target, left, right):
        @pl.loop(0, left.shape[1] // THIRD)
        def _(step):
            rows = pl.ds(pl.multiple_of(step * THIRD, THIRD), THIRD)
            target[rows] = dot(left[:, rows], right[...], TN).astype(BF16)

    def third_loop(body):
        @pl.loop(0, SEQ // THIRD)
        def _(step):
            body(pl.ds(pl.multiple_of(step * THIRD, THIRD), THIRD))

    def clear():
        r.acc[...] = jnp.zeros_like(r.acc)
        r.small[...] = jnp.zeros_like(r.small)

    def store_input_grad(chunk):
        rows = chunk_rows(chunk)
        return pltpu.make_async_copy(r.h1f.at[rows], r.gin.at[rows], r.out_sem.at[0, chunk])

    def store_result(chunk):
        rows = chunk_rows(chunk)
        return pltpu.make_async_copy(r.ybuf.at[rows], r.y.at[rows], r.out_sem.at[1, chunk])

    def small_copies():
        copies = []
        for side_step in range(2):
            for steps in range(4):
                if side_step == 0 and steps == 0:
                    continue
                device = (lax.rem(stream + side_step, 2), other(steps), place)
                copies.append(pltpu.make_async_remote_copy(
                    r.small, r.small_got.at[stream * 4 + member], r.small_send.at[len(copies)],
                    r.small_recv.at[stream * 4 + member], device_id=device, device_id_type=MESH))
        return copies

    def start_small():
        for copy in small_copies():
            copy.start()
        r.small_got[stream * 4 + member] = r.small[...]

    def end_small():
        for side_step in range(2):
            for steps in range(4):
                if side_step == 0 and steps == 0:
                    continue
                source = lax.rem(stream + side_step, 2) * 4 + lax.rem(member + steps, 4)
                pltpu.make_async_remote_copy(
                    r.small, r.small_got.at[source], r.small_send.at[0], r.small_recv.at[source],
                    device_id=(stream, mate, place), device_id_type=MESH).wait_recv()
        for copy in small_copies():
            copy.wait_send()
        total = r.small_got[0]
        for index in range(1, 8):
            total = total + r.small_got[index]
        loss = r.small_got[member, pl.ds(12, 1)]
        r.small_out[...] = total
        r.small_out[pl.ds(12, 1)] = loss

    def reader():
        side.size = THIRD
        order = (2, 1, 0)
        inputs.hid.start()
        inputs.qkv.start()
        r.params[pl.ds(8, 3)] = r.scale_gain[...].astype(F32)
        starts = bucket_starts(SEQ, buckets)
        shape = (2 * LANES, LANES)
        apart = (
            lax.broadcasted_iota(jnp.int32, shape, 1) + LANES - lax.broadcasted_iota(jnp.int32, shape, 0))
        shifts = r.position_bias[...].astype(F32)
        shifts = shifts - shifts[:, buckets - 1:]
        for head in range(heads):
            band = jnp.broadcast_to(shifts[head:head + 1, 0:1], shape)
            for bucket in range(1, buckets):
                band = jnp.where(apart >= starts[bucket], shifts[head:head + 1, bucket:bucket + 1], band)
            r.band[head] = jnp.where(apart >= 0, band, NEG)
        fill_tails(r.qa, r.ka, in_target)

        inputs.hid.wait()
        for copy in (inputs.proj, inputs.enc, inputs.ckv, inputs.cq, inputs.cproj):
            copy.start()
        for copy in (inputs.up, inputs.down, inputs.cot):
            copy.start()
        gain = param(8)

        def normalize(rows):
            values = r.hid[rows].astype(F32)
            r.buf_a[rows] = (values * lax.rsqrt(mean(values * values) + EPS) * gain).astype(BF16)
        third_loop(normalize)
        inputs.qkv.wait()

        def project(rows):
            r.pkb[rows] = dot(r.buf_a[rows], r.w_qkv[...], NT).astype(BF16)
            split_packed(rows)
        third_loop(project)
        inputs.proj.wait()
        for chunk in order:
            attend(
                r.qa, r.ka, r.va, r.e1, r.o1, r.linv1, chunk, 0, (chunk + 1) * THIRD, True, False)
            if chunk == order[-1]:
                pump()
            if chunk == order[0]:
                meet()
            project_out(0, 0, chunk, r.o1, r.w_proj)

        clear()
        r.mass_rows[...] = jnp.zeros_like(r.mass_rows)
        r.band_grad[...] = jnp.zeros_like(r.band_grad)
        fill_tails(r.cqa, r.cka, in_passage)

        inputs.enc.wait()
        inputs.ckv.wait()
        pump()

        def encode(rows):
            r.encb[rows] = r.h2f[rows].astype(BF16)
            r.ckb[rows] = dot(r.encb[rows], r.w_ckv[...], NN).astype(BF16)
            for head in range(heads):
                low = pl.ds(0, HEAD_DIM)
                r.cka[head, rows, low] = r.ckb[rows, pl.ds(2 * HEAD_DIM * head, HEAD_DIM)]
                r.cva[head, rows, low] = r.ckb[rows, pl.ds(2 * HEAD_DIM * head + HEAD_DIM, HEAD_DIM)]
        third_loop(encode)
        pump()
        inputs.down.wait()
        inputs.cot.wait()

        def act_grad(rows):
            r.buf_c[rows] = dot(r.cot[rows], r.w_down[...], NT).astype(BF16)
        third_loop(act_grad)
        inputs.cq.wait()
        inputs.cproj.wait()
        inputs.up.wait()

        gain = param(9)
        for chunk in order:
            rows = chunk_rows(chunk)
            collect(0, 0, chunk)

            def first_sum(rows, _):
                values = r.hid[rows].astype(F32) + r.total[0, rows].astype(F32)
                r.h1f[rows] = values
                r.buf_b[rows] = (values * lax.rsqrt(mean(values * values) + EPS) * gain).astype(BF16)
            row_loop(chunk, first_sum)
            r.cqb[rows] = dot(r.buf_b[rows], r.w_cq[...], NT).astype(BF16)
            for head in range(heads):
                r.cqa[head, rows, pl.ds(0, HEAD_DIM)] = (
                    r.cqb[rows, pl.ds(head * HEAD_DIM, HEAD_DIM)].astype(F32) * HEAD_DIM ** (-0.5)
                ).astype(BF16)
            pump()
            attend(r.cqa, r.cka, r.cva, r.e2, r.o2, r.linv2, chunk, 0, SEQ, False, True)
            pump()
            project_out(1, 1, chunk, r.o2, r.w_cproj, (0, 0))

        lane = lax.broadcasted_iota(jnp.int32, (8, LANES), 1)
        masses = [jnp.sum(r.mass_rows[pl.ds(p, 1)], axis=1, keepdims=True) for p in range(NPASS)]
        r.mass[...] = jnp.where(lane == 0, masses[0], jnp.where(lane == 1, masses[1], 0.0))

        def mass_copy(steps):
            return pltpu.make_async_remote_copy(
                r.mass, r.mass_got.at[place], r.mass_send.at[steps], r.mass_recv.at[place],
                device_id=(1 - stream, query, lax.rem(place + steps, 4)), device_id_type=MESH)

        for steps in range(4):
            mass_copy(steps).start()

        gain = param(10)
        for chunk in order:
            rows = chunk_rows(chunk)
            collect(1, 1, chunk)

            def second_sum(rows, _):
                values = r.h1f[rows] + r.total[1, rows].astype(F32)
                r.h2f[rows] = values
                r.ybuf[rows] = values.astype(BF16)
                r.buf_u[rows] = (values * lax.rsqrt(mean(values * values) + EPS) * gain).astype(BF16)
            row_loop(chunk, second_sum)
            r.wide[pl.ds(0, side.size)] = dot(r.buf_u[rows], r.w_up[...], NN)
            pump()

            def bend(rows, local):
                value, slope = gelu_parts(r.wide[local])
                r.act[rows] = value.astype(BF16)
                r.dpre[rows] = (r.buf_c[rows].astype(F32) * slope).astype(BF16)
            row_loop(chunk, bend)
            pump()
            r.part[0, rows] = dot(r.dpre[rows], r.w_up[...], NT).astype(BF16)
            hand_on(2, 0, chunk, (1, 1))
            r.part[2, rows] = dot(r.act[rows], r.w_down[...], NN).astype(BF16)
            if chunk != order[-1]:
                hand_over(chunk).start()

        weight_grad(r.d_up, r.buf_u, r.dpre)
        w_start(UP)
        pump()
        weight_grad(r.d_down, r.act, r.cot)
        w_start(DOWN)
        pump()

        for chunk in order:
            rows = chunk_rows(chunk)
            collect(2, 0, chunk)
            if chunk == order[0]:
                w_combine(UP)
                w_combine(DOWN)

            def second_grad(rows, _):
                values = r.h2f[rows]
                grads = r.total[0, rows].astype(F32)
                root = lax.rsqrt(mean(values * values) + EPS)
                add_to(2, grads * values * root)
                scaled = grads * gain
                back = root * scaled - values * (root * root * root) * mean(scaled * values)
                result = r.cot[rows].astype(F32) + back
                r.h2f[rows] = result
                r.buf_c[rows] = result.astype(BF16)
            row_loop(chunk, second_grad)
            grad_of_mixed(r.w_cproj, r.buf_c, r.linv2, chunk)
            pump()
            attend_back(r.cqa, r.cka, r.cva, r.e2, r.o2, chunk, 0, SEQ, chunk == order[0], False)
            pump()
            for head in range(heads):
                r.cqb[rows, pl.ds(head * HEAD_DIM, HEAD_DIM)] = r.cqa[head, rows, pl.ds(0, HEAD_DIM)]
            r.part[1, rows] = dot(r.cqb[rows], r.w_cq[...], NN).astype(BF16)
            hand_on(3, 1, chunk, (2, 0))

        pump()
        for chunk in order:
            rows = chunk_rows(chunk)
            for head in range(heads):
                low = pl.ds(0, HEAD_DIM)
                r.ckb[rows, pl.ds(2 * HEAD_DIM * head, HEAD_DIM)] = r.dk[head, rows, low].astype(BF16)
                r.ckb[rows, pl.ds(2 * HEAD_DIM * head + HEAD_DIM, HEAD_DIM)] = (
                    r.dv[head, rows, low].astype(BF16))
        r.d_cproj[...] = dot(r.o2[...], r.buf_c[...], NN).astype(BF16)
        w_start(CPROJ)
        r.d_cq[...] = dot(r.cqb[...], r.buf_b[...], TN).astype(BF16)
        w_start(CQ)
        pump()
        weight_grad(r.d_ckv, r.encb, r.ckb)
        w_start(CKV)

        gain = param(9)
        for chunk in order:
            rows = chunk_rows(chunk)
            collect(3, 1, chunk)
            if chunk == order[0]:
                for name in (CPROJ, CQ, CKV):
                    w_combine(name)

            def first_grad(rows, _):
                values = r.h1f[rows]
                grads = r.total[1, rows].astype(F32)
                root = lax.rsqrt(mean(values * values) + EPS)
                add_to(1, grads * values * root)
                scaled = grads * gain
                back = root * scaled - values * (root * root * root) * mean(scaled * values)
                result = r.h2f[rows] + back
                r.h1f[rows] = result
                r.ag[rows] = result.astype(BF16)
            row_loop(chunk, first_grad)
            grad_of_mixed(r.w_proj, r.ag, r.linv1, chunk)
            pump()
            attend_back(
                r.qa, r.ka, r.va, r.e1, r.o1, chunk, 0, (chunk + 1) * THIRD, chunk == order[0], True)
            pump()
            pack_grads(chunk)
            input_part(4, 0, chunk, (3, 1))
            if chunk == order[1]:
                w_store(UP)
                w_store(DOWN)
        produce(5, 2, third_pieces(0))
        r.d_qkv[...] = dot(r.pkb[...], r.buf_a[...], TN).astype(BF16)
        w_start(QKV)
        r.d_proj[...] = dot(r.o1[...], r.ag[...], NN).astype(BF16)
        w_start(PROJ)
        for name in (CPROJ, CQ, CKV):
            w_store(name)
        w_combine(QKV)
        w_combine(PROJ)
        pump()

        lane = lax.broadcasted_iota(jnp.int32, (1, LANES), 1)
        table = jnp.zeros((1, LANES), F32)
        for head in range(heads):
            grads = r.band_grad[head]
            rest = jnp.sum(
                jnp.sum(r.dk[head], axis=0, keepdims=True)[:, HEAD_DIM:HEAD_DIM + 1], axis=1, keepdims=True)
            for bucket in range(buckets - 1):
                inside = (apart >= starts[bucket]) & (apart < starts[bucket + 1])
                value = jnp.sum(
                    jnp.sum(jnp.where(inside, grads, 0.0), axis=0, keepdims=True), axis=1, keepdims=True)
                rest = rest - value
                table = jnp.where(lane == head * buckets + bucket, value, table)
            table = jnp.where(lane == head * buckets + buckets - 1, rest, table)
        r.small[pl.ds(11, 1), pl.ds(0, LANES)] = table

        def last_sum(chunk):
            def add(rows, _):
                r.ybuf[rows] = (r.ybuf[rows].astype(F32) + r.total[2, rows].astype(F32)).astype(BF16)
            row_loop(chunk, add)
            store_result(chunk).start()

        gain = param(8)
        for chunk in order:
            if chunk != order[-1]:
                hand_back(chunk).wait_recv()
                last_sum(chunk)
            collect(4, 0, chunk)

            def input_grad(rows, _):
                values = r.hid[rows].astype(F32)
                grads = r.total[0, rows].astype(F32)
                root = lax.rsqrt(mean(values * values) + EPS)
                add_to(0, grads * values * root)
                scaled = grads * gain
                back = root * scaled - values * (root * root * root) * mean(scaled * values)
                r.h1f[rows] = r.h1f[rows] + back
            row_loop(chunk, input_grad)
            store_input_grad(chunk).start()

        for slot in range(3):
            r.small[pl.ds(8 + slot, 1)] = jnp.sum(r.acc[slot], axis=0, keepdims=True)
        start_small()
        w_store(QKV)
        w_store(PROJ)
        collect(5, 2, 0)
        last_sum(0)
        end_small()
        settle(5, 2, third_pieces(0))
        for chunk in order:
            settle(4, 0, chunk_pieces(chunk))
            if chunk != order[-1]:
                hand_over(chunk).wait_send()
            store_input_grad(chunk).wait()
            store_result(chunk).wait()
        for name in WEIGHTS:
            w_end(name)
        for steps in range(4):
            mass_copy(steps).wait_send()

    def retriever():
        side.size = HALF
        order = (1, 0)
        inputs.hid.start()
        inputs.qkv.start()
        r.params[pl.ds(0, 2)] = r.layer_gain[...].astype(F32)
        r.params[pl.ds(2, 2)] = r.layer_shift[...].astype(F32)
        r.params[pl.ds(4, 2)] = r.output_bias[...].astype(F32)
        r.params[pl.ds(6, 1)] = r.biases[:, pl.ds(2 * heads * HEAD_DIM, WIDTH)].astype(F32)
        r.colsum[...] = jnp.zeros_like(r.colsum)
        r.params[pl.ds(11, 1), pl.ds(0, 2 * heads * HEAD_DIM)] = (
            r.biases[:, pl.ds(0, 2 * heads * HEAD_DIM)].astype(F32))
        for head in range(heads):
            base = 3 * HEAD_DIM * head
            for k in range(2):
                r.colsum[pl.ds(0, 1), pl.ds(base + 2 * k * HEAD_DIM, HEAD_DIM)] = (
                    r.params[pl.ds(11, 1), pl.ds((2 * head + k) * HEAD_DIM, HEAD_DIM)])
        shift = r.colsum[pl.ds(0, 1)]
        fill_tails(r.qa, r.ka, in_passage)
        inputs.hid.wait()
        for copy in (inputs.proj, inputs.up, inputs.down, inputs.cot):
            copy.start()
        inputs.qkv.wait()
        inputs.proj.wait()
        for chunk in order:
            rows = chunk_rows(chunk)
            r.pkb[rows] = (dot(r.hid[rows], r.w_qkv[...], NT) + shift).astype(BF16)
            split_packed(rows)
            attend(r.qa, r.ka, r.va, r.e1, r.o1, r.linv1, chunk, chunk * HALF, HALF, False, False)
            if chunk == order[0]:
                meet()
            project_out(0, 0, chunk, r.o1, r.w_proj)
        r.colsum[...] = jnp.zeros_like(r.colsum)
        clear()

        inputs.up.wait()
        inputs.down.wait()
        inputs.cot.wait()
        gain1, gain2 = param(0), param(1)
        shift1, shift2 = param(2), param(3)
        out1, out2, unit = param(4), param(5), param(6)
        side.size = THIRD
        thirds = (2, 1, 0)
        for chunk in thirds:
            rows = chunk_rows(chunk)
            collect(0, 0, chunk)

            def first_norm(rows, _):
                values = r.hid[rows].astype(F32) + r.total[0, rows].astype(F32) + out1
                centered = values - mean(values)
                root = lax.rsqrt(mean(centered * centered) + EPS)
                r.h1f[rows] = values
                r.buf_u[rows] = (centered * root * gain1 + shift1).astype(BF16)
            row_loop(chunk, first_norm)
            r.wide[pl.ds(0, THIRD)] = dot(r.buf_u[rows], r.w_up[...], NN)
            pump()

            def bend(rows, local):
                value, slope = gelu_parts(r.wide[local] + unit)
                r.act[rows] = value.astype(BF16)
                r.buf_a[rows] = slope.astype(BF16)
            row_loop(chunk, bend)
            pump()
            r.part[1, rows] = dot(r.act[rows], r.w_down[...], NN).astype(BF16)
            hand_on(1, 1, chunk, (0, 0))

        def valid(rows):
            token = lax.broadcasted_iota(jnp.int32, (LANES, 1), 0) + rows.start
            low = (token < HALF) & (token < r.passage_lengths[0, 0])
            return low, (token >= HALF) & (token - HALF < r.passage_lengths[0, 1])

        for chunk in thirds:
            collect(1, 1, chunk)

            def second_norm(rows, _):
                values = r.h1f[rows]
                centered = values - mean(values)
                root = lax.rsqrt(mean(centered * centered) + EPS)
                values = centered * root * gain1 + shift1 + r.total[1, rows].astype(F32) + out2
                r.h2f[rows] = values
                centered = values - mean(values)
                root = lax.rsqrt(mean(centered * centered) + EPS)
                result = centered * root * gain2 + shift2
                r.ybuf[rows] = result.astype(BF16)
                for p, token in enumerate(valid(rows)):
                    add_to(8 + p, jnp.where(token, result, 0.0))
            row_loop(chunk, second_norm)
            store_result(chunk).start()
            if chunk == 1:
                hand_over(2).wait_recv()
                produce(5, 2, third_pieces(2))

        vector = r.query_vectors[...]
        scores = [
            jnp.sum(jnp.sum(r.acc[8 + p], axis=0, keepdims=True) * vector, axis=1, keepdims=True)
            / r.passage_lengths[0, p].astype(F32)
            for p in range(NPASS)
        ]

        def mass_wait(source):
            return pltpu.make_async_remote_copy(
                r.mass, r.mass_got.at[source], r.mass_send.at[0], r.mass_recv.at[source],
                device_id=(1 - stream, query, place), device_id_type=MESH)

        for source in range(4):
            mass_wait(source).wait_recv()
        masses = r.mass_got[0].astype(BF16).astype(F32)
        for source in range(1, 4):
            masses = masses + r.mass_got[source].astype(BF16).astype(F32)
        scale = HEADS * r.target_lengths[0].astype(F32)
        targets = [masses[0:1, p:p + 1] / scale for p in range(NPASS)]
        top = jnp.maximum(scores[0], scores[1])
        norm = top + jnp.log(jnp.exp(scores[0] - top) + jnp.exp(scores[1] - top))
        logs = [score - norm for score in scores]
        loss = targets[0] * (jnp.log(targets[0]) - logs[0]) + targets[1] * (jnp.log(targets[1]) - logs[1])
        r.small[pl.ds(12, 1)] = jnp.broadcast_to(loss, (1, WIDTH))
        pulls = [
            (jnp.exp(logs[p]) * (targets[0] + targets[1]) - targets[p])
            / r.passage_lengths[0, p].astype(F32) * vector
            for p in range(NPASS)
        ]

        for chunk in thirds:
            rows = chunk_rows(chunk)

            def final_grad(rows, _):
                low, high = valid(rows)
                upstream = r.cot[rows].astype(F32) + jnp.where(
                    low, pulls[0], jnp.where(high, pulls[1], 0.0))
                values = r.h2f[rows]
                centered = values - mean(values)
                root = lax.rsqrt(mean(centered * centered) + EPS)
                normed = centered * root
                scaled = upstream * gain2
                result = root * (scaled - mean(scaled) - normed * mean(scaled * normed))
                add_to(1, upstream * normed)
                add_to(3, upstream)
                r.h2f[rows] = result
                low = result.astype(BF16)
                r.buf_b[rows] = low
                add_to(5, low.astype(F32))
            row_loop(chunk, final_grad)
            if chunk == 2:
                pump()
            r.wide[pl.ds(0, THIRD)] = dot(r.buf_b[rows], r.w_down[...], NT)
            if chunk == 2:
                pump()

            def bend_back(rows, local):
                low = (r.wide[local] * r.buf_a[rows].astype(F32)).astype(BF16)
                r.dpre[rows] = low
                add_to(6, low.astype(F32))
            row_loop(chunk, bend_back)
            pump()
            r.part[0, rows] = dot(r.dpre[rows], r.w_up[...], NT).astype(BF16)
            hand_on(2, 0, chunk, (1, 1))
        hand_over(1).wait_recv()
        produce(5, 2, third_pieces(1))

        weight_grad(r.d_up, r.buf_u, r.dpre)
        w_start(UP)
        pump()
        weight_grad(r.d_down, r.act, r.buf_b)
        w_start(DOWN)
        pump()
        finish(5, 2, third_pieces(2))
        hand_back(2).start()

        side.size = HALF
        for chunk in order:
            rows = chunk_rows(chunk)
            collect(2, 0, chunk)
            if chunk == order[0]:
                w_combine(UP)
                w_combine(DOWN)

            def middle_grad(rows, _):
                upstream = r.h2f[rows] + r.total[0, rows].astype(F32)
                values = r.h1f[rows]
                centered = values - mean(values)
                root = lax.rsqrt(mean(centered * centered) + EPS)
                normed = centered * root
                scaled = upstream * gain1
                result = root * (scaled - mean(scaled) - normed * mean(scaled * normed))
                add_to(0, upstream * normed)
                add_to(2, upstream)
                r.h1f[rows] = result
                low = result.astype(BF16)
                r.ag[rows] = low
                add_to(4, low.astype(F32))
            row_loop(chunk, middle_grad)
            grad_of_mixed(r.w_proj, r.ag, r.linv1, chunk)
            pump()
            attend_back(r.qa, r.ka, r.va, r.e1, r.o1, chunk, chunk * HALF, HALF, True, False)
            pump()
            pack_grads(chunk)
            input_part(4, 1, chunk, (2, 0))
            r.colsum[...] += fold(r.pkb[rows].astype(F32))
            if chunk == order[0]:
                finish(5, 2, third_pieces(1))
                hand_back(1).start()
        r.d_qkv[...] = dot(r.pkb[...], r.hid[...], TN).astype(BF16)
        w_start(QKV)
        r.d_proj[...] = dot(r.o1[...], r.ag[...], NN).astype(BF16)
        w_start(PROJ)
        pump()

        w_combine(QKV)
        w_combine(PROJ)
        for chunk in order:
            rows = chunk_rows(chunk)
            collect(4, 1, chunk)
            if chunk == order[0]:
                w_store(UP)
                w_store(DOWN)

            def input_grad(rows, _):
                r.h1f[rows] = r.h1f[rows] + r.total[1, rows].astype(F32)
            row_loop(chunk, input_grad)
            store_input_grad(chunk).start()

        columns = jnp.sum(r.colsum[...], axis=0, keepdims=True)
        r.colsum[pl.ds(0, 1)] = columns
        for head in range(heads):
            base = 3 * HEAD_DIM * head
            for k in range(2):
                r.small[pl.ds(0, 1), pl.ds((2 * head + k) * HEAD_DIM, HEAD_DIM)] = (
                    r.colsum[pl.ds(0, 1), pl.ds(base + 2 * k * HEAD_DIM, HEAD_DIM)])
        r.small[pl.ds(1, 1)] = jnp.sum(r.acc[6], axis=0, keepdims=True)
        for slot in range(6):
            r.small[pl.ds(2 + slot, 1)] = jnp.sum(r.acc[slot], axis=0, keepdims=True)
        for name in (CQ, CKV, CPROJ):
            w_other_side(name).wait_recv()
            w_forward(name).start()
        start_small()
        w_store(QKV)
        w_store(PROJ)
        end_small()
        for chunk in order:
            settle(4, 1, chunk_pieces(chunk))
            store_input_grad(chunk).wait()
        side.size = THIRD
        for chunk in thirds:
            if chunk > 0:
                settle(5, 2, third_pieces(chunk))
                hand_back(chunk).wait_send()
            store_result(chunk).wait()
        for name in (UP, DOWN, QKV, PROJ):
            w_end(name)
        for name in (CQ, CKV, CPROJ):
            w_forward(name).wait()

    @pl.when(is_reader)
    def _():
        reader()

    for items in (made, added, summed):
        items.clear()

    @pl.when(jnp.logical_not(is_reader))
    def _():
        retriever()


def finish_kernel(heads, buckets, *refs):
    count = len(WEIGHTS)
    small, result, input_grad, *grads = refs[: count + 3]
    outs = refs[count + 3 : 2 * count + 5]
    small_outs = refs[2 * count + 5 : 2 * count + 13]
    scratch = refs[2 * count + 13 :]
    near, wide, (in_sem, out_sem) = scratch[: count + 2], scratch[count + 2 : -2], scratch[-2:]
    sources = [result, input_grad, *grads]
    loads = [
        pltpu.make_async_copy(source, target, in_sem.at[index])
        for index, (source, target) in enumerate(zip(sources, near))
    ]
    held = [*near[:2], *wide]
    stores = [
        pltpu.make_async_copy(source, target, out_sem.at[index])
        for index, (source, target) in enumerate(zip(held, outs))
    ]
    for load in loads:
        load.start()
    inner = heads * HEAD_DIM
    values, units, gains, shifts, biases, scales, table, loss = small_outs
    values[...] = small[0:1, : 2 * inner]
    units[...] = small[1:2]
    gains[...] = small[2:4]
    shifts[...] = small[4:6]
    biases[...] = small[6:8]
    scales[...] = small[8:11]
    for head in range(heads):
        table[head : head + 1] = small[11:12, head * buckets : (head + 1) * buckets]
    loss[...] = small[12:13, 0:1]
    for index in range(2, count + 2):
        loads[index].wait()
        source, target = near[index], wide[index - 2]
        step = 48 if source.shape[0] % 64 else 64

        @pl.loop(0, source.shape[0] // step)
        def _(i):
            part = pl.ds(pl.multiple_of(i * step, step), step)
            target[part] = source[part].astype(F32)

        stores[index].start()
        if index < 4:
            loads[index - 2].wait()
            stores[index - 2].start()
    for store in stores:
        store.wait()


def finish_results(heads, buckets, small, result, input_grad, grads):
    inner = heads * HEAD_DIM
    anywhere = pl.BlockSpec(memory_space=pl.ANY)
    vector = pl.BlockSpec(memory_space=pltpu.VMEM)
    low = [jax.ShapeDtypeStruct(grad.shape, F32) for grad in grads]
    rows = ((1, 2 * inner), (1, WIDTH), (2, WIDTH), (2, WIDTH), (2, WIDTH), (3, WIDTH), (heads, buckets), (1, 1))
    out_shape = [
        jax.ShapeDtypeStruct(result.shape, BF16), jax.ShapeDtypeStruct(input_grad.shape, F32), *low,
        *(jax.ShapeDtypeStruct(shape, F32) for shape in rows)]
    count = len(grads) + 2
    sources = [result, input_grad, *grads]
    return pl.pallas_call(
        partial(finish_kernel, heads, buckets),
        out_shape=out_shape,
        in_specs=[vector] + [anywhere] * count,
        out_specs=[anywhere] * count + [vector] * len(rows),
        scratch_shapes=[pltpu.VMEM(x.shape, x.dtype) for x in sources]
        + [pltpu.VMEM(x.shape, F32) for x in grads]
        + [pltpu.SemaphoreType.DMA((count,)), pltpu.SemaphoreType.DMA((count,))],
        compiler_params=pltpu.CompilerParams(vmem_limit_bytes=63 * 2**20),
    )(small, *sources)


def local(
    batch,
    hidden,
    cotangent,
    qkv_weight,
    proj_weight,
    up_weight,
    down_weight,
    query_value_bias,
    unit_bias,
    layer_gain,
    layer_shift,
    output_bias,
    scale_gain,
    position_bias,
    cross_query,
    cross_key_value,
    cross_proj,
    encodings,
    query_vectors,
    passage_lengths,
    target_lengths,
):
    heads = proj_weight.shape[1] // HEAD_DIM
    buckets = position_bias.shape[1]
    inner = heads * HEAD_DIM
    far = dict(
        hidden=hidden, cotangent=cotangent, qkv_weight=qkv_weight[0].T, proj_weight=proj_weight,
        up_weight=up_weight, down_weight=down_weight, cross_query=cross_query.T,
        cross_key_value=cross_key_value, cross_proj=cross_proj, encodings=encodings)
    near = dict(
        biases=jnp.concatenate([query_value_bias, unit_bias]).reshape(1, -1),
        layer_gain=layer_gain, layer_shift=layer_shift, output_bias=output_bias,
        scale_gain=scale_gain, query_vectors=query_vectors, position_bias=position_bias)
    scalars = dict(
        passage_lengths=passage_lengths, target_lengths=target_lengths)
    anywhere = pl.BlockSpec(memory_space=pl.ANY)
    vector = pl.BlockSpec(memory_space=pltpu.VMEM)
    scalar = pl.BlockSpec(memory_space=pltpu.SMEM)
    out_shapes = dict(
        small_out=jax.ShapeDtypeStruct((16, WIDTH), F32),
        y=jax.ShapeDtypeStruct((SEQ, WIDTH), BF16),
        gin=jax.ShapeDtypeStruct((SEQ, WIDTH), F32))
    for name, shape in weight_shapes(heads).items():
        out_shapes[name] = jax.ShapeDtypeStruct(shape, BF16)
    shapes = scratch_shapes(heads)
    names = [*far, *near, *scalars, *out_shapes, *shapes]
    small, result, input_grad, *grads = pl.pallas_call(
        partial(layer_kernel, heads, buckets, names),
        out_shape=list(out_shapes.values()),
        in_specs=[anywhere] * len(far) + [vector] * len(near) + [scalar] * len(scalars),
        out_specs=[vector] + [anywhere] * (len(out_shapes) - 1),
        scratch_shapes=list(shapes.values()),
        compiler_params=pltpu.CompilerParams(
            collective_id=0, has_side_effects=True, vmem_limit_bytes=63 * 2**20),
    )(*far.values(), *near.values(), *scalars.values())
    if batch > 4:
        groups = [[first + step for step in range(0, batch, 4)] for first in range(4)]
        grads = [grad.astype(F32) for grad in grads]
        grads, rows = lax.psum((grads, small[:12]), BATCH, axis_index_groups=groups)
        small_rows = (
            rows[0, : 2 * inner], rows[1], rows[2:4], rows[4:6], rows[6:8], rows[8:11],
            rows[11, : heads * buckets].reshape(heads, buckets), small[12, :1])
    else:
        result, input_grad, *rest = finish_results(heads, buckets, small, result, input_grad, grads)
        grads, small_rows = rest[: len(WEIGHTS)], rest[len(WEIGHTS) :]
    up, down, qkv, proj, cq, ckv, cproj = grads
    values, units, gains, shifts, biases, scales, table, loss = small_rows
    return (
        result[None],
        input_grad[None],
        qkv.T[None],
        proj[None],
        up[None],
        down[None],
        values.reshape(-1),
        units.reshape(-1),
        gains,
        shifts,
        biases,
        scales,
        table,
        cq.T,
        ckv,
        cproj,
        loss.reshape(-1),
    )


def solution(mesh):
    rows = P(STREAM, BATCH, None)
    columns_split = P(STREAM, None, TENSOR)
    rows_split = P(STREAM, TENSOR, None)
    weights = (columns_split, rows_split, columns_split, rows_split)
    cross = (P(None, TENSOR), P(None, TENSOR), P(TENSOR, None))
    vectors = (P(TENSOR), P(TENSOR), P(), P(), P(), P(), P(TENSOR, None))
    in_specs = (rows, rows, *weights, *vectors, *cross)
    in_specs = (*in_specs, P(BATCH, None, None), P(BATCH, None), P(BATCH, None), P(BATCH))
    out_specs = (rows, rows, *weights, *vectors, *cross, P(BATCH))
    return jax.shard_map(
        partial(local, mesh.shape[BATCH]), mesh=mesh, in_specs=in_specs, out_specs=out_specs,
        check_vma=False)
```

```python
from functools import partial

import jax
import jax.numpy as jnp
import numpy as np
from jax import lax
from jax.experimental import pallas as pl
from jax.experimental.pallas import tpu as pltpu
from jax.sharding import PartitionSpec as P

HEADS = 12
HEAD_DIM = 64
PLEN = 384
NPASS = 2
SEQ = 768
WIDTH = 768
HALF = 384
THIRD = 256
PIECE = 64
PIECES = SEQ // PIECE
AHEAD = 3
LANES = 128

EPS = 1e-06
NEG = -1000000000.0
MESH = pl.DeviceIdType.MESH
BF16 = jnp.bfloat16
F32 = jnp.float32

NN = (((1,), (0,)), ((), ()))
NT = (((1,), (1,)), ((), ()))
TN = (((0,), (0,)), ((), ()))

STREAM, BATCH, TENSOR = "stream", "batch", "tensor"
UP, DOWN, QKV, PROJ, CQ, CKV, CPROJ = "up", "down", "qkv", "proj", "cq", "ckv", "cproj"
WEIGHTS = (UP, DOWN, QKV, PROJ, CQ, CKV, CPROJ)


def bucket_starts(length, buckets):
    exact = buckets // 2
    distance = np.arange(length)
    far_bucket = exact + (
        np.log(np.maximum(distance, 1) / exact) / np.log(128.0 / exact) * (buckets - exact)
    ).astype(np.int64)
    near_table = np.where(distance < exact, distance, np.minimum(far_bucket, buckets - 1))
    return [int(np.argmax(near_table == bucket)) for bucket in range(buckets)]


def dot(left, right, dims):
    return lax.dot_general(left, right, dims, preferred_element_type=F32)


def fold(values):
    return jnp.sum(values.reshape(values.shape[0] // 8, 8, values.shape[1]), axis=0)


def mean(values):
    return jnp.mean(values, axis=-1, keepdims=True)


def weight_shapes(heads):
    inner = heads * HEAD_DIM
    return dict(
        up=(WIDTH, WIDTH),
        down=(WIDTH, WIDTH),
        qkv=(3 * inner, WIDTH),
        proj=(inner, WIDTH),
        cq=(inner, WIDTH),
        ckv=(WIDTH, 2 * inner),
        cproj=(inner, WIDTH),
    )


def scratch_shapes(heads):
    inner = heads * HEAD_DIM

    def low(*shape):
        return pltpu.VMEM(shape, BF16)

    def full(*shape):
        return pltpu.VMEM(shape, F32)

    whole = low(SEQ, WIDTH)
    head_rows = low(heads, SEQ, LANES)
    head_sums = full(heads, SEQ, LANES)
    scores = low(heads, SEQ, SEQ)
    bands = full(heads, 2 * LANES, LANES)
    room = low(3, SEQ, WIDTH)
    line = pltpu.SemaphoreType.DMA((3, 6, PIECES))
    shapes = dict(
        hid=whole, cot=whole, encb=whole, buf_a=whole, buf_b=whole, buf_c=whole, buf_u=whole,
        act=whole, dpre=whole, ag=whole, ybuf=whole,
        h1f=full(SEQ, WIDTH), h2f=full(SEQ, WIDTH),
        qa=head_rows, ka=head_rows, va=head_rows, cqa=head_rows, cka=head_rows, cva=head_rows,
        dk=head_sums, dv=head_sums, e1=scores, e2=scores,
        o1=low(inner, SEQ), o2=low(inner, SEQ), dot_in=low(inner, HALF),
        linv1=full(heads, 8, SEQ), linv2=full(heads, 8, SEQ),
        pkb=low(SEQ, 3 * inner), cqb=low(SEQ, inner), ckb=low(SEQ, 2 * inner),
        tall=full(SEQ, HALF), tall_low=low(SEQ, THIRD), wide=full(THIRD, WIDTH),
        band=bands, band_grad=bands, params=full(16, WIDTH), acc=full(10, 8, WIDTH),
        colsum=full(8, 3 * inner), mass_rows=full(8, HALF),
        small=full(16, WIDTH), small_got=full(8, 16, WIDTH), mass=full(8, LANES),
        mass_got=full(4, 8, LANES), part=room, outer=room, total=room,
        in_sem=pltpu.SemaphoreType.DMA((10,)), line_send=line, line_recv=line,
        w_send=pltpu.SemaphoreType.DMA((7, 6)), w_recv=pltpu.SemaphoreType.DMA((7, 5)),
        small_send=pltpu.SemaphoreType.DMA((7,)), small_recv=pltpu.SemaphoreType.DMA((8,)),
        mass_send=pltpu.SemaphoreType.DMA((4,)), mass_recv=pltpu.SemaphoreType.DMA((4,)),
        out_sem=pltpu.SemaphoreType.DMA((2, 3)),
        over_send=pltpu.SemaphoreType.DMA((2, 3)), over_recv=pltpu.SemaphoreType.DMA((2, 3)),
    )
    for name, shape in weight_shapes(heads).items():
        half = (shape[0] // 2, shape[1])
        shapes["w_" + name] = low(*shape)
        shapes["d_" + name] = low(*shape)
        shapes["rc_" + name] = low(*half)
        shapes["ry_" + name] = low(*half)
    return shapes


class Refs:
    pass


def layer_kernel(heads, buckets, names, *refs):
    r = Refs()
    for name, ref in zip(names, refs):
        setattr(r, name, ref)
    stream, query, place = (lax.axis_index(name) for name in (STREAM, BATCH, TENSOR))
    is_reader = stream == 1
    is_end = (place == 0) | (place == 3)
    is_middle = jnp.logical_not(is_end)
    inner_place = jnp.where(place == 0, 1, jnp.where(place == 3, 2, 3 - place))
    outer_place = jnp.where(place == 1, 0, 3)
    core = lax.rem(query, 2)
    group = query - lax.rem(query, 4)
    member = lax.rem(query, 4)

    def other(steps):
        return group + lax.rem(member + steps, 4)

    mate = query + 1 - 2 * core
    across_y = group + lax.rem(member + 2, 4)

    barrier = pltpu.get_barrier_semaphore()

    def greet(device):
        pl.semaphore_signal(barrier, inc=1, device_id=device, device_id_type=MESH)

    for steps in range(1, 4):
        greet((stream, other(steps), place))
    for steps in range(4):
        greet((1 - stream, other(steps), place))
    for steps in range(1, 4):
        greet((1 - stream, query, lax.rem(place + steps, 4)))
    greet((stream, query, inner_place))

    @pl.when(is_middle)
    def _():
        greet((stream, query, outer_place))

    def meet():
        @pl.when(is_end)
        def _():
            pl.semaphore_wait(barrier, 11)

        @pl.when(is_middle)
        def _():
            pl.semaphore_wait(barrier, 12)

    def bring(index, source, target):
        return pltpu.make_async_copy(source, target, r.in_sem.at[index])

    inputs = Refs()
    inputs.hid = bring(0, r.hidden.at[0], r.hid)
    inputs.qkv = bring(1, r.qkv_weight, r.w_qkv)
    inputs.proj = bring(2, r.proj_weight.at[0], r.w_proj)
    inputs.enc = bring(3, r.encodings.at[0], r.h2f)
    inputs.ckv = bring(4, r.cross_key_value, r.w_ckv)
    inputs.cq = bring(5, r.cross_query, r.w_cq)
    inputs.cproj = bring(6, r.cross_proj, r.w_cproj)
    inputs.up = bring(7, r.up_weight.at[0], r.w_up)
    inputs.down = bring(8, r.down_weight.at[0], r.w_down)
    inputs.cot = bring(9, r.cotangent.at[0], r.cot)

    def piece_rows(piece):
        return pl.ds(piece * PIECE, PIECE)

    side = Refs()

    def chunk_rows(chunk):
        return pl.ds(chunk * side.size, side.size)

    def row_loop(chunk, body):
        @pl.loop(0, side.size // LANES)
        def _(step):
            body(pl.ds(pl.multiple_of(chunk * side.size + step * LANES, LANES), LANES),
                 pl.ds(pl.multiple_of(step * LANES, LANES), LANES))

    def to_middle(line, room, piece):
        rows = piece_rows(piece)
        return pltpu.make_async_remote_copy(
            r.part.at[room, rows], r.outer.at[room, rows],
            r.line_send.at[0, line, piece], r.line_recv.at[0, line, piece],
            device_id=(stream, query, inner_place), device_id_type=MESH)

    def across(line, room, piece):
        rows = piece_rows(piece)
        return pltpu.make_async_remote_copy(
            r.outer.at[room, rows], r.total.at[room, rows],
            r.line_send.at[1, line, piece], r.line_recv.at[1, line, piece],
            device_id=(stream, query, inner_place), device_id_type=MESH)

    def to_end(line, room, piece):
        rows = piece_rows(piece)
        return pltpu.make_async_remote_copy(
            r.total.at[room, rows], r.total.at[room, rows],
            r.line_send.at[2, line, piece], r.line_recv.at[2, line, piece],
            device_id=(stream, query, outer_place), device_id_type=MESH)

    made, added, summed = [], [], []

    def chunk_pieces(chunk):
        count = side.size // PIECE
        return range(chunk * count, (chunk + 1) * count)

    def produce(line, room, pieces):
        @pl.when(is_end)
        def _():
            for piece in pieces:
                to_middle(line, room, piece).start()

        made.extend((line, room, piece) for piece in pieces)

    def add_outer(line, room, piece):
        rows = piece_rows(piece)
        to_middle(line, room, piece).wait_recv()
        r.outer[room, rows] += r.part[room, rows]
        across(line, room, piece).start()

    def add_inner(line, room, piece):
        rows = piece_rows(piece)
        across(line, room, piece).wait_recv()
        r.total[room, rows] += r.outer[room, rows]
        to_end(line, room, piece).start()

    def advance():
        if len(added) < len(made) and len(added) - len(summed) < AHEAD:
            item = made[len(added)]
            added.append(item)
            add_outer(*item)
        else:
            item = made[len(summed)]
            summed.append(item)
            add_inner(*item)

    def pump(count=1):
        steps = min(2 * count, 2 * len(made) - len(added) - len(summed))
        if steps > 0:
            @pl.when(is_middle)
            def _():
                for _ in range(steps):
                    advance()

    def finish(line, room, pieces):
        last = max(made.index((line, room, piece)) for piece in pieces)

        @pl.when(is_middle)
        def _():
            while len(summed) <= last:
                advance()

        @pl.when(is_end)
        def _():
            for piece in pieces:
                to_end(line, room, piece).wait_recv()
                to_middle(line, room, piece).wait_send()

    def settle(line, room, pieces):
        @pl.when(is_middle)
        def _():
            for piece in pieces:
                across(line, room, piece).wait_send()
                to_end(line, room, piece).wait_send()

    def hand_on(line, room, chunk, before=None):
        pieces = chunk_pieces(chunk)
        if before:
            settle(*before, pieces)
        produce(line, room, pieces)

    def collect(line, room, chunk):
        finish(line, room, chunk_pieces(chunk))

    def hand_over(chunk):
        rows = pl.ds(chunk * THIRD, THIRD)
        return pltpu.make_async_remote_copy(
            r.part.at[2, rows], r.part.at[2, rows], r.over_send.at[0, chunk], r.over_recv.at[0, chunk],
            device_id=(1 - stream, query, place), device_id_type=MESH)

    def hand_back(chunk):
        rows = pl.ds(chunk * THIRD, THIRD)
        return pltpu.make_async_remote_copy(
            r.total.at[2, rows], r.total.at[2, rows], r.over_send.at[1, chunk], r.over_recv.at[1, chunk],
            device_id=(1 - stream, query, place), device_id_type=MESH)

    def third_pieces(chunk):
        count = THIRD // PIECE
        return range(chunk * count, (chunk + 1) * count)

    def w_copy(source, target, index, send, recv, device):
        return pltpu.make_async_remote_copy(
            source, target, r.w_send.at[index, send], r.w_recv.at[index, recv],
            device_id=device, device_id_type=MESH)

    def w_parts(name):
        grad = getattr(r, "d_" + name)
        half = grad.shape[0] // 2
        mine = pl.ds(pl.multiple_of(core * half, half), half)
        theirs = pl.ds(pl.multiple_of((1 - core) * half, half), half)
        return WEIGHTS.index(name), grad, getattr(r, "rc_" + name), getattr(r, "ry_" + name), mine, theirs

    def w_first(name):
        index, grad, rc, ry, mine, theirs = w_parts(name)
        return w_copy(grad.at[theirs], rc, index, 0, 0, (stream, mate, place))

    def w_second(name):
        index, grad, rc, ry, mine, theirs = w_parts(name)
        return w_copy(rc, ry, index, 1, 1, (stream, across_y, place))

    def w_third(name):
        index, grad, rc, ry, mine, theirs = w_parts(name)
        out = getattr(r, name)
        return w_copy(grad.at[mine], out.at[mine], index, 2, 2, (stream, mate, place))

    def w_local(name):
        index, grad, rc, ry, mine, theirs = w_parts(name)
        return pltpu.make_async_copy(grad.at[mine], getattr(r, name).at[mine], r.w_send.at[index, 3])

    def w_other_side(name):
        index, grad, rc, ry, mine, theirs = w_parts(name)
        out = getattr(r, name)
        return w_copy(grad.at[mine], out.at[mine], index, 4, 3, (1 - stream, query, place))

    def w_forward(name):
        index, grad, rc, ry, mine, theirs = w_parts(name)
        out = getattr(r, name)
        return w_copy(out.at[mine], out.at[mine], index, 5, 4, (stream, mate, place))

    def w_start(name):
        w_first(name).start()

    def w_combine(name):
        index, grad, rc, ry, mine, theirs = w_parts(name)
        w_first(name).wait_recv()
        step = 48 if rc.shape[0] % 64 else 64

        @pl.loop(0, rc.shape[0] // step)
        def _(i):
            rows = pl.ds(pl.multiple_of(i * step, step), step)
            own = pl.ds(pl.multiple_of(core * rc.shape[0] + i * step, step), step)
            rc[rows] += grad[own]

        w_second(name).start()

    def w_store(name):
        index, grad, rc, ry, mine, theirs = w_parts(name)
        w_second(name).wait_recv()
        step = 48 if rc.shape[0] % 64 else 64

        @pl.loop(0, rc.shape[0] // step)
        def _(i):
            rows = pl.ds(pl.multiple_of(i * step, step), step)
            own = pl.ds(pl.multiple_of(core * rc.shape[0] + i * step, step), step)
            grad[own] = ry[rows] + rc[rows]

        w_third(name).start()
        w_local(name).start()
        if name in (CQ, CKV, CPROJ):
            w_other_side(name).start()

    def w_end(name):
        w_first(name).wait_send()
        w_second(name).wait_send()
        w_third(name).wait()
        w_local(name).wait()
        if name in (CQ, CKV, CPROJ):
            w_other_side(name).wait_send()

    def softmax(exp_ref, head, chunk, first_key, keys, banded):
        sums = []
        for tile in range(side.size // LANES):
            cols = pl.ds(tile * LANES, LANES)
            rows = pl.ds(chunk * side.size + tile * LANES, LANES)
            end = chunk * side.size + (tile + 1) * LANES if banded else keys
            if banded:
                near = min(end, 2 * LANES)
                r.tall[pl.ds(end - near, near), cols] += r.band[head, pl.ds(2 * LANES - near, near)]
            top = jnp.max(r.tall[pl.ds(0, end), cols], axis=0, keepdims=True)
            parts = [jnp.zeros((1, LANES), F32), jnp.zeros((1, LANES), F32)]
            for key in range(0, end, LANES):
                grown = jnp.exp(r.tall[pl.ds(key, LANES), cols] - top)
                exp_ref[head, pl.ds(first_key + key, LANES), rows] = grown.astype(BF16)
                parts[key // HALF] += jnp.sum(grown, axis=0, keepdims=True)
            for key in range(end, keys, LANES):
                exp_ref[head, pl.ds(first_key + key, LANES), rows] = jnp.zeros((LANES, LANES), BF16)
            sums.append(parts)
        return [jnp.concatenate([parts[p] for parts in sums], axis=1) for p in range(2)]

    def head_rows(head):
        return pl.ds(pl.multiple_of(head * HEAD_DIM, HEAD_DIM), HEAD_DIM)

    def attend(qa, ka, va, exp_ref, out_ref, inv_ref, chunk, first_key, keys, banded, mass):
        rows = chunk_rows(chunk)
        span = pl.ds(first_key, keys)
        cols = pl.ds(0, side.size)
        live = lax.broadcasted_iota(jnp.int32, (1, side.size), 1) + chunk * side.size < r.target_lengths[0]

        @pl.loop(0, heads)
        def _(head):
            r.tall[pl.ds(0, keys), cols] = dot(ka[head, span], qa[head, rows], NT)
            parts = softmax(exp_ref, head, chunk, first_key, keys, banded)
            inverse = 1.0 / (parts[0] + parts[1])
            inv_ref[head, pl.ds(0, 1), rows] = inverse
            if mass:
                for p in range(NPASS):
                    r.mass_rows[pl.ds(p, 1), cols] += jnp.where(live, parts[p] * inverse, 0.0)
            mixed = dot(va[head, span, pl.ds(0, HEAD_DIM)], exp_ref[head, span, rows], TN)
            out_ref[head_rows(head), rows] = (mixed * inverse).astype(BF16)

    def attend_back(qa, ka, va, exp_ref, out_ref, chunk, first_key, keys, fresh, banded):
        rows = chunk_rows(chunk)
        span = pl.ds(first_key, keys)
        cols = pl.ds(0, side.size)
        low = pl.ds(0, HEAD_DIM)

        @pl.loop(0, heads)
        def _(head):
            lanes = head_rows(head)
            grad_out = r.dot_in[lanes, cols]
            spread = jnp.sum(
                grad_out.astype(F32) * out_ref[lanes, rows].astype(F32), axis=0, keepdims=True)
            weight = exp_ref[head, span, rows]
            score_grad = (
                weight.astype(F32) * (dot(va[head, span, low], grad_out, NN) - spread)).astype(BF16)
            if banded:
                r.tall_low[pl.ds(0, keys), cols] = score_grad
                for tile in range(side.size // LANES):
                    end = chunk * side.size + (tile + 1) * LANES
                    near = min(end, 2 * LANES)
                    r.band_grad[head, pl.ds(2 * LANES - near, near)] += (
                        r.tall_low[pl.ds(end - near, near), pl.ds(tile * LANES, LANES)].astype(F32))
            query_grad = dot(score_grad, ka[head, span], TN)
            key_grad = dot(score_grad, qa[head, rows], NN)
            value_grad = dot(weight, grad_out, NT)
            qa[head, rows, low] = (query_grad[:, :HEAD_DIM] * HEAD_DIM ** (-0.5)).astype(BF16)
            if fresh:
                r.dk[head, span] = key_grad
                r.dv[head, span, low] = value_grad
            else:
                r.dk[head, span] += key_grad
                r.dv[head, span, low] += value_grad

    def grad_of_mixed(weight, grad_ref, inv_ref, chunk):
        grads = dot(weight[...], grad_ref[chunk_rows(chunk)], NT)
        for head in range(heads):
            lanes = pl.ds(head * HEAD_DIM, HEAD_DIM)
            r.dot_in[lanes, pl.ds(0, side.size)] = (
                grads[head * HEAD_DIM:(head + 1) * HEAD_DIM] * inv_ref[head, pl.ds(0, 1), chunk_rows(chunk)]
            ).astype(BF16)

    def fill_tails(qa, ka, valid):
        shape = (SEQ, HEAD_DIM)
        lane = lax.broadcasted_iota(jnp.int32, shape, 1)
        key = lax.broadcasted_iota(jnp.int32, shape, 0)
        ones = jnp.where(lane == 0, 1.0, 0.0).astype(BF16)
        fence = jnp.where((lane == 0) & jnp.logical_not(valid(key)), NEG, 0.0).astype(BF16)
        for head in range(heads):
            qa[head, :, pl.ds(HEAD_DIM, HEAD_DIM)] = ones
            ka[head, :, pl.ds(HEAD_DIM, HEAD_DIM)] = fence

    def in_passage(key):
        low = (key < HALF) & (key < r.passage_lengths[0, 0])
        return low | ((key >= HALF) & (key - HALF < r.passage_lengths[0, 1]))

    def in_target(key):
        return key < r.target_lengths[0]

    def split_packed(rows):
        for head in range(heads):
            base = 3 * HEAD_DIM * head
            low = pl.ds(0, HEAD_DIM)
            r.qa[head, rows, low] = (
                r.pkb[rows, pl.ds(base, HEAD_DIM)].astype(F32) * HEAD_DIM ** (-0.5)).astype(BF16)
            r.ka[head, rows, low] = r.pkb[rows, pl.ds(base + HEAD_DIM, HEAD_DIM)]
            r.va[head, rows, low] = r.pkb[rows, pl.ds(base + 2 * HEAD_DIM, HEAD_DIM)]

    def project_out(line, room, chunk, out_ref, weight, before=None):
        for tile in range(side.size // LANES):
            rows = pl.ds(chunk * side.size + tile * LANES, LANES)
            r.part[room, rows] = dot(out_ref[:, rows], weight[...], TN).astype(BF16)
        hand_on(line, room, chunk, before)

    def param(row):
        return r.params[pl.ds(row, 1)]

    def add_to(slot, values):
        r.acc[slot] += fold(values)

    def gelu_parts(values):
        cubic = 0.7978845608028654 * (values + 0.044715 * values * values * values)
        bend = jnp.tanh(cubic)
        slope = 0.7978845608028654 * (1.0 + 3.0 * 0.044715 * values * values)
        return 0.5 * values * (1.0 + bend), 0.5 * (1.0 + bend) + 0.5 * values * (1.0 - bend * bend) * slope

    def pack_grads(chunk):
        rows = chunk_rows(chunk)
        for head in range(heads):
            base = 3 * HEAD_DIM * head
            low = pl.ds(0, HEAD_DIM)
            r.pkb[rows, pl.ds(base, HEAD_DIM)] = r.qa[head, rows, low]
            r.pkb[rows, pl.ds(base + HEAD_DIM, HEAD_DIM)] = r.dk[head, rows, low].astype(BF16)
            r.pkb[rows, pl.ds(base + 2 * HEAD_DIM, HEAD_DIM)] = r.dv[head, rows, low].astype(BF16)

    def input_part(line, room, chunk, before):
        rows = chunk_rows(chunk)
        r.part[room, rows] = dot(r.pkb[rows], r.w_qkv[...], NN).astype(BF16)
        hand_on(line, room, chunk, before)

    def weight_grad(target, left, right):
        @pl.loop(0, left.shape[1] // THIRD)
        def _(step):
            rows = pl.ds(pl.multiple_of(step * THIRD, THIRD), THIRD)
            target[rows] = dot(left[:, rows], right[...], TN).astype(BF16)

    def third_loop(body):
        @pl.loop(0, SEQ // THIRD)
        def _(step):
            body(pl.ds(pl.multiple_of(step * THIRD, THIRD), THIRD))

    def clear():
        r.acc[...] = jnp.zeros_like(r.acc)
        r.small[...] = jnp.zeros_like(r.small)

    def store_input_grad(chunk):
        rows = chunk_rows(chunk)
        return pltpu.make_async_copy(r.h1f.at[rows], r.gin.at[rows], r.out_sem.at[0, chunk])

    def store_result(chunk):
        rows = chunk_rows(chunk)
        return pltpu.make_async_copy(r.ybuf.at[rows], r.y.at[rows], r.out_sem.at[1, chunk])

    def small_copies():
        copies = []
        for side_step in range(2):
            for steps in range(4):
                if side_step == 0 and steps == 0:
                    continue
                device = (lax.rem(stream + side_step, 2), other(steps), place)
                copies.append(pltpu.make_async_remote_copy(
                    r.small, r.small_got.at[stream * 4 + member], r.small_send.at[len(copies)],
                    r.small_recv.at[stream * 4 + member], device_id=device, device_id_type=MESH))
        return copies

    def start_small():
        for copy in small_copies():
            copy.start()
        r.small_got[stream * 4 + member] = r.small[...]

    def end_small():
        for side_step in range(2):
            for steps in range(4):
                if side_step == 0 and steps == 0:
                    continue
                source = lax.rem(stream + side_step, 2) * 4 + lax.rem(member + steps, 4)
                pltpu.make_async_remote_copy(
                    r.small, r.small_got.at[source], r.small_send.at[0], r.small_recv.at[source],
                    device_id=(stream, mate, place), device_id_type=MESH).wait_recv()
        for copy in small_copies():
            copy.wait_send()
        total = r.small_got[0]
        for index in range(1, 8):
            total = total + r.small_got[index]
        loss = r.small_got[member, pl.ds(12, 1)]
        r.small_out[...] = total
        r.small_out[pl.ds(12, 1)] = loss

    def reader():
        side.size = THIRD
        order = (2, 1, 0)
        inputs.hid.start()
        inputs.qkv.start()
        r.params[pl.ds(8, 3)] = r.scale_gain[...].astype(F32)
        starts = bucket_starts(SEQ, buckets)
        shape = (2 * LANES, LANES)
        apart = (
            lax.broadcasted_iota(jnp.int32, shape, 1) + LANES - lax.broadcasted_iota(jnp.int32, shape, 0))
        shifts = r.position_bias[...].astype(F32)
        shifts = shifts - shifts[:, buckets - 1:]
        for head in range(heads):
            band = jnp.broadcast_to(shifts[head:head + 1, 0:1], shape)
            for bucket in range(1, buckets):
                band = jnp.where(apart >= starts[bucket], shifts[head:head + 1, bucket:bucket + 1], band)
            r.band[head] = jnp.where(apart >= 0, band, NEG)
        fill_tails(r.qa, r.ka, in_target)

        inputs.hid.wait()
        for copy in (inputs.proj, inputs.enc, inputs.ckv, inputs.cq, inputs.cproj):
            copy.start()
        for copy in (inputs.up, inputs.down, inputs.cot):
            copy.start()
        gain = param(8)

        def normalize(rows):
            values = r.hid[rows].astype(F32)
            r.buf_a[rows] = (values * lax.rsqrt(mean(values * values) + EPS) * gain).astype(BF16)
        third_loop(normalize)
        inputs.qkv.wait()

        def project(rows):
            r.pkb[rows] = dot(r.buf_a[rows], r.w_qkv[...], NT).astype(BF16)
            split_packed(rows)
        third_loop(project)
        inputs.proj.wait()
        for chunk in order:
            attend(
                r.qa, r.ka, r.va, r.e1, r.o1, r.linv1, chunk, 0, (chunk + 1) * THIRD, True, False)
            if chunk == order[-1]:
                pump()
            if chunk == order[0]:
                meet()
            project_out(0, 0, chunk, r.o1, r.w_proj)

        clear()
        r.mass_rows[...] = jnp.zeros_like(r.mass_rows)
        r.band_grad[...] = jnp.zeros_like(r.band_grad)
        fill_tails(r.cqa, r.cka, in_passage)

        inputs.enc.wait()
        inputs.ckv.wait()
        pump()

        def encode(rows):
            r.encb[rows] = r.h2f[rows].astype(BF16)
            r.ckb[rows] = dot(r.encb[rows], r.w_ckv[...], NN).astype(BF16)
            for head in range(heads):
                low = pl.ds(0, HEAD_DIM)
                r.cka[head, rows, low] = r.ckb[rows, pl.ds(2 * HEAD_DIM * head, HEAD_DIM)]
                r.cva[head, rows, low] = r.ckb[rows, pl.ds(2 * HEAD_DIM * head + HEAD_DIM, HEAD_DIM)]
        third_loop(encode)
        pump()
        inputs.down.wait()
        inputs.cot.wait()

        def act_grad(rows):
            r.buf_c[rows] = dot(r.cot[rows], r.w_down[...], NT).astype(BF16)
        third_loop(act_grad)
        inputs.cq.wait()
        inputs.cproj.wait()
        inputs.up.wait()

        gain = param(9)
        for chunk in order:
            rows = chunk_rows(chunk)
            collect(0, 0, chunk)

            def first_sum(rows, _):
                values = r.hid[rows].astype(F32) + r.total[0, rows].astype(F32)
                r.h1f[rows] = values
                r.buf_b[rows] = (values * lax.rsqrt(mean(values * values) + EPS) * gain).astype(BF16)
            row_loop(chunk, first_sum)
            r.cqb[rows] = dot(r.buf_b[rows], r.w_cq[...], NT).astype(BF16)
            for head in range(heads):
                r.cqa[head, rows, pl.ds(0, HEAD_DIM)] = (
                    r.cqb[rows, pl.ds(head * HEAD_DIM, HEAD_DIM)].astype(F32) * HEAD_DIM ** (-0.5)
                ).astype(BF16)
            pump()
            attend(r.cqa, r.cka, r.cva, r.e2, r.o2, r.linv2, chunk, 0, SEQ, False, True)
            pump()
            project_out(1, 1, chunk, r.o2, r.w_cproj, (0, 0))

        lane = lax.broadcasted_iota(jnp.int32, (8, LANES), 1)
        masses = [jnp.sum(r.mass_rows[pl.ds(p, 1)], axis=1, keepdims=True) for p in range(NPASS)]
        r.mass[...] = jnp.where(lane == 0, masses[0], jnp.where(lane == 1, masses[1], 0.0))

        def mass_copy(steps):
            return pltpu.make_async_remote_copy(
                r.mass, r.mass_got.at[place], r.mass_send.at[steps], r.mass_recv.at[place],
                device_id=(1 - stream, query, lax.rem(place + steps, 4)), device_id_type=MESH)

        for steps in range(4):
            mass_copy(steps).start()

        gain = param(10)
        for chunk in order:
            rows = chunk_rows(chunk)
            collect(1, 1, chunk)

            def second_sum(rows, _):
                values = r.h1f[rows] + r.total[1, rows].astype(F32)
                r.h2f[rows] = values
                r.ybuf[rows] = values.astype(BF16)
                r.buf_u[rows] = (values * lax.rsqrt(mean(values * values) + EPS) * gain).astype(BF16)
            row_loop(chunk, second_sum)
            r.wide[pl.ds(0, side.size)] = dot(r.buf_u[rows], r.w_up[...], NN)
            pump()

            def bend(rows, local):
                value, slope = gelu_parts(r.wide[local])
                r.act[rows] = value.astype(BF16)
                r.dpre[rows] = (r.buf_c[rows].astype(F32) * slope).astype(BF16)
            row_loop(chunk, bend)
            pump()
            r.part[0, rows] = dot(r.dpre[rows], r.w_up[...], NT).astype(BF16)
            hand_on(2, 0, chunk, (1, 1))
            r.part[2, rows] = dot(r.act[rows], r.w_down[...], NN).astype(BF16)
            if chunk != order[-1]:
                hand_over(chunk).start()

        weight_grad(r.d_up, r.buf_u, r.dpre)
        w_start(UP)
        pump()
        weight_grad(r.d_down, r.act, r.cot)
        w_start(DOWN)
        pump()

        for chunk in order:
            rows = chunk_rows(chunk)
            collect(2, 0, chunk)
            if chunk == order[0]:
                w_combine(UP)
                w_combine(DOWN)

            def second_grad(rows, _):
                values = r.h2f[rows]
                grads = r.total[0, rows].astype(F32)
                root = lax.rsqrt(mean(values * values) + EPS)
                add_to(2, grads * values * root)
                scaled = grads * gain
                back = root * scaled - values * (root * root * root) * mean(scaled * values)
                result = r.cot[rows].astype(F32) + back
                r.h2f[rows] = result
                r.buf_c[rows] = result.astype(BF16)
            row_loop(chunk, second_grad)
            grad_of_mixed(r.w_cproj, r.buf_c, r.linv2, chunk)
            pump()
            attend_back(r.cqa, r.cka, r.cva, r.e2, r.o2, chunk, 0, SEQ, chunk == order[0], False)
            pump()
            for head in range(heads):
                r.cqb[rows, pl.ds(head * HEAD_DIM, HEAD_DIM)] = r.cqa[head, rows, pl.ds(0, HEAD_DIM)]
            r.part[1, rows] = dot(r.cqb[rows], r.w_cq[...], NN).astype(BF16)
            hand_on(3, 1, chunk, (2, 0))

        pump()
        for chunk in order:
            rows = chunk_rows(chunk)
            for head in range(heads):
                low = pl.ds(0, HEAD_DIM)
                r.ckb[rows, pl.ds(2 * HEAD_DIM * head, HEAD_DIM)] = r.dk[head, rows, low].astype(BF16)
                r.ckb[rows, pl.ds(2 * HEAD_DIM * head + HEAD_DIM, HEAD_DIM)] = (
                    r.dv[head, rows, low].astype(BF16))
        r.d_cproj[...] = dot(r.o2[...], r.buf_c[...], NN).astype(BF16)
        w_start(CPROJ)
        r.d_cq[...] = dot(r.cqb[...], r.buf_b[...], TN).astype(BF16)
        w_start(CQ)
        pump()
        weight_grad(r.d_ckv, r.encb, r.ckb)
        w_start(CKV)

        gain = param(9)
        for chunk in order:
            rows = chunk_rows(chunk)
            collect(3, 1, chunk)
            if chunk == order[0]:
                for name in (CPROJ, CQ, CKV):
                    w_combine(name)

            def first_grad(rows, _):
                values = r.h1f[rows]
                grads = r.total[1, rows].astype(F32)
                root = lax.rsqrt(mean(values * values) + EPS)
                add_to(1, grads * values * root)
                scaled = grads * gain
                back = root * scaled - values * (root * root * root) * mean(scaled * values)
                result = r.h2f[rows] + back
                r.h1f[rows] = result
                r.ag[rows] = result.astype(BF16)
            row_loop(chunk, first_grad)
            grad_of_mixed(r.w_proj, r.ag, r.linv1, chunk)
            pump()
            attend_back(
                r.qa, r.ka, r.va, r.e1, r.o1, chunk, 0, (chunk + 1) * THIRD, chunk == order[0], True)
            pump()
            pack_grads(chunk)
            input_part(4, 0, chunk, (3, 1))
            if chunk == order[1]:
                w_store(UP)
                w_store(DOWN)
        produce(5, 2, third_pieces(0))
        r.d_qkv[...] = dot(r.pkb[...], r.buf_a[...], TN).astype(BF16)
        w_start(QKV)
        r.d_proj[...] = dot(r.o1[...], r.ag[...], NN).astype(BF16)
        w_start(PROJ)
        for name in (CPROJ, CQ, CKV):
            w_store(name)
        w_combine(QKV)
        w_combine(PROJ)
        pump()

        lane = lax.broadcasted_iota(jnp.int32, (1, LANES), 1)
        table = jnp.zeros((1, LANES), F32)
        for head in range(heads):
            grads = r.band_grad[head]
            rest = jnp.sum(
                jnp.sum(r.dk[head], axis=0, keepdims=True)[:, HEAD_DIM:HEAD_DIM + 1], axis=1, keepdims=True)
            for bucket in range(buckets - 1):
                inside = (apart >= starts[bucket]) & (apart < starts[bucket + 1])
                value = jnp.sum(
                    jnp.sum(jnp.where(inside, grads, 0.0), axis=0, keepdims=True), axis=1, keepdims=True)
                rest = rest - value
                table = jnp.where(lane == head * buckets + bucket, value, table)
            table = jnp.where(lane == head * buckets + buckets - 1, rest, table)
        r.small[pl.ds(11, 1), pl.ds(0, LANES)] = table

        def last_sum(chunk):
            def add(rows, _):
                r.ybuf[rows] = (r.ybuf[rows].astype(F32) + r.total[2, rows].astype(F32)).astype(BF16)
            row_loop(chunk, add)
            store_result(chunk).start()

        gain = param(8)
        for chunk in order:
            if chunk != order[-1]:
                hand_back(chunk).wait_recv()
                last_sum(chunk)
            collect(4, 0, chunk)

            def input_grad(rows, _):
                values = r.hid[rows].astype(F32)
                grads = r.total[0, rows].astype(F32)
                root = lax.rsqrt(mean(values * values) + EPS)
                add_to(0, grads * values * root)
                scaled = grads * gain
                back = root * scaled - values * (root * root * root) * mean(scaled * values)
                r.h1f[rows] = r.h1f[rows] + back
            row_loop(chunk, input_grad)
            store_input_grad(chunk).start()

        for slot in range(3):
            r.small[pl.ds(8 + slot, 1)] = jnp.sum(r.acc[slot], axis=0, keepdims=True)
        start_small()
        w_store(QKV)
        w_store(PROJ)
        collect(5, 2, 0)
        last_sum(0)
        end_small()
        settle(5, 2, third_pieces(0))
        for chunk in order:
            settle(4, 0, chunk_pieces(chunk))
            if chunk != order[-1]:
                hand_over(chunk).wait_send()
            store_input_grad(chunk).wait()
            store_result(chunk).wait()
        for name in WEIGHTS:
            w_end(name)
        for steps in range(4):
            mass_copy(steps).wait_send()

    def retriever():
        side.size = HALF
        order = (1, 0)
        inputs.hid.start()
        inputs.qkv.start()
        r.params[pl.ds(0, 2)] = r.layer_gain[...].astype(F32)
        r.params[pl.ds(2, 2)] = r.layer_shift[...].astype(F32)
        r.params[pl.ds(4, 2)] = r.output_bias[...].astype(F32)
        r.params[pl.ds(6, 1)] = r.biases[:, pl.ds(2 * heads * HEAD_DIM, WIDTH)].astype(F32)
        r.colsum[...] = jnp.zeros_like(r.colsum)
        r.params[pl.ds(11, 1), pl.ds(0, 2 * heads * HEAD_DIM)] = (
            r.biases[:, pl.ds(0, 2 * heads * HEAD_DIM)].astype(F32))
        for head in range(heads):
            base = 3 * HEAD_DIM * head
            for k in range(2):
                r.colsum[pl.ds(0, 1), pl.ds(base + 2 * k * HEAD_DIM, HEAD_DIM)] = (
                    r.params[pl.ds(11, 1), pl.ds((2 * head + k) * HEAD_DIM, HEAD_DIM)])
        shift = r.colsum[pl.ds(0, 1)]
        fill_tails(r.qa, r.ka, in_passage)
        inputs.hid.wait()
        for copy in (inputs.proj, inputs.up, inputs.down, inputs.cot):
            copy.start()
        inputs.qkv.wait()
        inputs.proj.wait()
        for chunk in order:
            rows = chunk_rows(chunk)
            r.pkb[rows] = (dot(r.hid[rows], r.w_qkv[...], NT) + shift).astype(BF16)
            split_packed(rows)
            attend(r.qa, r.ka, r.va, r.e1, r.o1, r.linv1, chunk, chunk * HALF, HALF, False, False)
            if chunk == order[0]:
                meet()
            project_out(0, 0, chunk, r.o1, r.w_proj)
        r.colsum[...] = jnp.zeros_like(r.colsum)
        clear()

        inputs.up.wait()
        inputs.down.wait()
        inputs.cot.wait()
        gain1, gain2 = param(0), param(1)
        shift1, shift2 = param(2), param(3)
        out1, out2, unit = param(4), param(5), param(6)
        side.size = THIRD
        thirds = (2, 1, 0)
        for chunk in thirds:
            rows = chunk_rows(chunk)
            collect(0, 0, chunk)

            def first_norm(rows, _):
                values = r.hid[rows].astype(F32) + r.total[0, rows].astype(F32) + out1
                centered = values - mean(values)
                root = lax.rsqrt(mean(centered * centered) + EPS)
                r.h1f[rows] = values
                r.buf_u[rows] = (centered * root * gain1 + shift1).astype(BF16)
            row_loop(chunk, first_norm)
            r.wide[pl.ds(0, THIRD)] = dot(r.buf_u[rows], r.w_up[...], NN)
            pump()

            def bend(rows, local):
                value, slope = gelu_parts(r.wide[local] + unit)
                r.act[rows] = value.astype(BF16)
                r.buf_a[rows] = slope.astype(BF16)
            row_loop(chunk, bend)
            pump()
            r.part[1, rows] = dot(r.act[rows], r.w_down[...], NN).astype(BF16)
            hand_on(1, 1, chunk, (0, 0))

        def valid(rows):
            token = lax.broadcasted_iota(jnp.int32, (LANES, 1), 0) + rows.start
            low = (token < HALF) & (token < r.passage_lengths[0, 0])
            return low, (token >= HALF) & (token - HALF < r.passage_lengths[0, 1])

        for chunk in thirds:
            collect(1, 1, chunk)

            def second_norm(rows, _):
                values = r.h1f[rows]
                centered = values - mean(values)
                root = lax.rsqrt(mean(centered * centered) + EPS)
                values = centered * root * gain1 + shift1 + r.total[1, rows].astype(F32) + out2
                r.h2f[rows] = values
                centered = values - mean(values)
                root = lax.rsqrt(mean(centered * centered) + EPS)
                result = centered * root * gain2 + shift2
                r.ybuf[rows] = result.astype(BF16)
                for p, token in enumerate(valid(rows)):
                    add_to(8 + p, jnp.where(token, result, 0.0))
            row_loop(chunk, second_norm)
            store_result(chunk).start()
            if chunk == 1:
                hand_over(2).wait_recv()
                produce(5, 2, third_pieces(2))

        vector = r.query_vectors[...]
        scores = [
            jnp.sum(jnp.sum(r.acc[8 + p], axis=0, keepdims=True) * vector, axis=1, keepdims=True)
            / r.passage_lengths[0, p].astype(F32)
            for p in range(NPASS)
        ]

        def mass_wait(source):
            return pltpu.make_async_remote_copy(
                r.mass, r.mass_got.at[source], r.mass_send.at[0], r.mass_recv.at[source],
                device_id=(1 - stream, query, place), device_id_type=MESH)

        for source in range(4):
            mass_wait(source).wait_recv()
        masses = r.mass_got[0].astype(BF16).astype(F32)
        for source in range(1, 4):
            masses = masses + r.mass_got[source].astype(BF16).astype(F32)
        scale = HEADS * r.target_lengths[0].astype(F32)
        targets = [masses[0:1, p:p + 1] / scale for p in range(NPASS)]
        top = jnp.maximum(scores[0], scores[1])
        norm = top + jnp.log(jnp.exp(scores[0] - top) + jnp.exp(scores[1] - top))
        logs = [score - norm for score in scores]
        loss = targets[0] * (jnp.log(targets[0]) - logs[0]) + targets[1] * (jnp.log(targets[1]) - logs[1])
        r.small[pl.ds(12, 1)] = jnp.broadcast_to(loss, (1, WIDTH))
        pulls = [
            (jnp.exp(logs[p]) * (targets[0] + targets[1]) - targets[p])
            / r.passage_lengths[0, p].astype(F32) * vector
            for p in range(NPASS)
        ]

        for chunk in thirds:
            rows = chunk_rows(chunk)

            def final_grad(rows, _):
                low, high = valid(rows)
                upstream = r.cot[rows].astype(F32) + jnp.where(
                    low, pulls[0], jnp.where(high, pulls[1], 0.0))
                values = r.h2f[rows]
                centered = values - mean(values)
                root = lax.rsqrt(mean(centered * centered) + EPS)
                normed = centered * root
                scaled = upstream * gain2
                result = root * (scaled - mean(scaled) - normed * mean(scaled * normed))
                add_to(1, upstream * normed)
                add_to(3, upstream)
                r.h2f[rows] = result
                low = result.astype(BF16)
                r.buf_b[rows] = low
                add_to(5, low.astype(F32))
            row_loop(chunk, final_grad)
            if chunk == 2:
                pump()
            r.wide[pl.ds(0, THIRD)] = dot(r.buf_b[rows], r.w_down[...], NT)
            if chunk == 2:
                pump()

            def bend_back(rows, local):
                low = (r.wide[local] * r.buf_a[rows].astype(F32)).astype(BF16)
                r.dpre[rows] = low
                add_to(6, low.astype(F32))
            row_loop(chunk, bend_back)
            pump()
            r.part[0, rows] = dot(r.dpre[rows], r.w_up[...], NT).astype(BF16)
            hand_on(2, 0, chunk, (1, 1))
        hand_over(1).wait_recv()
        produce(5, 2, third_pieces(1))

        weight_grad(r.d_up, r.buf_u, r.dpre)
        w_start(UP)
        pump()
        weight_grad(r.d_down, r.act, r.buf_b)
        w_start(DOWN)
        pump()
        finish(5, 2, third_pieces(2))
        hand_back(2).start()

        side.size = HALF
        for chunk in order:
            rows = chunk_rows(chunk)
            collect(2, 0, chunk)
            if chunk == order[0]:
                w_combine(UP)
                w_combine(DOWN)

            def middle_grad(rows, _):
                upstream = r.h2f[rows] + r.total[0, rows].astype(F32)
                values = r.h1f[rows]
                centered = values - mean(values)
                root = lax.rsqrt(mean(centered * centered) + EPS)
                normed = centered * root
                scaled = upstream * gain1
                result = root * (scaled - mean(scaled) - normed * mean(scaled * normed))
                add_to(0, upstream * normed)
                add_to(2, upstream)
                r.h1f[rows] = result
                low = result.astype(BF16)
                r.ag[rows] = low
                add_to(4, low.astype(F32))
            row_loop(chunk, middle_grad)
            grad_of_mixed(r.w_proj, r.ag, r.linv1, chunk)
            pump()
            attend_back(r.qa, r.ka, r.va, r.e1, r.o1, chunk, chunk * HALF, HALF, True, False)
            pump()
            pack_grads(chunk)
            input_part(4, 1, chunk, (2, 0))
            r.colsum[...] += fold(r.pkb[rows].astype(F32))
            if chunk == order[0]:
                finish(5, 2, third_pieces(1))
                hand_back(1).start()
        r.d_qkv[...] = dot(r.pkb[...], r.hid[...], TN).astype(BF16)
        w_start(QKV)
        r.d_proj[...] = dot(r.o1[...], r.ag[...], NN).astype(BF16)
        w_start(PROJ)
        pump()

        w_combine(QKV)
        w_combine(PROJ)
        for chunk in order:
            rows = chunk_rows(chunk)
            collect(4, 1, chunk)
            if chunk == order[0]:
                w_store(UP)
                w_store(DOWN)

            def input_grad(rows, _):
                r.h1f[rows] = r.h1f[rows] + r.total[1, rows].astype(F32)
            row_loop(chunk, input_grad)
            store_input_grad(chunk).start()

        columns = jnp.sum(r.colsum[...], axis=0, keepdims=True)
        r.colsum[pl.ds(0, 1)] = columns
        for head in range(heads):
            base = 3 * HEAD_DIM * head
            for k in range(2):
                r.small[pl.ds(0, 1), pl.ds((2 * head + k) * HEAD_DIM, HEAD_DIM)] = (
                    r.colsum[pl.ds(0, 1), pl.ds(base + 2 * k * HEAD_DIM, HEAD_DIM)])
        r.small[pl.ds(1, 1)] = jnp.sum(r.acc[6], axis=0, keepdims=True)
        for slot in range(6):
            r.small[pl.ds(2 + slot, 1)] = jnp.sum(r.acc[slot], axis=0, keepdims=True)
        start_small()
        w_store(QKV)
        w_store(PROJ)
        for name in (CQ, CKV, CPROJ):
            w_other_side(name).wait_recv()
            w_forward(name).start()
        end_small()
        for chunk in order:
            settle(4, 1, chunk_pieces(chunk))
            store_input_grad(chunk).wait()
        side.size = THIRD
        for chunk in thirds:
            if chunk > 0:
                settle(5, 2, third_pieces(chunk))
                hand_back(chunk).wait_send()
            store_result(chunk).wait()
        for name in (UP, DOWN, QKV, PROJ):
            w_end(name)
        for name in (CQ, CKV, CPROJ):
            w_forward(name).wait()

    @pl.when(is_reader)
    def _():
        reader()

    for items in (made, added, summed):
        items.clear()

    @pl.when(jnp.logical_not(is_reader))
    def _():
        retriever()


def finish_kernel(heads, buckets, *refs):
    count = len(WEIGHTS)
    small, result, input_grad, *grads = refs[: count + 3]
    outs = refs[count + 3 : 2 * count + 5]
    small_outs = refs[2 * count + 5 : 2 * count + 13]
    scratch = refs[2 * count + 13 :]
    near, wide, (in_sem, out_sem) = scratch[: count + 2], scratch[count + 2 : -2], scratch[-2:]
    sources = [result, input_grad, *grads]
    loads = [
        pltpu.make_async_copy(source, target, in_sem.at[index])
        for index, (source, target) in enumerate(zip(sources, near))
    ]
    held = [*near[:2], *wide]
    stores = [
        pltpu.make_async_copy(source, target, out_sem.at[index])
        for index, (source, target) in enumerate(zip(held, outs))
    ]
    for load in loads:
        load.start()
    inner = heads * HEAD_DIM
    values, units, gains, shifts, biases, scales, table, loss = small_outs
    values[...] = small[0, : 2 * inner]
    units[...] = small[1]
    gains[...] = small[2:4]
    shifts[...] = small[4:6]
    biases[...] = small[6:8]
    scales[...] = small[8:11]
    for head in range(heads):
        table[head : head + 1] = small[11:12, head * buckets : (head + 1) * buckets]
    loss[...] = small[12:13, 0:1]
    for index in range(2, count + 2):
        loads[index].wait()
        source, target = near[index], wide[index - 2]
        step = 48 if source.shape[0] % 64 else 64

        @pl.loop(0, source.shape[0] // step)
        def _(i):
            part = pl.ds(pl.multiple_of(i * step, step), step)
            target[part] = source[part].astype(F32)

        stores[index].start()
        if index < 4:
            loads[index - 2].wait()
            stores[index - 2].start()
    for store in stores:
        store.wait()


def finish_results(heads, buckets, small, result, input_grad, grads):
    inner = heads * HEAD_DIM
    anywhere = pl.BlockSpec(memory_space=pl.ANY)
    vector = pl.BlockSpec(memory_space=pltpu.VMEM)
    low = [jax.ShapeDtypeStruct(grad.shape, F32) for grad in grads]
    rows = ((2 * inner,), (WIDTH,), (2, WIDTH), (2, WIDTH), (2, WIDTH), (3, WIDTH), (heads, buckets), (1, 1))
    out_shape = [
        jax.ShapeDtypeStruct(result.shape, BF16), jax.ShapeDtypeStruct(input_grad.shape, F32), *low,
        *(jax.ShapeDtypeStruct(shape, F32) for shape in rows)]
    count = len(grads) + 2
    sources = [result, input_grad, *grads]
    return pl.pallas_call(
        partial(finish_kernel, heads, buckets),
        out_shape=out_shape,
        in_specs=[vector] + [anywhere] * count,
        out_specs=[anywhere] * count + [vector] * len(rows),
        scratch_shapes=[pltpu.VMEM(x.shape, x.dtype) for x in sources]
        + [pltpu.VMEM(x.shape, F32) for x in grads]
        + [pltpu.SemaphoreType.DMA((count,)), pltpu.SemaphoreType.DMA((count,))],
        compiler_params=pltpu.CompilerParams(vmem_limit_bytes=63 * 2**20),
    )(small, *sources)


def local(
    batch,
    hidden,
    cotangent,
    qkv_weight,
    proj_weight,
    up_weight,
    down_weight,
    query_value_bias,
    unit_bias,
    layer_gain,
    layer_shift,
    output_bias,
    scale_gain,
    position_bias,
    cross_query,
    cross_key_value,
    cross_proj,
    encodings,
    query_vectors,
    passage_lengths,
    target_lengths,
):
    heads = proj_weight.shape[1] // HEAD_DIM
    buckets = position_bias.shape[1]
    inner = heads * HEAD_DIM
    far = dict(
        hidden=hidden, cotangent=cotangent, qkv_weight=qkv_weight[0].T, proj_weight=proj_weight,
        up_weight=up_weight, down_weight=down_weight, cross_query=cross_query.T,
        cross_key_value=cross_key_value, cross_proj=cross_proj, encodings=encodings)
    near = dict(
        biases=jnp.concatenate([query_value_bias, unit_bias]).reshape(1, -1),
        layer_gain=layer_gain, layer_shift=layer_shift, output_bias=output_bias,
        scale_gain=scale_gain, query_vectors=query_vectors, position_bias=position_bias)
    scalars = dict(
        passage_lengths=passage_lengths, target_lengths=target_lengths)
    anywhere = pl.BlockSpec(memory_space=pl.ANY)
    vector = pl.BlockSpec(memory_space=pltpu.VMEM)
    scalar = pl.BlockSpec(memory_space=pltpu.SMEM)
    out_shapes = dict(
        small_out=jax.ShapeDtypeStruct((16, WIDTH), F32),
        y=jax.ShapeDtypeStruct((SEQ, WIDTH), BF16),
        gin=jax.ShapeDtypeStruct((SEQ, WIDTH), F32))
    for name, shape in weight_shapes(heads).items():
        out_shapes[name] = jax.ShapeDtypeStruct(shape, BF16)
    shapes = scratch_shapes(heads)
    names = [*far, *near, *scalars, *out_shapes, *shapes]
    small, result, input_grad, *grads = pl.pallas_call(
        partial(layer_kernel, heads, buckets, names),
        out_shape=list(out_shapes.values()),
        in_specs=[anywhere] * len(far) + [vector] * len(near) + [scalar] * len(scalars),
        out_specs=[vector] + [anywhere] * (len(out_shapes) - 1),
        scratch_shapes=list(shapes.values()),
        compiler_params=pltpu.CompilerParams(
            collective_id=0, has_side_effects=True, vmem_limit_bytes=63 * 2**20),
    )(*far.values(), *near.values(), *scalars.values())
    if batch > 4:
        groups = [[first + step for step in range(0, batch, 4)] for first in range(4)]
        grads = [grad.astype(F32) for grad in grads]
        grads, rows = lax.psum((grads, small[:12]), BATCH, axis_index_groups=groups)
        small_rows = (
            rows[0, : 2 * inner], rows[1], rows[2:4], rows[4:6], rows[6:8], rows[8:11],
            rows[11, : heads * buckets].reshape(heads, buckets), small[12, :1])
    else:
        result, input_grad, *rest = finish_results(heads, buckets, small, result, input_grad, grads)
        grads, small_rows = rest[: len(WEIGHTS)], rest[len(WEIGHTS) :]
    up, down, qkv, proj, cq, ckv, cproj = grads
    values, units, gains, shifts, biases, scales, table, loss = small_rows
    return (
        result[None],
        input_grad[None],
        qkv.T[None],
        proj[None],
        up[None],
        down[None],
        values,
        units,
        gains,
        shifts,
        biases,
        scales,
        table,
        cq.T,
        ckv,
        cproj,
        loss.reshape(-1),
    )


def solution(mesh):
    rows = P(STREAM, BATCH, None)
    columns_split = P(STREAM, None, TENSOR)
    rows_split = P(STREAM, TENSOR, None)
    weights = (columns_split, rows_split, columns_split, rows_split)
    cross = (P(None, TENSOR), P(None, TENSOR), P(TENSOR, None))
    vectors = (P(TENSOR), P(TENSOR), P(), P(), P(), P(), P(TENSOR, None))
    in_specs = (rows, rows, *weights, *vectors, *cross)
    in_specs = (*in_specs, P(BATCH, None, None), P(BATCH, None), P(BATCH, None), P(BATCH))
    out_specs = (rows, rows, *weights, *vectors, *cross, P(BATCH))
    return jax.shard_map(
        partial(local, mesh.shape[BATCH]), mesh=mesh, in_specs=in_specs, out_specs=out_specs,
        check_vma=False)
```

```python
from functools import partial

import jax
import jax.numpy as jnp
import numpy as np
from jax import lax
from jax.experimental import pallas as pl
from jax.experimental.pallas import tpu as pltpu
from jax.sharding import PartitionSpec as P

HEADS = 12
HEAD_DIM = 64
PLEN = 384
NPASS = 2
SEQ = 768
WIDTH = 768
HALF = 384
THIRD = 256
PIECE = 64
PIECES = SEQ // PIECE
AHEAD = 3
LANES = 128

EPS = 1e-06
NEG = -1000000000.0
MESH = pl.DeviceIdType.MESH
BF16 = jnp.bfloat16
F32 = jnp.float32

NN = (((1,), (0,)), ((), ()))
NT = (((1,), (1,)), ((), ()))
TN = (((0,), (0,)), ((), ()))

STREAM, BATCH, TENSOR = "stream", "batch", "tensor"
UP, DOWN, QKV, PROJ, CQ, CKV, CPROJ = "up", "down", "qkv", "proj", "cq", "ckv", "cproj"
WEIGHTS = (UP, DOWN, QKV, PROJ, CQ, CKV, CPROJ)


def bucket_starts(length, buckets):
    exact = buckets // 2
    distance = np.arange(length)
    far_bucket = exact + (
        np.log(np.maximum(distance, 1) / exact) / np.log(128.0 / exact) * (buckets - exact)
    ).astype(np.int64)
    near_table = np.where(distance < exact, distance, np.minimum(far_bucket, buckets - 1))
    return [int(np.argmax(near_table == bucket)) for bucket in range(buckets)]


def dot(left, right, dims):
    return lax.dot_general(left, right, dims, preferred_element_type=F32)


def fold(values):
    return jnp.sum(values.reshape(values.shape[0] // 8, 8, values.shape[1]), axis=0)


def mean(values):
    return jnp.mean(values, axis=-1, keepdims=True)


def weight_shapes(heads):
    inner = heads * HEAD_DIM
    return dict(
        up=(WIDTH, WIDTH),
        down=(WIDTH, WIDTH),
        qkv=(3 * inner, WIDTH),
        proj=(inner, WIDTH),
        cq=(inner, WIDTH),
        ckv=(WIDTH, 2 * inner),
        cproj=(inner, WIDTH),
    )


def scratch_shapes(heads):
    inner = heads * HEAD_DIM

    def low(*shape):
        return pltpu.VMEM(shape, BF16)

    def full(*shape):
        return pltpu.VMEM(shape, F32)

    whole = low(SEQ, WIDTH)
    head_rows = low(heads, SEQ, LANES)
    head_sums = full(heads, SEQ, LANES)
    scores = low(heads, SEQ, SEQ)
    bands = full(heads, 2 * LANES, LANES)
    room = low(3, SEQ, WIDTH)
    line = pltpu.SemaphoreType.DMA((3, 6, PIECES))
    shapes = dict(
        hid=whole, cot=whole, encb=whole, buf_a=whole, buf_b=whole, buf_c=whole, buf_u=whole,
        act=whole, dpre=whole, ag=whole, ybuf=whole,
        h1f=full(SEQ, WIDTH), h2f=full(SEQ, WIDTH),
        qa=head_rows, ka=head_rows, va=head_rows, cqa=head_rows, cka=head_rows, cva=head_rows,
        dk=head_sums, dv=head_sums, e1=scores, e2=scores,
        o1=low(inner, SEQ), o2=low(inner, SEQ), dot_in=low(inner, HALF),
        linv1=full(heads, 8, SEQ), linv2=full(heads, 8, SEQ),
        pkb=low(SEQ, 3 * inner), cqb=low(SEQ, inner), ckb=low(SEQ, 2 * inner),
        tall=full(SEQ, HALF), tall_low=low(SEQ, THIRD), wide=full(THIRD, WIDTH),
        band=bands, band_grad=bands, params=full(16, WIDTH), acc=full(10, 8, WIDTH),
        colsum=full(8, 3 * inner), mass_rows=full(8, HALF),
        small=full(16, WIDTH), small_got=full(8, 16, WIDTH), mass=full(8, LANES),
        mass_got=full(4, 8, LANES), part=room, outer=room, total=room,
        in_sem=pltpu.SemaphoreType.DMA((10,)), line_send=line, line_recv=line,
        w_send=pltpu.SemaphoreType.DMA((7, 6)), w_recv=pltpu.SemaphoreType.DMA((7, 5)),
        small_send=pltpu.SemaphoreType.DMA((7,)), small_recv=pltpu.SemaphoreType.DMA((8,)),
        mass_send=pltpu.SemaphoreType.DMA((4,)), mass_recv=pltpu.SemaphoreType.DMA((4,)),
        out_sem=pltpu.SemaphoreType.DMA((2, 3)),
        over_send=pltpu.SemaphoreType.DMA((2, 3)), over_recv=pltpu.SemaphoreType.DMA((2, 3)),
    )
    for name, shape in weight_shapes(heads).items():
        half = (shape[0] // 2, shape[1])
        shapes["w_" + name] = low(*shape)
        shapes["d_" + name] = low(*shape)
        shapes["rc_" + name] = low(*half)
        shapes["ry_" + name] = low(*half)
    return shapes


class Refs:
    pass


def layer_kernel(heads, buckets, names, *refs):
    r = Refs()
    for name, ref in zip(names, refs):
        setattr(r, name, ref)
    stream, query, place = (lax.axis_index(name) for name in (STREAM, BATCH, TENSOR))
    is_reader = stream == 1
    is_end = (place == 0) | (place == 3)
    is_middle = jnp.logical_not(is_end)
    inner_place = jnp.where(place == 0, 1, jnp.where(place == 3, 2, 3 - place))
    outer_place = jnp.where(place == 1, 0, 3)
    core = lax.rem(query, 2)
    group = query - lax.rem(query, 4)
    member = lax.rem(query, 4)

    def other(steps):
        return group + lax.rem(member + steps, 4)

    mate = query + 1 - 2 * core
    across_y = group + lax.rem(member + 2, 4)

    barrier = pltpu.get_barrier_semaphore()

    def greet(device):
        pl.semaphore_signal(barrier, inc=1, device_id=device, device_id_type=MESH)

    for steps in range(1, 4):
        greet((stream, other(steps), place))
    for steps in range(4):
        greet((1 - stream, other(steps), place))
    for steps in range(1, 4):
        greet((1 - stream, query, lax.rem(place + steps, 4)))
    greet((stream, query, inner_place))

    @pl.when(is_middle)
    def _():
        greet((stream, query, outer_place))

    def meet():
        @pl.when(is_end)
        def _():
            pl.semaphore_wait(barrier, 11)

        @pl.when(is_middle)
        def _():
            pl.semaphore_wait(barrier, 12)

    def bring(index, source, target):
        return pltpu.make_async_copy(source, target, r.in_sem.at[index])

    inputs = Refs()
    inputs.hid = bring(0, r.hidden.at[0], r.hid)
    inputs.qkv = bring(1, r.qkv_weight, r.w_qkv)
    inputs.proj = bring(2, r.proj_weight.at[0], r.w_proj)
    inputs.enc = bring(3, r.encodings.at[0], r.h2f)
    inputs.ckv = bring(4, r.cross_key_value, r.w_ckv)
    inputs.cq = bring(5, r.cross_query, r.w_cq)
    inputs.cproj = bring(6, r.cross_proj, r.w_cproj)
    inputs.up = bring(7, r.up_weight.at[0], r.w_up)
    inputs.down = bring(8, r.down_weight.at[0], r.w_down)
    inputs.cot = bring(9, r.cotangent.at[0], r.cot)

    def piece_rows(piece):
        return pl.ds(piece * PIECE, PIECE)

    side = Refs()

    def chunk_rows(chunk):
        return pl.ds(chunk * side.size, side.size)

    def row_loop(chunk, body):
        @pl.loop(0, side.size // LANES)
        def _(step):
            body(pl.ds(pl.multiple_of(chunk * side.size + step * LANES, LANES), LANES),
                 pl.ds(pl.multiple_of(step * LANES, LANES), LANES))

    def to_middle(line, room, piece):
        rows = piece_rows(piece)
        return pltpu.make_async_remote_copy(
            r.part.at[room, rows], r.outer.at[room, rows],
            r.line_send.at[0, line, piece], r.line_recv.at[0, line, piece],
            device_id=(stream, query, inner_place), device_id_type=MESH)

    def across(line, room, piece):
        rows = piece_rows(piece)
        return pltpu.make_async_remote_copy(
            r.outer.at[room, rows], r.total.at[room, rows],
            r.line_send.at[1, line, piece], r.line_recv.at[1, line, piece],
            device_id=(stream, query, inner_place), device_id_type=MESH)

    def to_end(line, room, piece):
        rows = piece_rows(piece)
        return pltpu.make_async_remote_copy(
            r.total.at[room, rows], r.total.at[room, rows],
            r.line_send.at[2, line, piece], r.line_recv.at[2, line, piece],
            device_id=(stream, query, outer_place), device_id_type=MESH)

    made, added, summed = [], [], []

    def chunk_pieces(chunk):
        count = side.size // PIECE
        return range(chunk * count, (chunk + 1) * count)

    def produce(line, room, pieces):
        @pl.when(is_end)
        def _():
            for piece in pieces:
                to_middle(line, room, piece).start()

        made.extend((line, room, piece) for piece in pieces)

    def add_outer(line, room, piece):
        rows = piece_rows(piece)
        to_middle(line, room, piece).wait_recv()
        r.outer[room, rows] += r.part[room, rows]
        across(line, room, piece).start()

    def add_inner(line, room, piece):
        rows = piece_rows(piece)
        across(line, room, piece).wait_recv()
        r.total[room, rows] += r.outer[room, rows]
        to_end(line, room, piece).start()

    def advance():
        if len(added) < len(made) and len(added) - len(summed) < AHEAD:
            item = made[len(added)]
            added.append(item)
            add_outer(*item)
        else:
            item = made[len(summed)]
            summed.append(item)
            add_inner(*item)

    def pump(count=1):
        steps = min(2 * count, 2 * len(made) - len(added) - len(summed))
        if steps > 0:
            @pl.when(is_middle)
            def _():
                for _ in range(steps):
                    advance()

    def finish(line, room, pieces):
        last = max(made.index((line, room, piece)) for piece in pieces)

        @pl.when(is_middle)
        def _():
            while len(summed) <= last:
                advance()

        @pl.when(is_end)
        def _():
            for piece in pieces:
                to_end(line, room, piece).wait_recv()
                to_middle(line, room, piece).wait_send()

    def settle(line, room, pieces):
        @pl.when(is_middle)
        def _():
            for piece in pieces:
                across(line, room, piece).wait_send()
                to_end(line, room, piece).wait_send()

    def hand_on(line, room, chunk, before=None):
        pieces = chunk_pieces(chunk)
        if before:
            settle(*before, pieces)
        produce(line, room, pieces)

    def collect(line, room, chunk):
        finish(line, room, chunk_pieces(chunk))

    def hand_over(chunk):
        rows = pl.ds(chunk * THIRD, THIRD)
        return pltpu.make_async_remote_copy(
            r.part.at[2, rows], r.part.at[2, rows], r.over_send.at[0, chunk], r.over_recv.at[0, chunk],
            device_id=(1 - stream, query, place), device_id_type=MESH)

    def hand_back(chunk):
        rows = pl.ds(chunk * THIRD, THIRD)
        return pltpu.make_async_remote_copy(
            r.total.at[2, rows], r.total.at[2, rows], r.over_send.at[1, chunk], r.over_recv.at[1, chunk],
            device_id=(1 - stream, query, place), device_id_type=MESH)

    def third_pieces(chunk):
        count = THIRD // PIECE
        return range(chunk * count, (chunk + 1) * count)

    def w_copy(source, target, index, send, recv, device):
        return pltpu.make_async_remote_copy(
            source, target, r.w_send.at[index, send], r.w_recv.at[index, recv],
            device_id=device, device_id_type=MESH)

    def w_parts(name):
        grad = getattr(r, "d_" + name)
        half = grad.shape[0] // 2
        mine = pl.ds(pl.multiple_of(core * half, half), half)
        theirs = pl.ds(pl.multiple_of((1 - core) * half, half), half)
        return WEIGHTS.index(name), grad, getattr(r, "rc_" + name), getattr(r, "ry_" + name), mine, theirs

    def w_first(name):
        index, grad, rc, ry, mine, theirs = w_parts(name)
        return w_copy(grad.at[theirs], rc, index, 0, 0, (stream, mate, place))

    def w_second(name):
        index, grad, rc, ry, mine, theirs = w_parts(name)
        return w_copy(rc, ry, index, 1, 1, (stream, across_y, place))

    def w_third(name):
        index, grad, rc, ry, mine, theirs = w_parts(name)
        out = getattr(r, name)
        return w_copy(grad.at[mine], out.at[mine], index, 2, 2, (stream, mate, place))

    def w_local(name):
        index, grad, rc, ry, mine, theirs = w_parts(name)
        return pltpu.make_async_copy(grad.at[mine], getattr(r, name).at[mine], r.w_send.at[index, 3])

    def w_other_side(name):
        index, grad, rc, ry, mine, theirs = w_parts(name)
        out = getattr(r, name)
        return w_copy(grad.at[mine], out.at[mine], index, 4, 3, (1 - stream, query, place))

    def w_forward(name):
        index, grad, rc, ry, mine, theirs = w_parts(name)
        out = getattr(r, name)
        return w_copy(out.at[mine], out.at[mine], index, 5, 4, (stream, mate, place))

    def w_start(name):
        w_first(name).start()

    def w_combine(name):
        index, grad, rc, ry, mine, theirs = w_parts(name)
        w_first(name).wait_recv()
        step = 48 if rc.shape[0] % 64 else 64

        @pl.loop(0, rc.shape[0] // step)
        def _(i):
            rows = pl.ds(pl.multiple_of(i * step, step), step)
            own = pl.ds(pl.multiple_of(core * rc.shape[0] + i * step, step), step)
            rc[rows] += grad[own]

        w_second(name).start()

    def w_store(name):
        index, grad, rc, ry, mine, theirs = w_parts(name)
        w_second(name).wait_recv()
        step = 48 if rc.shape[0] % 64 else 64

        @pl.loop(0, rc.shape[0] // step)
        def _(i):
            rows = pl.ds(pl.multiple_of(i * step, step), step)
            own = pl.ds(pl.multiple_of(core * rc.shape[0] + i * step, step), step)
            grad[own] = ry[rows] + rc[rows]

        w_third(name).start()
        w_local(name).start()
        if name in (CQ, CKV, CPROJ):
            w_other_side(name).start()

    def w_end(name):
        w_first(name).wait_send()
        w_second(name).wait_send()
        w_third(name).wait()
        w_local(name).wait()
        if name in (CQ, CKV, CPROJ):
            w_other_side(name).wait_send()

    def softmax(exp_ref, head, chunk, first_key, keys, banded):
        sums = []
        for tile in range(side.size // LANES):
            cols = pl.ds(tile * LANES, LANES)
            rows = pl.ds(chunk * side.size + tile * LANES, LANES)
            end = chunk * side.size + (tile + 1) * LANES if banded else keys
            if banded:
                near = min(end, 2 * LANES)
                r.tall[pl.ds(end - near, near), cols] += r.band[head, pl.ds(2 * LANES - near, near)]
            top = jnp.max(r.tall[pl.ds(0, end), cols], axis=0, keepdims=True)
            parts = [jnp.zeros((1, LANES), F32), jnp.zeros((1, LANES), F32)]
            for key in range(0, end, LANES):
                grown = jnp.exp(r.tall[pl.ds(key, LANES), cols] - top)
                exp_ref[head, pl.ds(first_key + key, LANES), rows] = grown.astype(BF16)
                parts[key // HALF] += jnp.sum(grown, axis=0, keepdims=True)
            for key in range(end, keys, LANES):
                exp_ref[head, pl.ds(first_key + key, LANES), rows] = jnp.zeros((LANES, LANES), BF16)
            sums.append(parts)
        return [jnp.concatenate([parts[p] for parts in sums], axis=1) for p in range(2)]

    def head_rows(head):
        return pl.ds(pl.multiple_of(head * HEAD_DIM, HEAD_DIM), HEAD_DIM)

    def attend(qa, ka, va, exp_ref, out_ref, inv_ref, chunk, first_key, keys, banded, mass):
        rows = chunk_rows(chunk)
        span = pl.ds(first_key, keys)
        cols = pl.ds(0, side.size)
        live = lax.broadcasted_iota(jnp.int32, (1, side.size), 1) + chunk * side.size < r.target_lengths[0]

        @pl.loop(0, heads)
        def _(head):
            r.tall[pl.ds(0, keys), cols] = dot(ka[head, span], qa[head, rows], NT)
            parts = softmax(exp_ref, head, chunk, first_key, keys, banded)
            inverse = 1.0 / (parts[0] + parts[1])
            inv_ref[head, pl.ds(0, 1), rows] = inverse
            if mass:
                for p in range(NPASS):
                    r.mass_rows[pl.ds(p, 1), cols] += jnp.where(live, parts[p] * inverse, 0.0)
            mixed = dot(va[head, span, pl.ds(0, HEAD_DIM)], exp_ref[head, span, rows], TN)
            out_ref[head_rows(head), rows] = (mixed * inverse).astype(BF16)

    def attend_back(qa, ka, va, exp_ref, out_ref, chunk, first_key, keys, fresh, banded):
        rows = chunk_rows(chunk)
        span = pl.ds(first_key, keys)
        cols = pl.ds(0, side.size)
        low = pl.ds(0, HEAD_DIM)

        @pl.loop(0, heads)
        def _(head):
            lanes = head_rows(head)
            grad_out = r.dot_in[lanes, cols]
            spread = jnp.sum(
                grad_out.astype(F32) * out_ref[lanes, rows].astype(F32), axis=0, keepdims=True)
            weight = exp_ref[head, span, rows]
            score_grad = (
                weight.astype(F32) * (dot(va[head, span, low], grad_out, NN) - spread)).astype(BF16)
            if banded:
                r.tall_low[pl.ds(0, keys), cols] = score_grad
                for tile in range(side.size // LANES):
                    end = chunk * side.size + (tile + 1) * LANES
                    near = min(end, 2 * LANES)
                    r.band_grad[head, pl.ds(2 * LANES - near, near)] += (
                        r.tall_low[pl.ds(end - near, near), pl.ds(tile * LANES, LANES)].astype(F32))
            query_grad = dot(score_grad, ka[head, span], TN)
            key_grad = dot(score_grad, qa[head, rows], NN)
            value_grad = dot(weight, grad_out, NT)
            qa[head, rows, low] = (query_grad[:, :HEAD_DIM] * HEAD_DIM ** (-0.5)).astype(BF16)
            if fresh:
                r.dk[head, span] = key_grad
                r.dv[head, span, low] = value_grad
            else:
                r.dk[head, span] += key_grad
                r.dv[head, span, low] += value_grad

    def grad_of_mixed(weight, grad_ref, inv_ref, chunk):
        grads = dot(weight[...], grad_ref[chunk_rows(chunk)], NT)
        for head in range(heads):
            lanes = pl.ds(head * HEAD_DIM, HEAD_DIM)
            r.dot_in[lanes, pl.ds(0, side.size)] = (
                grads[head * HEAD_DIM:(head + 1) * HEAD_DIM] * inv_ref[head, pl.ds(0, 1), chunk_rows(chunk)]
            ).astype(BF16)

    def fill_tails(qa, ka, valid):
        shape = (SEQ, HEAD_DIM)
        lane = lax.broadcasted_iota(jnp.int32, shape, 1)
        key = lax.broadcasted_iota(jnp.int32, shape, 0)
        ones = jnp.where(lane == 0, 1.0, 0.0).astype(BF16)
        fence = jnp.where((lane == 0) & jnp.logical_not(valid(key)), NEG, 0.0).astype(BF16)
        for head in range(heads):
            qa[head, :, pl.ds(HEAD_DIM, HEAD_DIM)] = ones
            ka[head, :, pl.ds(HEAD_DIM, HEAD_DIM)] = fence

    def in_passage(key):
        low = (key < HALF) & (key < r.passage_lengths[0, 0])
        return low | ((key >= HALF) & (key - HALF < r.passage_lengths[0, 1]))

    def in_target(key):
        return key < r.target_lengths[0]

    def split_packed(rows):
        for head in range(heads):
            base = 3 * HEAD_DIM * head
            low = pl.ds(0, HEAD_DIM)
            r.qa[head, rows, low] = (
                r.pkb[rows, pl.ds(base, HEAD_DIM)].astype(F32) * HEAD_DIM ** (-0.5)).astype(BF16)
            r.ka[head, rows, low] = r.pkb[rows, pl.ds(base + HEAD_DIM, HEAD_DIM)]
            r.va[head, rows, low] = r.pkb[rows, pl.ds(base + 2 * HEAD_DIM, HEAD_DIM)]

    def project_out(line, room, chunk, out_ref, weight, before=None):
        for tile in range(side.size // LANES):
            rows = pl.ds(chunk * side.size + tile * LANES, LANES)
            r.part[room, rows] = dot(out_ref[:, rows], weight[...], TN).astype(BF16)
        hand_on(line, room, chunk, before)

    def param(row):
        return r.params[pl.ds(row, 1)]

    def add_to(slot, values):
        r.acc[slot] += fold(values)

    def gelu_parts(values):
        cubic = 0.7978845608028654 * (values + 0.044715 * values * values * values)
        bend = jnp.tanh(cubic)
        slope = 0.7978845608028654 * (1.0 + 3.0 * 0.044715 * values * values)
        return 0.5 * values * (1.0 + bend), 0.5 * (1.0 + bend) + 0.5 * values * (1.0 - bend * bend) * slope

    def pack_grads(chunk):
        rows = chunk_rows(chunk)
        for head in range(heads):
            base = 3 * HEAD_DIM * head
            low = pl.ds(0, HEAD_DIM)
            r.pkb[rows, pl.ds(base, HEAD_DIM)] = r.qa[head, rows, low]
            r.pkb[rows, pl.ds(base + HEAD_DIM, HEAD_DIM)] = r.dk[head, rows, low].astype(BF16)
            r.pkb[rows, pl.ds(base + 2 * HEAD_DIM, HEAD_DIM)] = r.dv[head, rows, low].astype(BF16)

    def input_part(line, room, chunk, before):
        rows = chunk_rows(chunk)
        r.part[room, rows] = dot(r.pkb[rows], r.w_qkv[...], NN).astype(BF16)
        hand_on(line, room, chunk, before)

    def weight_grad(target, left, right):
        @pl.loop(0, left.shape[1] // THIRD)
        def _(step):
            rows = pl.ds(pl.multiple_of(step * THIRD, THIRD), THIRD)
            target[rows] = dot(left[:, rows], right[...], TN).astype(BF16)

    def third_loop(body):
        @pl.loop(0, SEQ // THIRD)
        def _(step):
            body(pl.ds(pl.multiple_of(step * THIRD, THIRD), THIRD))

    def clear():
        r.acc[...] = jnp.zeros_like(r.acc)
        r.small[...] = jnp.zeros_like(r.small)

    def store_input_grad(chunk):
        rows = chunk_rows(chunk)
        return pltpu.make_async_copy(r.ag.at[rows], r.gin.at[rows], r.out_sem.at[0, chunk])

    def store_result(chunk):
        rows = chunk_rows(chunk)
        return pltpu.make_async_copy(r.ybuf.at[rows], r.y.at[rows], r.out_sem.at[1, chunk])

    def small_copies():
        copies = []
        for side_step in range(2):
            for steps in range(4):
                if side_step == 0 and steps == 0:
                    continue
                device = (lax.rem(stream + side_step, 2), other(steps), place)
                copies.append(pltpu.make_async_remote_copy(
                    r.small, r.small_got.at[stream * 4 + member], r.small_send.at[len(copies)],
                    r.small_recv.at[stream * 4 + member], device_id=device, device_id_type=MESH))
        return copies

    def start_small():
        for copy in small_copies():
            copy.start()
        r.small_got[stream * 4 + member] = r.small[...]

    def end_small():
        for side_step in range(2):
            for steps in range(4):
                if side_step == 0 and steps == 0:
                    continue
                source = lax.rem(stream + side_step, 2) * 4 + lax.rem(member + steps, 4)
                pltpu.make_async_remote_copy(
                    r.small, r.small_got.at[source], r.small_send.at[0], r.small_recv.at[source],
                    device_id=(stream, mate, place), device_id_type=MESH).wait_recv()
        for copy in small_copies():
            copy.wait_send()
        total = r.small_got[0]
        for index in range(1, 8):
            total = total + r.small_got[index]
        loss = r.small_got[member, pl.ds(12, 1)]
        r.small_out[...] = total
        r.small_out[pl.ds(12, 1)] = loss

    def reader():
        side.size = THIRD
        order = (2, 1, 0)
        inputs.hid.start()
        inputs.qkv.start()
        r.params[pl.ds(8, 3)] = r.scale_gain[...].astype(F32)
        starts = bucket_starts(SEQ, buckets)
        shape = (2 * LANES, LANES)
        apart = (
            lax.broadcasted_iota(jnp.int32, shape, 1) + LANES - lax.broadcasted_iota(jnp.int32, shape, 0))
        shifts = r.position_bias[...].astype(F32)
        shifts = shifts - shifts[:, buckets - 1:]
        for head in range(heads):
            band = jnp.broadcast_to(shifts[head:head + 1, 0:1], shape)
            for bucket in range(1, buckets):
                band = jnp.where(apart >= starts[bucket], shifts[head:head + 1, bucket:bucket + 1], band)
            r.band[head] = jnp.where(apart >= 0, band, NEG)
        fill_tails(r.qa, r.ka, in_target)

        inputs.hid.wait()
        for copy in (inputs.proj, inputs.enc, inputs.ckv, inputs.cq, inputs.cproj):
            copy.start()
        for copy in (inputs.up, inputs.down, inputs.cot):
            copy.start()
        gain = param(8)

        def normalize(rows):
            values = r.hid[rows].astype(F32)
            r.buf_a[rows] = (values * lax.rsqrt(mean(values * values) + EPS) * gain).astype(BF16)
        third_loop(normalize)
        inputs.qkv.wait()

        def project(rows):
            r.pkb[rows] = dot(r.buf_a[rows], r.w_qkv[...], NT).astype(BF16)
            split_packed(rows)
        third_loop(project)
        inputs.proj.wait()
        for chunk in order:
            attend(
                r.qa, r.ka, r.va, r.e1, r.o1, r.linv1, chunk, 0, (chunk + 1) * THIRD, True, False)
            if chunk == order[-1]:
                pump()
            if chunk == order[0]:
                meet()
            project_out(0, 0, chunk, r.o1, r.w_proj)

        clear()
        r.mass_rows[...] = jnp.zeros_like(r.mass_rows)
        r.band_grad[...] = jnp.zeros_like(r.band_grad)
        fill_tails(r.cqa, r.cka, in_passage)

        inputs.enc.wait()
        inputs.ckv.wait()
        pump()

        def encode(rows):
            r.encb[rows] = r.h2f[rows].astype(BF16)
            r.ckb[rows] = dot(r.encb[rows], r.w_ckv[...], NN).astype(BF16)
            for head in range(heads):
                low = pl.ds(0, HEAD_DIM)
                r.cka[head, rows, low] = r.ckb[rows, pl.ds(2 * HEAD_DIM * head, HEAD_DIM)]
                r.cva[head, rows, low] = r.ckb[rows, pl.ds(2 * HEAD_DIM * head + HEAD_DIM, HEAD_DIM)]
        third_loop(encode)
        pump()
        inputs.down.wait()
        inputs.cot.wait()

        def act_grad(rows):
            r.buf_c[rows] = dot(r.cot[rows], r.w_down[...], NT).astype(BF16)
        third_loop(act_grad)
        inputs.cq.wait()
        inputs.cproj.wait()
        inputs.up.wait()

        gain = param(9)
        for chunk in order:
            rows = chunk_rows(chunk)
            collect(0, 0, chunk)

            def first_sum(rows, _):
                values = r.hid[rows].astype(F32) + r.total[0, rows].astype(F32)
                r.h1f[rows] = values
                r.buf_b[rows] = (values * lax.rsqrt(mean(values * values) + EPS) * gain).astype(BF16)
            row_loop(chunk, first_sum)
            r.cqb[rows] = dot(r.buf_b[rows], r.w_cq[...], NT).astype(BF16)
            for head in range(heads):
                r.cqa[head, rows, pl.ds(0, HEAD_DIM)] = (
                    r.cqb[rows, pl.ds(head * HEAD_DIM, HEAD_DIM)].astype(F32) * HEAD_DIM ** (-0.5)
                ).astype(BF16)
            pump()
            attend(r.cqa, r.cka, r.cva, r.e2, r.o2, r.linv2, chunk, 0, SEQ, False, True)
            pump()
            project_out(1, 1, chunk, r.o2, r.w_cproj, (0, 0))

        lane = lax.broadcasted_iota(jnp.int32, (8, LANES), 1)
        masses = [jnp.sum(r.mass_rows[pl.ds(p, 1)], axis=1, keepdims=True) for p in range(NPASS)]
        r.mass[...] = jnp.where(lane == 0, masses[0], jnp.where(lane == 1, masses[1], 0.0))

        def mass_copy(steps):
            return pltpu.make_async_remote_copy(
                r.mass, r.mass_got.at[place], r.mass_send.at[steps], r.mass_recv.at[place],
                device_id=(1 - stream, query, lax.rem(place + steps, 4)), device_id_type=MESH)

        for steps in range(4):
            mass_copy(steps).start()

        gain = param(10)
        for chunk in order:
            rows = chunk_rows(chunk)
            collect(1, 1, chunk)

            def second_sum(rows, _):
                values = r.h1f[rows] + r.total[1, rows].astype(F32)
                r.h2f[rows] = values
                r.ybuf[rows] = values.astype(BF16)
                r.buf_u[rows] = (values * lax.rsqrt(mean(values * values) + EPS) * gain).astype(BF16)
            row_loop(chunk, second_sum)
            r.wide[pl.ds(0, side.size)] = dot(r.buf_u[rows], r.w_up[...], NN)
            pump()

            def bend(rows, local):
                value, slope = gelu_parts(r.wide[local])
                r.act[rows] = value.astype(BF16)
                r.dpre[rows] = (r.buf_c[rows].astype(F32) * slope).astype(BF16)
            row_loop(chunk, bend)
            pump()
            r.part[0, rows] = dot(r.dpre[rows], r.w_up[...], NT).astype(BF16)
            hand_on(2, 0, chunk, (1, 1))
            r.part[2, rows] = dot(r.act[rows], r.w_down[...], NN).astype(BF16)
            if chunk != order[-1]:
                hand_over(chunk).start()

        weight_grad(r.d_up, r.buf_u, r.dpre)
        w_start(UP)
        pump()
        weight_grad(r.d_down, r.act, r.cot)
        w_start(DOWN)
        pump()

        for chunk in order:
            rows = chunk_rows(chunk)
            collect(2, 0, chunk)
            if chunk == order[0]:
                w_combine(UP)
                w_combine(DOWN)

            def second_grad(rows, _):
                values = r.h2f[rows]
                grads = r.total[0, rows].astype(F32)
                root = lax.rsqrt(mean(values * values) + EPS)
                add_to(2, grads * values * root)
                scaled = grads * gain
                back = root * scaled - values * (root * root * root) * mean(scaled * values)
                result = r.cot[rows].astype(F32) + back
                r.h2f[rows] = result
                r.buf_c[rows] = result.astype(BF16)
            row_loop(chunk, second_grad)
            grad_of_mixed(r.w_cproj, r.buf_c, r.linv2, chunk)
            pump()
            attend_back(r.cqa, r.cka, r.cva, r.e2, r.o2, chunk, 0, SEQ, chunk == order[0], False)
            pump()
            for head in range(heads):
                r.cqb[rows, pl.ds(head * HEAD_DIM, HEAD_DIM)] = r.cqa[head, rows, pl.ds(0, HEAD_DIM)]
            r.part[1, rows] = dot(r.cqb[rows], r.w_cq[...], NN).astype(BF16)
            hand_on(3, 1, chunk, (2, 0))

        pump()
        for chunk in order:
            rows = chunk_rows(chunk)
            for head in range(heads):
                low = pl.ds(0, HEAD_DIM)
                r.ckb[rows, pl.ds(2 * HEAD_DIM * head, HEAD_DIM)] = r.dk[head, rows, low].astype(BF16)
                r.ckb[rows, pl.ds(2 * HEAD_DIM * head + HEAD_DIM, HEAD_DIM)] = (
                    r.dv[head, rows, low].astype(BF16))
        r.d_cproj[...] = dot(r.o2[...], r.buf_c[...], NN).astype(BF16)
        w_start(CPROJ)
        r.d_cq[...] = dot(r.cqb[...], r.buf_b[...], TN).astype(BF16)
        w_start(CQ)
        pump()
        weight_grad(r.d_ckv, r.encb, r.ckb)
        w_start(CKV)

        gain = param(9)
        for chunk in order:
            rows = chunk_rows(chunk)
            collect(3, 1, chunk)
            if chunk == order[0]:
                for name in (CPROJ, CQ, CKV):
                    w_combine(name)

            def first_grad(rows, _):
                values = r.h1f[rows]
                grads = r.total[1, rows].astype(F32)
                root = lax.rsqrt(mean(values * values) + EPS)
                add_to(1, grads * values * root)
                scaled = grads * gain
                back = root * scaled - values * (root * root * root) * mean(scaled * values)
                result = r.h2f[rows] + back
                r.h1f[rows] = result
                r.ag[rows] = result.astype(BF16)
            row_loop(chunk, first_grad)
            grad_of_mixed(r.w_proj, r.ag, r.linv1, chunk)
            pump()
            attend_back(
                r.qa, r.ka, r.va, r.e1, r.o1, chunk, 0, (chunk + 1) * THIRD, chunk == order[0], True)
            pump()
            pack_grads(chunk)
            input_part(4, 0, chunk, (3, 1))
            if chunk == order[1]:
                w_store(UP)
                w_store(DOWN)
        produce(5, 2, third_pieces(0))
        r.d_qkv[...] = dot(r.pkb[...], r.buf_a[...], TN).astype(BF16)
        w_start(QKV)
        r.d_proj[...] = dot(r.o1[...], r.ag[...], NN).astype(BF16)
        w_start(PROJ)
        for name in (CPROJ, CQ, CKV):
            w_store(name)
        w_combine(QKV)
        w_combine(PROJ)
        pump()

        lane = lax.broadcasted_iota(jnp.int32, (1, LANES), 1)
        table = jnp.zeros((1, LANES), F32)
        for head in range(heads):
            grads = r.band_grad[head]
            rest = jnp.sum(
                jnp.sum(r.dk[head], axis=0, keepdims=True)[:, HEAD_DIM:HEAD_DIM + 1], axis=1, keepdims=True)
            for bucket in range(buckets - 1):
                inside = (apart >= starts[bucket]) & (apart < starts[bucket + 1])
                value = jnp.sum(
                    jnp.sum(jnp.where(inside, grads, 0.0), axis=0, keepdims=True), axis=1, keepdims=True)
                rest = rest - value
                table = jnp.where(lane == head * buckets + bucket, value, table)
            table = jnp.where(lane == head * buckets + buckets - 1, rest, table)
        r.small[pl.ds(11, 1), pl.ds(0, LANES)] = table

        def last_sum(chunk):
            def add(rows, _):
                r.ybuf[rows] = (r.ybuf[rows].astype(F32) + r.total[2, rows].astype(F32)).astype(BF16)
            row_loop(chunk, add)
            store_result(chunk).start()

        gain = param(8)
        for chunk in order:
            if chunk != order[-1]:
                hand_back(chunk).wait_recv()
                last_sum(chunk)
            collect(4, 0, chunk)

            def input_grad(rows, _):
                values = r.hid[rows].astype(F32)
                grads = r.total[0, rows].astype(F32)
                root = lax.rsqrt(mean(values * values) + EPS)
                add_to(0, grads * values * root)
                scaled = grads * gain
                back = root * scaled - values * (root * root * root) * mean(scaled * values)
                r.ag[rows] = (r.h1f[rows] + back).astype(BF16)
            row_loop(chunk, input_grad)
            store_input_grad(chunk).start()

        for slot in range(3):
            r.small[pl.ds(8 + slot, 1)] = jnp.sum(r.acc[slot], axis=0, keepdims=True)
        start_small()
        w_store(QKV)
        w_store(PROJ)
        collect(5, 2, 0)
        last_sum(0)
        end_small()
        settle(5, 2, third_pieces(0))
        for chunk in order:
            settle(4, 0, chunk_pieces(chunk))
            if chunk != order[-1]:
                hand_over(chunk).wait_send()
            store_input_grad(chunk).wait()
            store_result(chunk).wait()
        for name in WEIGHTS:
            w_end(name)
        for steps in range(4):
            mass_copy(steps).wait_send()

    def retriever():
        side.size = HALF
        order = (1, 0)
        inputs.hid.start()
        inputs.qkv.start()
        r.params[pl.ds(0, 2)] = r.layer_gain[...].astype(F32)
        r.params[pl.ds(2, 2)] = r.layer_shift[...].astype(F32)
        r.params[pl.ds(4, 2)] = r.output_bias[...].astype(F32)
        r.params[pl.ds(6, 1)] = r.biases[:, pl.ds(2 * heads * HEAD_DIM, WIDTH)].astype(F32)
        r.colsum[...] = jnp.zeros_like(r.colsum)
        r.params[pl.ds(11, 1), pl.ds(0, 2 * heads * HEAD_DIM)] = (
            r.biases[:, pl.ds(0, 2 * heads * HEAD_DIM)].astype(F32))
        for head in range(heads):
            base = 3 * HEAD_DIM * head
            for k in range(2):
                r.colsum[pl.ds(0, 1), pl.ds(base + 2 * k * HEAD_DIM, HEAD_DIM)] = (
                    r.params[pl.ds(11, 1), pl.ds((2 * head + k) * HEAD_DIM, HEAD_DIM)])
        shift = r.colsum[pl.ds(0, 1)]
        fill_tails(r.qa, r.ka, in_passage)
        inputs.hid.wait()
        for copy in (inputs.proj, inputs.up, inputs.down, inputs.cot):
            copy.start()
        inputs.qkv.wait()
        inputs.proj.wait()
        for chunk in order:
            rows = chunk_rows(chunk)
            r.pkb[rows] = (dot(r.hid[rows], r.w_qkv[...], NT) + shift).astype(BF16)
            split_packed(rows)
            attend(r.qa, r.ka, r.va, r.e1, r.o1, r.linv1, chunk, chunk * HALF, HALF, False, False)
            if chunk == order[0]:
                meet()
            project_out(0, 0, chunk, r.o1, r.w_proj)
        r.colsum[...] = jnp.zeros_like(r.colsum)
        clear()

        inputs.up.wait()
        inputs.down.wait()
        inputs.cot.wait()
        gain1, gain2 = param(0), param(1)
        shift1, shift2 = param(2), param(3)
        out1, out2, unit = param(4), param(5), param(6)
        side.size = THIRD
        thirds = (2, 1, 0)
        for chunk in thirds:
            rows = chunk_rows(chunk)
            collect(0, 0, chunk)

            def first_norm(rows, _):
                values = r.hid[rows].astype(F32) + r.total[0, rows].astype(F32) + out1
                centered = values - mean(values)
                root = lax.rsqrt(mean(centered * centered) + EPS)
                r.h1f[rows] = values
                r.buf_u[rows] = (centered * root * gain1 + shift1).astype(BF16)
            row_loop(chunk, first_norm)
            r.wide[pl.ds(0, THIRD)] = dot(r.buf_u[rows], r.w_up[...], NN)
            pump()

            def bend(rows, local):
                value, slope = gelu_parts(r.wide[local] + unit)
                r.act[rows] = value.astype(BF16)
                r.buf_a[rows] = slope.astype(BF16)
            row_loop(chunk, bend)
            pump()
            r.part[1, rows] = dot(r.act[rows], r.w_down[...], NN).astype(BF16)
            hand_on(1, 1, chunk, (0, 0))

        def valid(rows):
            token = lax.broadcasted_iota(jnp.int32, (LANES, 1), 0) + rows.start
            low = (token < HALF) & (token < r.passage_lengths[0, 0])
            return low, (token >= HALF) & (token - HALF < r.passage_lengths[0, 1])

        for chunk in thirds:
            collect(1, 1, chunk)

            def second_norm(rows, _):
                values = r.h1f[rows]
                centered = values - mean(values)
                root = lax.rsqrt(mean(centered * centered) + EPS)
                values = centered * root * gain1 + shift1 + r.total[1, rows].astype(F32) + out2
                r.h2f[rows] = values
                centered = values - mean(values)
                root = lax.rsqrt(mean(centered * centered) + EPS)
                result = centered * root * gain2 + shift2
                r.ybuf[rows] = result.astype(BF16)
                for p, token in enumerate(valid(rows)):
                    add_to(8 + p, jnp.where(token, result, 0.0))
            row_loop(chunk, second_norm)
            store_result(chunk).start()
            if chunk == 1:
                hand_over(2).wait_recv()
                produce(5, 2, third_pieces(2))

        vector = r.query_vectors[...]
        scores = [
            jnp.sum(jnp.sum(r.acc[8 + p], axis=0, keepdims=True) * vector, axis=1, keepdims=True)
            / r.passage_lengths[0, p].astype(F32)
            for p in range(NPASS)
        ]

        def mass_wait(source):
            return pltpu.make_async_remote_copy(
                r.mass, r.mass_got.at[source], r.mass_send.at[0], r.mass_recv.at[source],
                device_id=(1 - stream, query, place), device_id_type=MESH)

        for source in range(4):
            mass_wait(source).wait_recv()
        masses = r.mass_got[0].astype(BF16).astype(F32)
        for source in range(1, 4):
            masses = masses + r.mass_got[source].astype(BF16).astype(F32)
        scale = HEADS * r.target_lengths[0].astype(F32)
        targets = [masses[0:1, p:p + 1] / scale for p in range(NPASS)]
        top = jnp.maximum(scores[0], scores[1])
        norm = top + jnp.log(jnp.exp(scores[0] - top) + jnp.exp(scores[1] - top))
        logs = [score - norm for score in scores]
        loss = targets[0] * (jnp.log(targets[0]) - logs[0]) + targets[1] * (jnp.log(targets[1]) - logs[1])
        r.small[pl.ds(12, 1)] = jnp.broadcast_to(loss, (1, WIDTH))
        pulls = [
            (jnp.exp(logs[p]) * (targets[0] + targets[1]) - targets[p])
            / r.passage_lengths[0, p].astype(F32) * vector
            for p in range(NPASS)
        ]

        for chunk in thirds:
            rows = chunk_rows(chunk)

            def final_grad(rows, _):
                low, high = valid(rows)
                upstream = r.cot[rows].astype(F32) + jnp.where(
                    low, pulls[0], jnp.where(high, pulls[1], 0.0))
                values = r.h2f[rows]
                centered = values - mean(values)
                root = lax.rsqrt(mean(centered * centered) + EPS)
                normed = centered * root
                scaled = upstream * gain2
                result = root * (scaled - mean(scaled) - normed * mean(scaled * normed))
                add_to(1, upstream * normed)
                add_to(3, upstream)
                r.h2f[rows] = result
                low = result.astype(BF16)
                r.buf_b[rows] = low
                add_to(5, low.astype(F32))
            row_loop(chunk, final_grad)
            if chunk == 2:
                pump()
            r.wide[pl.ds(0, THIRD)] = dot(r.buf_b[rows], r.w_down[...], NT)
            if chunk == 2:
                pump()

            def bend_back(rows, local):
                low = (r.wide[local] * r.buf_a[rows].astype(F32)).astype(BF16)
                r.dpre[rows] = low
                add_to(6, low.astype(F32))
            row_loop(chunk, bend_back)
            pump()
            r.part[0, rows] = dot(r.dpre[rows], r.w_up[...], NT).astype(BF16)
            hand_on(2, 0, chunk, (1, 1))
        hand_over(1).wait_recv()
        produce(5, 2, third_pieces(1))

        weight_grad(r.d_up, r.buf_u, r.dpre)
        w_start(UP)
        pump()
        weight_grad(r.d_down, r.act, r.buf_b)
        w_start(DOWN)
        pump()
        finish(5, 2, third_pieces(2))
        hand_back(2).start()

        side.size = HALF
        for chunk in order:
            rows = chunk_rows(chunk)
            collect(2, 0, chunk)
            if chunk == order[0]:
                w_combine(UP)
                w_combine(DOWN)

            def middle_grad(rows, _):
                upstream = r.h2f[rows] + r.total[0, rows].astype(F32)
                values = r.h1f[rows]
                centered = values - mean(values)
                root = lax.rsqrt(mean(centered * centered) + EPS)
                normed = centered * root
                scaled = upstream * gain1
                result = root * (scaled - mean(scaled) - normed * mean(scaled * normed))
                add_to(0, upstream * normed)
                add_to(2, upstream)
                r.h1f[rows] = result
                low = result.astype(BF16)
                r.ag[rows] = low
                add_to(4, low.astype(F32))
            row_loop(chunk, middle_grad)
            grad_of_mixed(r.w_proj, r.ag, r.linv1, chunk)
            pump()
            attend_back(r.qa, r.ka, r.va, r.e1, r.o1, chunk, chunk * HALF, HALF, True, False)
            pump()
            pack_grads(chunk)
            input_part(4, 1, chunk, (2, 0))
            r.colsum[...] += fold(r.pkb[rows].astype(F32))
            if chunk == order[0]:
                finish(5, 2, third_pieces(1))
                hand_back(1).start()
        r.d_qkv[...] = dot(r.pkb[...], r.hid[...], TN).astype(BF16)
        w_start(QKV)
        r.d_proj[...] = dot(r.o1[...], r.ag[...], NN).astype(BF16)
        w_start(PROJ)
        pump()

        w_combine(QKV)
        w_combine(PROJ)
        for chunk in order:
            rows = chunk_rows(chunk)
            collect(4, 1, chunk)
            if chunk == order[0]:
                w_store(UP)
                w_store(DOWN)

            def input_grad(rows, _):
                r.ag[rows] = (r.h1f[rows] + r.total[1, rows].astype(F32)).astype(BF16)
            row_loop(chunk, input_grad)
            store_input_grad(chunk).start()

        columns = jnp.sum(r.colsum[...], axis=0, keepdims=True)
        r.colsum[pl.ds(0, 1)] = columns
        for head in range(heads):
            base = 3 * HEAD_DIM * head
            for k in range(2):
                r.small[pl.ds(0, 1), pl.ds((2 * head + k) * HEAD_DIM, HEAD_DIM)] = (
                    r.colsum[pl.ds(0, 1), pl.ds(base + 2 * k * HEAD_DIM, HEAD_DIM)])
        r.small[pl.ds(1, 1)] = jnp.sum(r.acc[6], axis=0, keepdims=True)
        for slot in range(6):
            r.small[pl.ds(2 + slot, 1)] = jnp.sum(r.acc[slot], axis=0, keepdims=True)
        start_small()
        w_store(QKV)
        w_store(PROJ)
        for name in (CQ, CKV, CPROJ):
            w_other_side(name).wait_recv()
            w_forward(name).start()
        end_small()
        for chunk in order:
            settle(4, 1, chunk_pieces(chunk))
            store_input_grad(chunk).wait()
        side.size = THIRD
        for chunk in thirds:
            if chunk > 0:
                settle(5, 2, third_pieces(chunk))
                hand_back(chunk).wait_send()
            store_result(chunk).wait()
        for name in (UP, DOWN, QKV, PROJ):
            w_end(name)
        for name in (CQ, CKV, CPROJ):
            w_forward(name).wait()

    @pl.when(is_reader)
    def _():
        reader()

    for items in (made, added, summed):
        items.clear()

    @pl.when(jnp.logical_not(is_reader))
    def _():
        retriever()


def finish_kernel(heads, buckets, *refs):
    count = len(WEIGHTS)
    small, result, *grads = refs[: count + 3]
    outs = refs[count + 3 : 2 * count + 5]
    small_outs = refs[2 * count + 5 : 2 * count + 13]
    scratch = refs[2 * count + 13 :]
    near, wide, (in_sem, out_sem) = scratch[: count + 2], scratch[count + 2 : -2], scratch[-2:]
    sources = [result, *grads]
    loads = [
        pltpu.make_async_copy(source, target, in_sem.at[index])
        for index, (source, target) in enumerate(zip(sources, near))
    ]
    held = [near[0], *wide]
    stores = [
        pltpu.make_async_copy(source, target, out_sem.at[index])
        for index, (source, target) in enumerate(zip(held, outs))
    ]
    for load in loads:
        load.start()
    inner = heads * HEAD_DIM
    values, units, gains, shifts, biases, scales, table, loss = small_outs
    values[...] = small[0, : 2 * inner]
    units[...] = small[1]
    gains[...] = small[2:4]
    shifts[...] = small[4:6]
    biases[...] = small[6:8]
    scales[...] = small[8:11]
    for head in range(heads):
        table[head : head + 1] = small[11:12, head * buckets : (head + 1) * buckets]
    loss[...] = small[12:13, 0:1]
    for index in range(1, count + 2):
        loads[index].wait()
        source, target = near[index], wide[index - 1]
        step = 48 if source.shape[0] % 64 else 64

        @pl.loop(0, source.shape[0] // step)
        def _(i):
            part = pl.ds(pl.multiple_of(i * step, step), step)
            target[part] = source[part].astype(F32)

        stores[index].start()
        if index == 1:
            loads[0].wait()
            stores[0].start()
    for store in stores:
        store.wait()


def finish_results(heads, buckets, small, result, input_grad, grads):
    inner = heads * HEAD_DIM
    anywhere = pl.BlockSpec(memory_space=pl.ANY)
    vector = pl.BlockSpec(memory_space=pltpu.VMEM)
    low = [jax.ShapeDtypeStruct(grad.shape, F32) for grad in grads]
    rows = ((2 * inner,), (WIDTH,), (2, WIDTH), (2, WIDTH), (2, WIDTH), (3, WIDTH), (heads, buckets), (1, 1))
    out_shape = [
        jax.ShapeDtypeStruct(result.shape, BF16), jax.ShapeDtypeStruct(input_grad.shape, F32), *low,
        *(jax.ShapeDtypeStruct(shape, F32) for shape in rows)]
    count = len(grads) + 2
    sources = [result, input_grad, *grads]
    return pl.pallas_call(
        partial(finish_kernel, heads, buckets),
        out_shape=out_shape,
        in_specs=[vector] + [anywhere] * count,
        out_specs=[anywhere] * count + [vector] * len(rows),
        scratch_shapes=[pltpu.VMEM(x.shape, x.dtype) for x in sources]
        + [pltpu.VMEM(x.shape, F32) for x in sources[1:]]
        + [pltpu.SemaphoreType.DMA((count,)), pltpu.SemaphoreType.DMA((count,))],
        compiler_params=pltpu.CompilerParams(vmem_limit_bytes=63 * 2**20),
    )(small, *sources)


def local(
    batch,
    hidden,
    cotangent,
    qkv_weight,
    proj_weight,
    up_weight,
    down_weight,
    query_value_bias,
    unit_bias,
    layer_gain,
    layer_shift,
    output_bias,
    scale_gain,
    position_bias,
    cross_query,
    cross_key_value,
    cross_proj,
    encodings,
    query_vectors,
    passage_lengths,
    target_lengths,
):
    heads = proj_weight.shape[1] // HEAD_DIM
    buckets = position_bias.shape[1]
    inner = heads * HEAD_DIM
    far = dict(
        hidden=hidden, cotangent=cotangent, qkv_weight=qkv_weight[0].T, proj_weight=proj_weight,
        up_weight=up_weight, down_weight=down_weight, cross_query=cross_query.T,
        cross_key_value=cross_key_value, cross_proj=cross_proj, encodings=encodings)
    near = dict(
        biases=jnp.concatenate([query_value_bias, unit_bias]).reshape(1, -1),
        layer_gain=layer_gain, layer_shift=layer_shift, output_bias=output_bias,
        scale_gain=scale_gain, query_vectors=query_vectors, position_bias=position_bias)
    scalars = dict(
        passage_lengths=passage_lengths, target_lengths=target_lengths)
    anywhere = pl.BlockSpec(memory_space=pl.ANY)
    vector = pl.BlockSpec(memory_space=pltpu.VMEM)
    scalar = pl.BlockSpec(memory_space=pltpu.SMEM)
    out_shapes = dict(
        small_out=jax.ShapeDtypeStruct((16, WIDTH), F32),
        y=jax.ShapeDtypeStruct((SEQ, WIDTH), BF16),
        gin=jax.ShapeDtypeStruct((SEQ, WIDTH), BF16))
    for name, shape in weight_shapes(heads).items():
        out_shapes[name] = jax.ShapeDtypeStruct(shape, BF16)
    shapes = scratch_shapes(heads)
    names = [*far, *near, *scalars, *out_shapes, *shapes]
    small, result, input_grad, *grads = pl.pallas_call(
        partial(layer_kernel, heads, buckets, names),
        out_shape=list(out_shapes.values()),
        in_specs=[anywhere] * len(far) + [vector] * len(near) + [scalar] * len(scalars),
        out_specs=[vector] + [anywhere] * (len(out_shapes) - 1),
        scratch_shapes=list(shapes.values()),
        compiler_params=pltpu.CompilerParams(
            collective_id=0, has_side_effects=True, vmem_limit_bytes=63 * 2**20),
    )(*far.values(), *near.values(), *scalars.values())
    if batch > 4:
        groups = [[first + step for step in range(0, batch, 4)] for first in range(4)]
        grads = [grad.astype(F32) for grad in grads]
        input_grad = input_grad.astype(F32)
        grads, rows = lax.psum((grads, small[:12]), BATCH, axis_index_groups=groups)
        small_rows = (
            rows[0, : 2 * inner], rows[1], rows[2:4], rows[4:6], rows[6:8], rows[8:11],
            rows[11, : heads * buckets].reshape(heads, buckets), small[12, :1])
    else:
        result, input_grad, *rest = finish_results(heads, buckets, small, result, input_grad, grads)
        grads, small_rows = rest[: len(WEIGHTS)], rest[len(WEIGHTS) :]
    up, down, qkv, proj, cq, ckv, cproj = grads
    values, units, gains, shifts, biases, scales, table, loss = small_rows
    return (
        result[None],
        input_grad[None],
        qkv.T[None],
        proj[None],
        up[None],
        down[None],
        values,
        units,
        gains,
        shifts,
        biases,
        scales,
        table,
        cq.T,
        ckv,
        cproj,
        loss.reshape(-1),
    )


def solution(mesh):
    rows = P(STREAM, BATCH, None)
    columns_split = P(STREAM, None, TENSOR)
    rows_split = P(STREAM, TENSOR, None)
    weights = (columns_split, rows_split, columns_split, rows_split)
    cross = (P(None, TENSOR), P(None, TENSOR), P(TENSOR, None))
    vectors = (P(TENSOR), P(TENSOR), P(), P(), P(), P(), P(TENSOR, None))
    in_specs = (rows, rows, *weights, *vectors, *cross)
    in_specs = (*in_specs, P(BATCH, None, None), P(BATCH, None), P(BATCH, None), P(BATCH))
    out_specs = (rows, rows, *weights, *vectors, *cross, P(BATCH))
    return jax.shard_map(
        partial(local, mesh.shape[BATCH]), mesh=mesh, in_specs=in_specs, out_specs=out_specs,
        check_vma=False)
```
